128 devices in a mesh: dp: 16 (over z, y), row: 2 (over x_hi), col: 4 (over x_lo, core).
Axes of the slice: x: 4 (x_hi: 2, x_lo: 2; x = x_hi * 2 + x_lo), y: 4, z: 4, core: 2. Of those that a mesh axis runs over, the one named last changes fastest.
Arguments:
- tokens: bfloat16 [16384, 1152], P(('dp', 'row', 'col')), may hold values from -6 to 6
- cotangent: bfloat16 [16384, 1152], P(('dp', 'row', 'col')), may hold values from -6 to 6
- branch: int32 [16, 2], P('dp'), may hold values from 256 to 512, as said below
- w_query: float32 [2, 576, 4, 256], P('row', 'dp', 'col'), may hold values from -0.1875 to 0.1875
- w_keyval: float32 [2, 2, 576, 256], P(None, 'row', 'dp'), may hold values from -0.1875 to 0.1875
- w_out: float32 [4, 256, 2, 576], P('col', None, 'row', 'dp'), may hold values from -0.1875 to 0.1875
- w_gate_up: float32 [2, 4, 16, 124416], P('row', 'col', 'dp'), may hold values from -0.1875 to 0.1875
- w_down: float32 [2, 4, 16, 62208], P('row', 'col', 'dp'), may hold values from -0.078125 to 0.078125
- mom_query: float32 [2, 576, 4, 256], P('row', 'dp', 'col'), may hold values from -160 to 160
- mom_keyval: float32 [2, 2, 576, 256], P(None, 'row', 'dp'), may hold values from -160 to 160
- mom_out: float32 [4, 256, 2, 576], P('col', None, 'row', 'dp'), may hold values from -160 to 160
- mom_gate_up: float32 [2, 4, 16, 124416], P('row', 'col', 'dp'), may hold values from -320 to 320
- mom_down: float32 [2, 4, 16, 62208], P('row', 'col', 'dp'), may hold values from -384 to 384
- norm_gains: float32 [4, 1152], replicated
- qk_gains: float32 [2, 256], replicated, may hold values from 0.25 to 1.75
- mom_norm: float32 [4, 1152], replicated, may hold values from -768 to 768
- mom_qk: float32 [2, 256], replicated, may hold values from -224 to 224
Outputs:
- layer_out: bfloat16 [16384, 1152], P(('dp', 'row', 'col'))
- input_grad: float32 [16384, 1152], P(('dp', 'row', 'col'))
- new_mom_query: float32 [2, 576, 4, 256], P('row', 'dp', 'col')
- new_query: float32 [2, 576, 4, 256], P('row', 'dp', 'col')
- low_query: bfloat16 [2, 576, 4, 256], P('row', 'dp', 'col')
- new_mom_keyval: float32 [2, 2, 576, 256], P(None, 'row', 'dp')
- new_keyval: float32 [2, 2, 576, 256], P(None, 'row', 'dp')
- low_keyval: bfloat16 [2, 2, 576, 256], P(None, 'row', 'dp')
- new_mom_out: float32 [4, 256, 2, 576], P('col', None, 'row', 'dp')
- new_out: float32 [4, 256, 2, 576], P('col', None, 'row', 'dp')
- low_out: bfloat16 [4, 256, 2, 576], P('col', None, 'row', 'dp')
- new_mom_gate_up: float32 [2, 4, 16, 124416], P('row', 'col', 'dp')
- new_gate_up: float32 [2, 4, 16, 124416], P('row', 'col', 'dp')
- low_gate_up: bfloat16 [2, 4, 16, 124416], P('row', 'col', 'dp')
- new_mom_down: float32 [2, 4, 16, 62208], P('row', 'col', 'dp')
- new_down: float32 [2, 4, 16, 62208], P('row', 'col', 'dp')
- low_down: bfloat16 [2, 4, 16, 62208], P('row', 'col', 'dp')
- new_mom_norm: float32 [4, 1152], replicated
- new_norm_gains: float32 [4, 1152], replicated
- new_mom_qk: float32 [2, 256], replicated
- new_qk_gains: float32 [2, 256], replicated
The draws below stay inside these ranges and needn't reach their ends.
Inputs may be any that keep to these rules, and one draw needn't show every extreme that they name: Continuation c of a replica follows the first branch[replica, c] prompt tokens and starts at that position; in every replica one continuation follows the whole prompt, 512 tokens.
All inputs are finite; a program needn't handle non-finite values.
Results may differ from the reference program's by a relative error of at most 0.0169.
Values may be sent and summed in bfloat16 or wider, within the bound.
No kernel may reach another device: no remote copies, remote signals or barrier semaphores. Data moves between devices by JAX's collectives and lax.ppermute only.
A program may use at most 192 MiB of HBM per device.

```python
import math
import jax
import jax.numpy as jnp
from jax import lax

D = 1152
HEADS = 4
HD = 256
FF = 6912
CONT_LEN = 256
WINDOW = 512
NS_STEPS = 5
DR = 576
FC = 1728
PROMPT = 512
CONTS = 2
REP_TOKENS = 1024
TOKENS = 16384
N_DP = 16
N_ROW = 2
N_COL = 4


def draw_branch(key, part):
    key = jax.random.fold_in(key, 11)
    first_key, second_key = jax.random.split(key)
    values = jax.random.randint(first_key, (N_DP, CONTS), PROMPT // 2, PROMPT + 1, dtype=jnp.int32)
    chosen = jax.random.randint(second_key, (N_DP, 1), 0, CONTS, dtype=jnp.int32)
    slots = jnp.arange(CONTS, dtype=jnp.int32)[None, :]
    return jnp.where(slots == chosen, PROMPT, values)


def draw_norm_gains(key, part):
    key = jax.random.fold_in(key, 23)
    ramp = jnp.arange(D, dtype=jnp.float32) / (D - 1)
    base = 0.6 + 1.2 * ramp
    rough = jax.random.uniform(key, (4, D), jnp.float32, 0.75, 1.25)
    return base[None, :] * rough


def shard_levels(rng, dims, pieces, low, top_value):
    gain, own = 1.0, jax.random.fold_in(rng, 6)
    for dim, blocks in pieces:
        steps = jnp.exp(jax.random.uniform(jax.random.fold_in(own, dim), (blocks,), jnp.float32, low / len(pieces), top_value / len(pieces)))
        gain = gain * jnp.repeat(steps, dims[dim] // blocks).reshape([-1 if axis == dim else 1 for axis in range(len(dims))])
    return gain


def gaussian(stream_key, extent, deviation, bound, cuts=(), kind=jnp.bfloat16):
    loudness = shard_levels(stream_key, extent, cuts, -0.22, 0.18) if cuts else 1.0
    entries = jax.random.normal(stream_key, extent, jnp.float32) * deviation * loudness
    return jnp.minimum(jnp.maximum(entries, -bound), bound).astype(kind)


def setup_inputs(seed: int = 0) -> dict:
    arg_keys = jax.random.split(jax.random.key(seed), 18)
    tokens = gaussian(arg_keys[0], (TOKENS, D), 1.0, 6.0, ((0, 128),))
    cotangent = gaussian(arg_keys[1], (TOKENS, D), 1.0, 6.0, ((0, 128),))
    branch = draw_branch(jax.random.fold_in(arg_keys[17], 71), 0)
    w_query = gaussian(arg_keys[3], (N_ROW, DR, HEADS, HD), D ** -0.5, 0.1875, ((0, 2), (1, 16), (2, 4)), jnp.float32)
    w_keyval = gaussian(arg_keys[4], (2, N_ROW, DR, HD), D ** -0.5, 0.1875, ((1, 2), (2, 16)), jnp.float32)
    w_out = gaussian(arg_keys[5], (HEADS, HD, N_ROW, DR), (HEADS * HD) ** -0.5, 0.1875, ((0, 4), (2, 2), (3, 16)), jnp.float32)
    w_gate_up = gaussian(arg_keys[6], (N_ROW, N_COL, N_DP, DR * 2 * FC // N_DP), D ** -0.5, 0.1875, ((0, 2), (1, 4), (2, 16)), jnp.float32)
    w_down = gaussian(arg_keys[7], (N_ROW, N_COL, N_DP, DR * FC // N_DP), FF ** -0.5, 0.078125, ((0, 2), (1, 4), (2, 16)), jnp.float32)
    mom_query = gaussian(arg_keys[8], (N_ROW, DR, HEADS, HD), (0.2 * TOKENS ** 0.5), 160.0, ((0, 2), (1, 16), (2, 4)), jnp.float32)
    mom_keyval = gaussian(arg_keys[9], (2, N_ROW, DR, HD), (0.2 * TOKENS ** 0.5), 160.0, ((1, 2), (2, 16)), jnp.float32)
    mom_out = gaussian(arg_keys[10], (HEADS, HD, N_ROW, DR), (0.2 * TOKENS ** 0.5), 160.0, ((0, 4), (2, 2), (3, 16)), jnp.float32)
    mom_gate_up = gaussian(arg_keys[11], (N_ROW, N_COL, N_DP, DR * 2 * FC // N_DP), (0.4 * TOKENS ** 0.5), 320.0, ((0, 2), (1, 4), (2, 16)), jnp.float32)
    mom_down = gaussian(arg_keys[12], (N_ROW, N_COL, N_DP, DR * FC // N_DP), (0.5 * TOKENS ** 0.5), 384.0, ((0, 2), (1, 4), (2, 16)), jnp.float32)
    norm_gains = draw_norm_gains(jax.random.fold_in(arg_keys[17], 71), 0)
    qk_gains = jnp.clip(1.0 + 0.15 * jax.random.normal(arg_keys[14], (2, HD), jnp.float32), 0.25, 1.75)
    mom_norm = gaussian(arg_keys[15], (4, D), (1.0 * TOKENS ** 0.5), 768.0, (), jnp.float32)
    mom_qk = gaussian(arg_keys[16], (2, HD), (0.3 * TOKENS ** 0.5), 224.0, (), jnp.float32)
    return dict(tokens=tokens, cotangent=cotangent, branch=branch, w_query=w_query, w_keyval=w_keyval, w_out=w_out, w_gate_up=w_gate_up, w_down=w_down, mom_query=mom_query, mom_keyval=mom_keyval, mom_out=mom_out, mom_gate_up=mom_gate_up, mom_down=mom_down, norm_gains=norm_gains, qk_gains=qk_gains, mom_norm=mom_norm, mom_qk=mom_qk)


NORM_EPS = 1e-06
MUON_EPS = 1e-07
COEF_A = 3.4445
COEF_B = -4.775
COEF_C = 2.0315
MUON_RATE = 0.5
MUON_DECAY = 0.5
WEIGHT_DECAY = 0.01
GAIN_RATE = 0.003
GAIN_MOMENTUM = 0.5
ROPE_BASE = 10000.0
HIGH = lax.Precision.HIGHEST

@jax.custom_vjp
def low(v):
    return lax.optimization_barrier(v.astype(jnp.bfloat16)).astype(jnp.float32)

@jax.custom_vjp
def low_back(v):
    return v

def low_keep(v):
    return (low(v), None)

def low_pass(kept, grad):
    return (grad,)

def back_keep(v):
    return (v, None)

def back_low(kept, grad):
    return (low(grad),)
low.defvjp(low_keep, low_pass)
low_back.defvjp(back_keep, back_low)

def matmul(left, right):
    return jnp.dot(left, right, precision=HIGH, preferred_element_type=jnp.float32)

def rms_norm(vector, scaling):
    return vector * lax.rsqrt(lax.optimization_barrier(jnp.mean(vector * vector, axis=-1, keepdims=True)) + NORM_EPS) * scaling

def rotate(vector, angle):
    middle = vector.shape[-1] // 2
    first_half = vector[..., :middle]
    second_half = vector[..., middle:]
    cosine = jnp.cos(angle)
    sine = jnp.sin(angle)
    return jnp.concatenate([first_half * cosine - second_half * sine, second_half * cosine + first_half * sine], axis=-1)

def angles(position, head_width):
    steps = jnp.arange(head_width // 2, dtype=jnp.float32) * (2.0 / head_width)
    inverse = jnp.exp(-math.log(ROPE_BASE) * steps)
    return position.astype(jnp.float32)[:, None] * inverse[None, :]

def token_info(token_index, branch_row, prompt_len):
    in_prompt = token_index < prompt_len
    offset = jnp.maximum(token_index - prompt_len, 0)
    segment = jnp.where(in_prompt, -1, offset // CONT_LEN)
    within = offset - offset // CONT_LEN * CONT_LEN
    slots = jnp.arange(branch_row.shape[0], dtype=jnp.int32)
    hits = segment[:, None] == slots[None, :]
    start = lax.optimization_barrier(jnp.max(jnp.where(hits, branch_row[None, :], 0), axis=1))
    position = jnp.where(in_prompt, token_index, start + within)
    return (segment, position, start)

def visible(query_segment, query_position, query_start, key_segment, key_position, key_valid):
    same = (query_segment[:, None] == key_segment[None, :]) & (key_position[None, :] <= query_position[:, None])
    forked = (query_segment[:, None] >= 0) & (key_segment[None, :] < 0) & (key_position[None, :] < query_start[:, None])
    allowed_keys = (same | forked) & key_valid[None, :]
    return allowed_keys & (query_position[:, None] - key_position[None, :] < WINDOW)

def attention(queries, keys, values, segment, position, start):
    key_count = keys.shape[0]
    block_rows = min(512, key_count)
    scale = HD ** (-0.5)
    key_valid = jnp.ones((key_count,), dtype=bool)

    def one_block(block_index):
        first_row = block_index * block_rows
        query_part = lax.dynamic_slice_in_dim(queries, first_row, block_rows, 1)
        allowed_keys = visible(lax.dynamic_slice_in_dim(segment, first_row, block_rows, 0), lax.dynamic_slice_in_dim(position, first_row, block_rows, 0), lax.dynamic_slice_in_dim(start, first_row, block_rows, 0), segment, position, key_valid)
        scores = low_back(jnp.einsum('hqd,kd->hqk', query_part, keys, precision=HIGH) * scale)
        scores = jnp.where(allowed_keys[None], scores, -1e+30)
        largest = lax.optimization_barrier(jnp.max(scores, axis=-1, keepdims=True))
        weights = jnp.exp(scores - largest)
        probs = low(weights / lax.optimization_barrier(jnp.sum(weights, axis=-1, keepdims=True)))
        return jnp.einsum('hqk,kd->hqd', probs, values, precision=HIGH)
    blocks = lax.map(jax.checkpoint(one_block), jnp.arange(key_count // block_rows, dtype=jnp.int32))
    return blocks.transpose(1, 0, 2, 3).reshape(HEADS, key_count, HD)

def gate_up_full(array):
    slab = FC // N_DP
    return jnp.transpose(array.reshape(N_ROW, N_COL, N_DP, DR, 2, slab), (4, 0, 3, 1, 2, 5)).reshape(2, D, FF)

def down_full(array):
    slab = FC // N_DP
    return jnp.transpose(array.reshape(N_ROW, N_COL, N_DP, DR, slab), (0, 3, 1, 2, 4)).reshape(D, FF)

def forward(stream, w_query, w_keyval, w_out, w_gate_up, w_down, norm_gains, qk_gains, segment, position, start):
    count = stream.shape[0]
    query_weight = low(w_query.reshape(D, HEADS * HD))
    keyval_weight = low(w_keyval.reshape(2, D, HD))
    out_weight = low(w_out.reshape(HEADS * HD, D))
    gate_up_weight = low(gate_up_full(w_gate_up))
    down_weight = low(down_full(w_down))
    angle = angles(position, HD)
    normed = low(rms_norm(stream, norm_gains[0]))
    query_raw = low_back(matmul(normed, query_weight))
    key_raw = low_back(matmul(normed, keyval_weight[0]))
    value_raw = low_back(matmul(normed, keyval_weight[1]))
    heads = rms_norm(query_raw.reshape(count, HEADS, HD), qk_gains[0]).transpose(1, 0, 2)
    queries = low(rotate(heads, angle))
    keys = low(rotate(rms_norm(key_raw, qk_gains[1]), angle))
    values = low(value_raw)
    attended = low_back(low(attention(queries, keys, values, segment, position, start)))
    merged = attended.transpose(1, 0, 2).reshape(count, HEADS * HD)
    attn_branch = low_back(matmul(merged, out_weight))
    middle = stream + rms_norm(attn_branch, norm_gains[1])
    normed_ff = low(rms_norm(middle, norm_gains[2]))
    gate_out = low_back(matmul(normed_ff, gate_up_weight[0]))
    up_out = low_back(matmul(normed_ff, gate_up_weight[1]))
    hidden = low(jax.nn.gelu(gate_out, approximate=True) * up_out)
    ff_branch = low_back(lax.dot_general(hidden, down_weight, (((1,), (1,)), ((), ())), precision=HIGH, preferred_element_type=jnp.float32))
    return middle + rms_norm(ff_branch, norm_gains[3])

def orthogonalize(stack):

    def one_matrix(matrix):
        current = matrix / (jnp.sqrt(jnp.sum(matrix * matrix)) + MUON_EPS)
        for step in range(NS_STEPS):
            gram = matmul(current, current.T)
            poly = COEF_B * gram + COEF_C * matmul(gram, gram)
            current = COEF_A * current + matmul(poly, current)
        return current
    return jax.vmap(one_matrix)(stack)

def query_wide(array):
    return jnp.transpose(array, (0, 2, 3, 1))

def query_back(array):
    return jnp.transpose(array, (0, 3, 1, 2))

def keyval_wide(array):
    return jnp.transpose(array, (0, 1, 3, 2))

def middle_swap(array):
    return jnp.transpose(array, (0, 2, 1, 3))

def gate_up_wide(array):
    slab = FC // N_DP
    return jnp.transpose(array.reshape(N_ROW, N_COL, N_DP, DR, 2, slab), (0, 1, 3, 4, 2, 5)).reshape(N_ROW, N_COL, DR, 2 * FC)

def gate_up_back(array):
    slab = FC // N_DP
    return jnp.transpose(array.reshape(N_ROW, N_COL, DR, 2, N_DP, slab), (0, 1, 4, 2, 3, 5)).reshape(N_ROW, N_COL, N_DP, DR * 2 * slab)

def down_wide(array):
    slab = FC // N_DP
    return jnp.transpose(array.reshape(N_ROW, N_COL, N_DP, DR, slab), (0, 1, 3, 2, 4)).reshape(N_ROW, N_COL, DR, FC)

def down_back(array):
    slab = FC // N_DP
    return jnp.transpose(array.reshape(N_ROW, N_COL, DR, N_DP, slab), (0, 1, 3, 2, 4)).reshape(N_ROW, N_COL, N_DP, DR * slab)

def muon(gradient, momentum, master, to_wide, from_wide, scale):
    renewed = MUON_DECAY * momentum + gradient
    wide = to_wide(renewed)
    shape = wide.shape
    result = orthogonalize(wide.reshape((-1,) + shape[-2:])).reshape(shape)
    master_new = master * (1.0 - MUON_RATE * WEIGHT_DECAY) - MUON_RATE * scale * from_wide(result)
    return (renewed, master_new, master_new.astype(jnp.bfloat16))

def reference(tokens, cotangent, branch, w_query, w_keyval, w_out, w_gate_up, w_down, mom_query, mom_keyval, mom_out, mom_gate_up, mom_down, norm_gains, qk_gains, mom_norm, mom_qk):
    weights = (w_query, w_keyval, w_out, w_gate_up, w_down, norm_gains, qk_gains)
    inputs = tokens.astype(jnp.float32).reshape(N_DP, REP_TOKENS, D)
    backs = cotangent.astype(jnp.float32).reshape(N_DP, REP_TOKENS, D)
    token_index = jnp.arange(REP_TOKENS, dtype=jnp.int32)

    def replica(totals, item):
        stream, upstream, branch_row = item
        segment, position, start = token_info(token_index, branch_row, PROMPT)

        def layer(stream_in, wq_in, wkv_in, wo_in, wgu_in, wd_in, gains_in, qk_in):
            return forward(stream_in, wq_in, wkv_in, wo_in, wgu_in, wd_in, gains_in, qk_in, segment, position, start)
        result, pullback = jax.vjp(layer, stream, w_query, w_keyval, w_out, w_gate_up, w_down, norm_gains, qk_gains)
        grads = pullback(upstream)
        summed = tuple((total + grad_item for total, grad_item in zip(totals, grads[1:])))
        return (summed, (result.astype(jnp.bfloat16), grads[0]))
    zeros = tuple((jnp.zeros_like(weight) for weight in weights))
    totals, (outputs, input_grads) = lax.scan(replica, zeros, (inputs, backs, branch))
    tall_scale = math.sqrt(max(1.0, DR / HD))
    query_new = muon(totals[0], mom_query, w_query, query_wide, query_back, tall_scale)
    keyval_new = muon(totals[1], mom_keyval, w_keyval, keyval_wide, keyval_wide, tall_scale)
    out_new = muon(totals[2], mom_out, w_out, middle_swap, middle_swap, math.sqrt(max(1.0, HD / DR)))
    gate_up_new = muon(totals[3], mom_gate_up, w_gate_up, gate_up_wide, gate_up_back, math.sqrt(max(1.0, DR / (2 * FC))))
    down_new = muon(totals[4], mom_down, w_down, down_wide, down_back, math.sqrt(max(1.0, DR / FC)))
    norm_renewed = GAIN_MOMENTUM * mom_norm + totals[5]
    qk_renewed = GAIN_MOMENTUM * mom_qk + totals[6]
    return (outputs.reshape(TOKENS, D), input_grads.reshape(TOKENS, D), query_new[0], query_new[1], query_new[2], keyval_new[0], keyval_new[1], keyval_new[2], out_new[0], out_new[1], out_new[2], gate_up_new[0], gate_up_new[1], gate_up_new[2], down_new[0], down_new[1], down_new[2], norm_renewed, norm_gains - GAIN_RATE * norm_renewed, qk_renewed, qk_gains - GAIN_RATE * qk_renewed)
```

```python
import functools
import math

import jax
import jax.numpy as jnp
from jax import lax
from jax.experimental import pallas as pl
from jax.experimental.pallas import tpu as pltpu
from jax.sharding import PartitionSpec as P

CONT_LEN = 256
WINDOW = 512
NS_STEPS = 5
NORM_EPS = 1e-06
MUON_EPS = 1e-07
COEF_A = 3.4445
COEF_B = -4.775
COEF_C = 2.0315
MUON_RATE = 0.5
MUON_DECAY = 0.5
WEIGHT_DECAY = 0.01
GAIN_RATE = 0.003
GAIN_MOMENTUM = 0.5
ROPE_BASE = 10000.0
HIGH = lax.Precision.HIGHEST
BF = jnp.bfloat16
F32 = jnp.float32
RING = ("row", "col")
MASKED = -1e30
VMEM = 56 * 2**20
PAD = 64
GELU_C = math.sqrt(2.0 / math.pi)

NN = (((1,), (0,)), ((), ()))
NT = (((1,), (1,)), ((), ()))
TN = (((0,), (0,)), ((), ()))


def mm(left, right, dims=NN, precision=None):
    return lax.dot_general(left, right, dims, precision=precision, preferred_element_type=F32)


def flip(block, bits):
    return lax.ppermute(block, RING, [(i, i ^ bits) for i in range(8)])


def gather8(block):
    chips = jnp.stack([block] + [flip(block, 2 * k) for k in (1, 2, 3)])
    return jnp.concatenate([chips, flip(chips, 1)]).reshape(8 * block.shape[0], block.shape[1])


def gather4(block):
    chips = jnp.stack([block, flip(block, 2)])
    return jnp.concatenate([chips, flip(chips, 1)]).reshape(4 * block.shape[0], block.shape[1])


def scatter8(parts, rows):
    parts = parts.reshape(2, 4, rows, parts.shape[1])
    paired = parts[0].astype(F32) + flip(parts[1], 1).astype(F32)
    low = paired.astype(BF)
    total = paired[0]
    for k in (1, 2, 3):
        total = total + flip(low[k], 2 * k).astype(F32)
    return total


def scatter4(parts, rows):
    parts = parts.reshape(4, rows, parts.shape[1])
    total = parts[0].astype(F32)
    for slot, bits in ((1, 2), (2, 1), (3, 3)):
        total = total + flip(parts[slot], bits).astype(F32)
    return total


def inv_rms(vector):
    return lax.rsqrt(jnp.mean(vector * vector, axis=-1, keepdims=True) + NORM_EPS)


def norm_back(vector, gain, grad):
    scale = inv_rms(vector)
    gz = grad * gain
    du = scale * gz - vector * (scale * scale * scale) * jnp.mean(
        gz * vector, axis=-1, keepdims=True
    )
    return du, jnp.sum(grad * vector * scale, axis=0, keepdims=True)


def rotate(vector, cosine, sine):
    half = vector.shape[-1] // 2
    first, second = vector[:, :half], vector[:, half:]
    return jnp.concatenate([first * cosine - second * sine, second * cosine + first * sine], axis=1)


def rotate_back(vector, cosine, sine):
    half = vector.shape[-1] // 2
    first, second = vector[:, :half], vector[:, half:]
    return jnp.concatenate([first * cosine + second * sine, second * cosine - first * sine], axis=1)


def own_rows(values):
    rows = values.shape[0] // 4
    return jnp.concatenate([values[:rows], values[2 * rows : 3 * rows]], axis=0)


def attn_fwd_kernel(
    nx, w, mask, cos, sin, gains, branch, qraw_o, kraw_o, q_o, k_o, v_o, att_o, lse_o
):
    hd = q_o.shape[1]
    x = nx[...]
    qraw = mm(own_rows(x), w[:, :hd])
    kv = mm(x, w[:, hd : 3 * hd])
    kraw = kv[:, :hd]
    cosine, sine = cos[...], sin[...]
    q = rotate(qraw * inv_rms(qraw) * gains[0:1, :], own_rows(cosine), own_rows(sine)).astype(BF)
    k = rotate(kraw * inv_rms(kraw) * gains[1:2, :], cosine, sine).astype(BF)
    v = kv[:, hd:].astype(BF)
    scores = mm(q, k, NT) * (hd**-0.5) + mask[...]
    largest = jnp.max(scores, axis=1, keepdims=True)
    weights = jnp.exp(scores - largest)
    total = jnp.sum(weights, axis=1, keepdims=True)
    att = mm((weights / total).astype(BF), v).astype(BF)
    branch[...] = mm(att, w[:, 3 * hd :], NT).astype(BF)
    qraw_o[...] = qraw
    kraw_o[...] = kraw
    q_o[...] = q
    k_o[...] = k
    v_o[...] = v
    att_o[...] = att
    lse_o[...] = jnp.broadcast_to(largest + jnp.log(total), lse_o.shape)


def attn_bwd_kernel(
    dattn, nx, w, mask, cos, sin, gains, qraw, kraw, q, k, v, att, lse, dnorm, dw, dgains
):
    hd = q.shape[1]
    half = nx.shape[0] // 2
    quarter = half // 2
    scale = hd**-0.5
    da = dattn[...]
    datt = mm(da, w[:, 3 * hd :]).astype(BF)
    scores = mm(q[...], k[...], NT) * scale + mask[...]
    weights = jnp.exp(scores - lse[:, 0:1])
    dv = mm(weights.astype(BF), datt, TN).astype(BF)
    dp = mm(datt, v[...], NT)
    inner = jnp.sum(weights * dp, axis=1, keepdims=True)
    ds = (weights * (dp - inner)).astype(BF)
    dq = mm(ds, k[...]) * scale
    dk = mm(ds, q[...], TN) * scale
    cosine, sine = cos[...], sin[...]
    dqraw, dgq = norm_back(
        qraw[...], gains[0:1, :], rotate_back(dq, own_rows(cosine), own_rows(sine))
    )
    dkraw, dgk = norm_back(kraw[...], gains[1:2, :], rotate_back(dk, cosine, sine))
    dqraw, dkraw = dqraw.astype(BF), dkraw.astype(BF)
    dgains[0:1, :] = dgq
    dgains[1:2, :] = dgk
    x = nx[...]
    width = x.shape[1]
    parts = (
        (mm(own_rows(x), dqraw, TN), 0),
        (mm(x, dkraw, TN), 1),
        (mm(x, dv, TN), 2),
        (mm(da, att[...], TN), 3),
    )
    for part, place in parts:
        low = part.astype(BF)
        dw[:, place * hd : (place + 1) * hd] = low[: width // 2]
        dw[:, (4 + place) * hd : (5 + place) * hd] = low[width // 2 :]
    back = mm(dkraw, w[:, hd : 2 * hd], NT) + mm(dv, w[:, 2 * hd : 3 * hd], NT)
    qback = mm(dqraw, w[:, :hd], NT)
    dnorm[:quarter] = (back[:quarter] + qback[:quarter]).astype(BF)
    dnorm[quarter:half] = back[quarter:half].astype(BF)
    dnorm[half : half + quarter] = (back[half : half + quarter] + qback[quarter:]).astype(BF)
    dnorm[half + quarter :] = back[half + quarter :].astype(BF)


def gelu_parts(gate):
    inner = GELU_C * (gate + 0.044715 * gate * gate * gate)
    th = jnp.tanh(inner)
    value = 0.5 * gate * (1.0 + th)
    slope = 0.5 * (1.0 + th) + 0.5 * gate * (1.0 - th * th) * GELU_C * (
        1.0 + 3.0 * 0.044715 * gate * gate
    )
    return value, slope


def ffn_fwd_kernel(nf, w, gate_o, up_o, hidden_o, branch, acc):
    step = pl.program_id(0)
    slabs, _, rows, width = w.shape
    x = nf[...]
    gate = mm(x, w[:, 0].reshape(slabs * rows, width), NT)
    up = mm(x, w[:, 1].reshape(slabs * rows, width), NT)
    value, _ = gelu_parts(gate)
    hidden = (value * up).astype(BF)
    gate_o[...] = gate
    up_o[...] = up
    hidden_o[...] = hidden
    term = mm(hidden, w[:, 2].reshape(slabs * rows, width))

    @pl.when(step == 0)
    def _():
        acc[...] = term

    @pl.when(step > 0)
    def _():
        acc[...] += term

    @pl.when(step == pl.num_programs(0) - 1)
    def _():
        branch[...] = acc[...].astype(BF)


def ffn_bwd_kernel(df, nf, w, gate_i, up_i, hidden_i, dw, dnorm, acc):
    step = pl.program_id(0)
    slabs, _, rows, width = w.shape
    d = df[...]
    x = nf[...]
    dhid = mm(d, w[:, 2].reshape(slabs * rows, width), NT)
    value, slope = gelu_parts(gate_i[...])
    dgate = (dhid * up_i[...] * slope).astype(BF)
    dup = (dhid * value).astype(BF)
    dw[:, 0] = mm(dgate, x, TN).reshape(slabs, rows, width)
    dw[:, 1] = mm(dup, x, TN).reshape(slabs, rows, width)
    dw[:, 2] = mm(hidden_i[...], d, TN).reshape(slabs, rows, width)
    term = mm(dgate, w[:, 0].reshape(slabs * rows, width)) + mm(
        dup, w[:, 1].reshape(slabs * rows, width)
    )

    @pl.when(step == 0)
    def _():
        acc[...] = term

    @pl.when(step > 0)
    def _():
        acc[...] += term

    @pl.when(step == pl.num_programs(0) - 1)
    def _():
        dnorm[...] = acc[...].astype(BF)


def split(values):
    top = values.astype(BF)
    return top, (values - top.astype(F32)).astype(BF)


def mm3(left, right, dims=NN):
    return mm(left[0], right[0], dims) + (mm(left[0], right[1], dims) + mm(left[1], right[0], dims))


def eye(n):
    return lax.broadcasted_iota(jnp.int32, (n, n), 0) == lax.broadcasted_iota(jnp.int32, (n, n), 1)


def muon_chain(gram, current, exact_steps, turn):
    n = gram.shape[0]
    diag = eye(n)
    trace = jnp.sum(jnp.sum(jnp.where(diag, gram, 0.0), axis=1, keepdims=True), axis=0, keepdims=True)
    factor = 1.0 / (jnp.sqrt(trace) + MUON_EPS)
    a = gram * (factor * factor)
    x = current * factor
    for step in range(NS_STEPS):
        exact = step < exact_steps
        last = step == NS_STEPS - 1
        if exact:
            square = mm(a, a, NN, HIGH)
            poly = COEF_B * a + COEF_C * square + jnp.where(diag, COEF_A, 0.0)
            if not last:
                a = mm(mm(a, poly, NN, HIGH), poly, NN, HIGH)
            x = mm(poly, x, NT, HIGH) if last and turn else mm(x, poly, NN, HIGH)
        else:
            sa = split(a)
            square = mm3(sa, sa)
            poly = COEF_B * a + COEF_C * square + jnp.where(diag, COEF_A, 0.0)
            sp = split(poly)
            if not last:
                a = mm3(split(mm3(sa, sp)), sp)
            x = mm3(sp, split(x), NT) if last and turn else mm3(split(x), sp)
    return x


def muon_large_kernel(gram, gu, down, gu_o, down_o):
    gu_o[...] = muon_chain(gram[0], gu[...], 1, True)
    down_o[...] = muon_chain(gram[1], down[...], 1, True)


def muon_small_kernel(gram, current, out):
    for i in range(current.shape[0]):
        out[i] = muon_chain(gram[i], current[i], NS_STEPS, False)


def kernel(body, out_shape, flops, nbytes, **extra):
    return pl.pallas_call(
        body,
        out_shape=out_shape,
        compiler_params=pltpu.CompilerParams(vmem_limit_bytes=VMEM),
        cost_estimate=pl.CostEstimate(flops=flops, bytes_accessed=nbytes, transcendentals=0),
        **extra,
    )


def sds(shape, dtype):
    return jax.ShapeDtypeStruct(shape, dtype)


def shards(
    tokens,
    cotangent,
    branch,
    w_query,
    w_keyval,
    w_out,
    w_gate_up,
    w_down,
    mom_query,
    mom_keyval,
    mom_out,
    mom_gate_up,
    mom_down,
    norm_gains,
    qk_gains,
    mom_norm,
    mom_qk,
):
    rows, width = tokens.shape
    hd = w_query.shape[3]
    replicas = lax.axis_size("dp")
    half = width // 2
    slab = half // replicas
    cols = w_down.shape[3] // half
    part = cols // 2
    row_index = lax.axis_index("row")
    col_index = lax.axis_index("col")
    me = row_index * 4 + col_index
    first_row = row_index == 0
    row_len = 4 * rows
    rep = 8 * rows

    att_own = jnp.concatenate(
        [
            w_query.reshape(slab, hd),
            w_keyval[0].reshape(slab, hd),
            w_keyval[1].reshape(slab, hd),
            w_out.reshape(hd, slab).T,
        ],
        axis=1,
    ).astype(BF)
    att_other = flip(att_own, 4)
    att_pack = jnp.concatenate(
        [jnp.where(first_row, att_own, att_other), jnp.where(first_row, att_other, att_own)], axis=1
    )
    ff_own = (
        jnp.concatenate(
            [
                w_gate_up.reshape(half, 2, cols).astype(BF).transpose(1, 2, 0),
                w_down.reshape(half, 1, cols).astype(BF).transpose(1, 2, 0),
            ],
            axis=0,
        )
        .reshape(3, 2, part, half)
    )
    ff_keep = jnp.where(first_row, ff_own[:, 0], ff_own[:, 1])
    ff_send = jnp.where(first_row, ff_own[:, 1], ff_own[:, 0])
    ff_got = flip(ff_send, 4)
    ff_pack = jnp.concatenate(
        [jnp.where(first_row, ff_keep, ff_got), jnp.where(first_row, ff_got, ff_keep)], axis=2
    )
    ff_pack = jnp.pad(ff_pack, ((0, 0), (0, PAD - part), (0, 0)))
    ff_w = lax.all_gather(ff_pack.reshape(3 * PAD, width), "dp", axis=0, tiled=True).reshape(
        replicas, 3, PAD, width
    )
    att_all = lax.all_to_all(
        jnp.broadcast_to(att_pack[None], (replicas,) + att_pack.shape), "dp", 0, 0, tiled=True
    ).reshape(half, 8 * hd)
    att_w = jnp.concatenate([att_all[:, : 4 * hd], att_all[:, 4 * hd :]], axis=0)

    slots = jnp.asarray([2 * k + core for core in (0, 1) for k in range(4)], jnp.int32)
    ids = ((me ^ slots)[:, None] * rows + jnp.arange(rows, dtype=jnp.int32)[None, :]).reshape(rep)
    starts = branch[0]
    in_prompt = ids < row_len
    offset = jnp.maximum(ids - row_len, 0)
    segment = jnp.where(in_prompt, -1, offset // CONT_LEN)
    start = jnp.max(
        jnp.where(
            segment[:, None] == jnp.arange(starts.shape[0], dtype=jnp.int32)[None, :],
            starts[None, :],
            0,
        ),
        axis=1,
    )
    position = jnp.where(in_prompt, ids, start + offset % CONT_LEN)
    q_seg, q_pos, q_start = own_rows(segment), own_rows(position), own_rows(start)
    same = (q_seg[:, None] == segment[None, :]) & (position[None, :] <= q_pos[:, None])
    forked = (q_seg[:, None] >= 0) & (segment[None, :] < 0) & (position[None, :] < q_start[:, None])
    seen = (same | forked) & (q_pos[:, None] - position[None, :] < WINDOW)
    mask = jnp.where(seen, 0.0, MASKED).astype(F32)
    steps = jnp.arange(hd // 2, dtype=F32) * (2.0 / hd)
    angle = position.astype(F32)[:, None] * jnp.exp(-math.log(ROPE_BASE) * steps)[None, :]
    cosine, sine = jnp.cos(angle), jnp.sin(angle)

    stream = tokens.astype(F32)
    normed = (stream * inv_rms(stream) * norm_gains[0]).astype(BF)
    normed_all = gather8(normed)
    attn_part, q_raw, k_raw, q, k, v, att, lse = kernel(
        attn_fwd_kernel,
        (
            sds((row_len, width), BF),
            sds((row_len, hd), F32),
            sds((rep, hd), F32),
            sds((row_len, hd), BF),
            sds((rep, hd), BF),
            sds((rep, hd), BF),
            sds((row_len, hd), BF),
            sds((row_len, 128), F32),
        ),
        3 * 10**9,
        12 * 10**6,
        name="attn_fwd",
    )(normed_all, att_w, mask, cosine, sine, qk_gains)
    attn_branch = scatter4(attn_part, rows)
    middle = stream + attn_branch * inv_rms(attn_branch) * norm_gains[1]
    normed_ff = (middle * inv_rms(middle) * norm_gains[2]).astype(BF)

    nf_all = gather8(normed_ff)
    group = 4
    units = group * PAD
    full = pl.BlockSpec((rep, width), lambda i: (0, 0))
    w_spec = pl.BlockSpec((group, 3, PAD, width), lambda i: (i, 0, 0, 0))
    h_spec = pl.BlockSpec((rep, units), lambda i: (0, i))
    gate, up, hidden, ff_part = kernel(
        ffn_fwd_kernel,
        (
            sds((rep, replicas * PAD), F32),
            sds((rep, replicas * PAD), F32),
            sds((rep, replicas * PAD), BF),
            sds((rep, width), BF),
        ),
        8 * 10**9,
        20 * 10**6,
        grid=(replicas // group,),
        in_specs=[full, w_spec],
        out_specs=[h_spec, h_spec, h_spec, full],
        scratch_shapes=[pltpu.VMEM((rep, width), F32)],
        name="ffn_fwd",
    )(nf_all, ff_w)
    ff_branch = scatter8(ff_part, rows)
    layer_out = middle + ff_branch * inv_rms(ff_branch) * norm_gains[3]

    upstream = cotangent.astype(F32)
    ff_grad, grad_post_ff = norm_back(ff_branch, norm_gains[3], upstream)
    df_all = gather8(ff_grad.astype(BF))
    ff_dw, nf_part = kernel(
        ffn_bwd_kernel,
        (sds((replicas, 3, PAD, width), F32), sds((rep, width), BF)),
        15 * 10**9,
        40 * 10**6,
        grid=(replicas // group,),
        in_specs=[full, full, w_spec, h_spec, h_spec, h_spec],
        out_specs=[w_spec, full],
        scratch_shapes=[pltpu.VMEM((rep, width), F32)],
        name="ffn_bwd",
    )(df_all, nf_all, ff_w, gate, up, hidden)
    ff_g = lax.psum_scatter(
        ff_dw.reshape(replicas * 3 * PAD, width), "dp", scatter_dimension=0, tiled=True
    ).reshape(3, PAD, width)
    normed_ff_grad = scatter8(nf_part, rows)
    middle_part, grad_pre_ff = norm_back(middle, norm_gains[2], normed_ff_grad)
    middle_grad = upstream + middle_part
    attn_grad, grad_post = norm_back(attn_branch, norm_gains[1], middle_grad)

    da_all = gather4(attn_grad.astype(BF))
    normed_part, att_dw, grad_qk = kernel(
        attn_bwd_kernel,
        (sds((rep, width), BF), sds((half, 8 * hd), BF), sds((2, hd), F32)),
        6 * 10**9,
        20 * 10**6,
        name="attn_bwd",
    )(da_all, normed_all, att_w, mask, cosine, sine, qk_gains, q_raw, k_raw, q, k, v, att, lse)
    att_got = lax.all_to_all(
        att_dw.reshape(replicas, slab, 8 * hd), "dp", 0, 0, tiled=True
    )
    att_sum = jnp.sum(att_got.astype(F32), axis=0)
    normed_grad = scatter8(normed_part, rows)
    stream_part, grad_pre = norm_back(stream, norm_gains[0], normed_grad)
    input_grad = middle_grad + stream_part

    att_lo, att_hi = att_sum[:, : 4 * hd], att_sum[:, 4 * hd :]
    att_g = jnp.where(first_row, att_lo, att_hi) + flip(jnp.where(first_row, att_hi, att_lo), 4)
    kv_g = jnp.sum(lax.all_gather(att_g[:, hd : 3 * hd], "col", axis=0, tiled=False), axis=0)
    grad_small = (att_g[:, :hd], kv_g[:, :hd], kv_g[:, hd:], att_g[:, 3 * hd :])
    mom_small = (
        mom_query.reshape(slab, hd),
        mom_keyval[0].reshape(slab, hd),
        mom_keyval[1].reshape(slab, hd),
        mom_out.reshape(hd, slab).T,
    )
    new_small = [MUON_DECAY * m + g for m, g in zip(mom_small, grad_small)]
    small_grams = [mm(m, m, TN, HIGH) for m in new_small]
    gain_part = jnp.concatenate([grad_pre, grad_post, grad_pre_ff, grad_post_ff], axis=0)
    gain_pack = jnp.concatenate([gain_part.reshape(-1), grad_qk.reshape(-1)]).reshape(-1, 128)
    gain_rows = gain_pack.shape[0]
    q2 = hd // 2
    pieces = [
        piece
        for g in small_grams
        for piece in (g[:q2, :q2], g[:q2, q2:], g[q2:, q2:])
    ]
    packed = jnp.concatenate(pieces + [gain_pack], axis=0)
    chunk = -(-packed.shape[0] // (8 * replicas)) * 8
    packed = jnp.pad(packed, ((0, chunk * replicas - packed.shape[0]), (0, 0)))
    shares = lax.all_to_all(packed.reshape(replicas, chunk, 128), "dp", 0, 0, tiled=True)
    summed = lax.all_gather(jnp.sum(shares, axis=0), "dp", axis=0, tiled=True)
    blocks = summed[: 12 * q2].reshape(4, 3, q2, q2)
    gram_small = jnp.concatenate(
        [
            jnp.concatenate([blocks[:, 0], blocks[:, 1]], axis=2),
            jnp.concatenate([blocks[:, 1].transpose(0, 2, 1), blocks[:, 2]], axis=2),
        ],
        axis=1,
    )
    gain_sum = jnp.sum(
        lax.all_gather(summed[12 * q2 : 12 * q2 + gain_rows], RING, axis=0, tiled=False), axis=0
    )
    norm_total = gain_sum.reshape(-1)[: 4 * width].reshape(4, width)
    qk_total = gain_sum.reshape(-1)[4 * width :].reshape(2, hd)
    small_x = kernel(
        muon_small_kernel,
        sds((4, slab, hd), F32),
        2 * 10**9,
        2 * 10**6,
        name="muon_small",
    )(gram_small, jnp.stack(new_small))

    ff_mine = jnp.where(first_row, ff_g[:, :, :half], ff_g[:, :, half:])
    ff_theirs = flip(jnp.where(first_row, ff_g[:, :, half:], ff_g[:, :, :half]), 4)
    ff_grad_t = jnp.concatenate(
        [
            jnp.where(first_row, ff_mine, ff_theirs)[:, :part],
            jnp.where(first_row, ff_theirs, ff_mine)[:, :part],
        ],
        axis=1,
    )
    mom_gu_t = mom_gate_up.reshape(half, 2, cols).transpose(1, 2, 0)
    mom_d_t = mom_down.reshape(half, cols).T
    new_gu_t = (MUON_DECAY * mom_gu_t + ff_grad_t[:2]).reshape(2 * cols, half)
    new_d_t = MUON_DECAY * mom_d_t + ff_grad_t[2]
    gram_large = lax.psum(
        jnp.concatenate([mm(new_gu_t, new_gu_t, TN, HIGH), mm(new_d_t, new_d_t, TN, HIGH)]), "dp"
    ).reshape(2, half, half)
    gu_x, d_x = kernel(
        muon_large_kernel,
        (sds((half, 2 * cols), F32), sds((half, cols), F32)),
        20 * 10**9,
        5 * 10**6,
        name="muon_large",
    )(gram_large, new_gu_t, new_d_t)

    shrink = 1.0 - MUON_RATE * WEIGHT_DECAY
    tall = MUON_RATE * math.sqrt(max(1.0, half / hd))
    flat = MUON_RATE * math.sqrt(max(1.0, hd / half))
    new_query = w_query * shrink - tall * small_x[0].reshape(w_query.shape)
    new_keyval = w_keyval * shrink - tall * small_x[1:3].reshape(w_keyval.shape)
    new_out = w_out * shrink - flat * small_x[3].T.reshape(w_out.shape)
    new_gate_up = w_gate_up * shrink - MUON_RATE * math.sqrt(
        max(1.0, half / (2 * cols * replicas))
    ) * gu_x.reshape(w_gate_up.shape)
    new_down = w_down * shrink - MUON_RATE * math.sqrt(
        max(1.0, half / (cols * replicas))
    ) * d_x.reshape(w_down.shape)
    norm_renewed = GAIN_MOMENTUM * mom_norm + norm_total
    qk_renewed = GAIN_MOMENTUM * mom_qk + qk_total
    return (
        layer_out.astype(BF),
        input_grad,
        new_small[0].reshape(mom_query.shape),
        new_query,
        new_query.astype(BF),
        jnp.stack(new_small[1:3]).reshape(mom_keyval.shape),
        new_keyval,
        new_keyval.astype(BF),
        new_small[3].T.reshape(mom_out.shape),
        new_out,
        new_out.astype(BF),
        new_gu_t.reshape(2, cols, half).transpose(2, 0, 1).reshape(mom_gate_up.shape),
        new_gate_up,
        new_gate_up.astype(BF),
        new_d_t.T.reshape(mom_down.shape),
        new_down,
        new_down.astype(BF),
        norm_renewed,
        norm_gains - GAIN_RATE * norm_renewed,
        qk_renewed,
        qk_gains - GAIN_RATE * qk_renewed,
    )


def solution(mesh):
    tok = P(("dp", "row", "col"), None)
    query = P("row", "dp", "col", None)
    keyval = P(None, "row", "dp", None)
    out = P("col", None, "row", "dp")
    slabs = P("row", "col", "dp", None)
    weights = (query, keyval, out, slabs, slabs)
    in_specs = (tok, tok, P("dp", None)) + weights + weights + (P(),) * 4
    out_specs = (tok, tok) + tuple(spec for spec in weights for _ in range(3)) + (P(),) * 4
    return jax.shard_map(shards, mesh=mesh, in_specs=in_specs, out_specs=out_specs, check_vma=False)
```

```python
import functools
import math

import jax
import jax.numpy as jnp
from jax import lax
from jax.experimental import pallas as pl
from jax.experimental.pallas import tpu as pltpu
from jax.sharding import PartitionSpec as P

CONT_LEN = 256
WINDOW = 512
NS_STEPS = 5
NORM_EPS = 1e-06
MUON_EPS = 1e-07
COEF_A = 3.4445
COEF_B = -4.775
COEF_C = 2.0315
MUON_RATE = 0.5
MUON_DECAY = 0.5
WEIGHT_DECAY = 0.01
GAIN_RATE = 0.003
GAIN_MOMENTUM = 0.5
ROPE_BASE = 10000.0
HIGH = lax.Precision.HIGHEST
BF = jnp.bfloat16
F32 = jnp.float32
RING = ("row", "col")
MASKED = -1e30
VMEM = 56 * 2**20
PAD = 64
GELU_C = math.sqrt(2.0 / math.pi)

NN = (((1,), (0,)), ((), ()))
NT = (((1,), (1,)), ((), ()))
TN = (((0,), (0,)), ((), ()))


def mm(left, right, dims=NN, precision=None):
    return lax.dot_general(left, right, dims, precision=precision, preferred_element_type=F32)


def flip(block, bits):
    return lax.ppermute(block, RING, [(i, i ^ bits) for i in range(8)])


def gather4(block):
    near = [block, flip(block, 2)]
    return near + [flip(part, 1) for part in near]


def gather8(block):
    near = [flip(block, 4), flip(block, 6)]
    return gather4(block) + near + [flip(part, 1) for part in near]


def scatter8(parts):
    def paired(near, far):
        return near.astype(F32) + flip(far, 1).astype(F32)

    across, last = paired(parts[4], parts[6]), paired(parts[5], parts[7])
    beside, total = paired(parts[1], parts[3]), paired(parts[0], parts[2])
    for value, bits in ((across, 4), (last, 6), (beside, 2)):
        total = total + flip(value.astype(BF), bits).astype(F32)
    return total


def scatter4(parts):
    total = parts[0].astype(F32)
    for slot, bits in ((1, 2), (2, 1), (3, 3)):
        total = total + flip(parts[slot], bits).astype(F32)
    return total


def after(value, *others):
    return lax.optimization_barrier((value,) + others)[0]


def swap_all(blocks):
    return lax.all_to_all(blocks, "dp", 0, 0, tiled=True)


def inv_rms(vector):
    return lax.rsqrt(jnp.mean(vector * vector, axis=-1, keepdims=True) + NORM_EPS)


def norm_back(vector, gain, grad):
    scale = inv_rms(vector)
    gz = grad * gain
    du = scale * gz - vector * (scale * scale * scale) * jnp.mean(
        gz * vector, axis=-1, keepdims=True
    )
    return du, jnp.sum(grad * vector * scale, axis=0, keepdims=True)


def rotate(vector, cosine, sine):
    half = vector.shape[-1] // 2
    first, second = vector[:, :half], vector[:, half:]
    return jnp.concatenate([first * cosine - second * sine, second * cosine + first * sine], axis=1)


def rotate_back(vector, cosine, sine):
    half = vector.shape[-1] // 2
    first, second = vector[:, :half], vector[:, half:]
    return jnp.concatenate([first * cosine + second * sine, second * cosine - first * sine], axis=1)


def own_rows(values):
    return values[: values.shape[0] // 2]


def join(*parts):
    return jnp.concatenate([part[...] for part in parts], axis=0)


def attn_fwd_kernel(*refs):
    xs, (w_all, mask, cos, sin, gains), bs = refs[:8], refs[8:13], refs[13:17]
    w, qraw_o, kraw_o, q_o, k_o, v_o, att_o, lse_o = refs[17:]
    hd = q_o.shape[1]
    half = w.shape[0] // 2
    slab = w_all.shape[1] // 2
    slabs = [w_all[d].astype(F32) for d in range(w_all.shape[0])]
    for side in (0, 1):
        rows = [both[side * slab : (side + 1) * slab] for both in slabs]
        w[side * half : (side + 1) * half, :] = jnp.concatenate(rows, axis=0).astype(BF)
    x = join(*xs)
    qraw = mm(own_rows(x), w[:, :hd])
    kv = mm(x, w[:, hd : 3 * hd])
    kraw = kv[:, :hd]
    cosine, sine = cos[...], sin[...]
    q = rotate(qraw * inv_rms(qraw) * gains[0:1, :], own_rows(cosine), own_rows(sine)).astype(BF)
    k = rotate(kraw * inv_rms(kraw) * gains[1:2, :], cosine, sine).astype(BF)
    v = kv[:, hd:].astype(BF)
    scores = mm(q, k, NT) * (hd**-0.5) + mask[...]
    largest = jnp.max(scores, axis=1, keepdims=True)
    weights = jnp.exp(scores - largest)
    total = jnp.sum(weights, axis=1, keepdims=True)
    att = mm((weights / total).astype(BF), v).astype(BF)
    branch = mm(att, w[:, 3 * hd :], NT).astype(BF)
    rows = bs[0].shape[0]
    for i, part in enumerate(bs):
        part[...] = branch[i * rows : (i + 1) * rows]
    qraw_o[...] = qraw
    kraw_o[...] = kraw
    q_o[...] = q
    k_o[...] = k
    v_o[...] = v
    att_o[...] = att
    lse_o[...] = jnp.broadcast_to(largest + jnp.log(total), lse_o.shape)


def attn_bwd_kernel(*refs):
    das, xs, refs = refs[:4], refs[4:12], refs[12:]
    w, mask, cos, sin, gains, qraw, kraw, q, k, v, att, lse = refs[:12]
    ns, (dw, dgains) = refs[12:20], refs[20:]
    hd = q.shape[1]
    half = q.shape[0]
    scale = hd**-0.5
    da = join(*das)
    datt = mm(da, w[:, 3 * hd :]).astype(BF)
    scores = mm(q[...], k[...], NT) * scale + mask[...]
    weights = jnp.exp(scores - lse[:, 0:1])
    dv = mm(weights.astype(BF), datt, TN).astype(BF)
    dp = mm(datt, v[...], NT)
    inner = jnp.sum(weights * dp, axis=1, keepdims=True)
    ds = (weights * (dp - inner)).astype(BF)
    dq = mm(ds, k[...]) * scale
    dk = mm(ds, q[...], TN) * scale
    cosine, sine = cos[...], sin[...]
    dqraw, dgq = norm_back(
        qraw[...], gains[0:1, :], rotate_back(dq, own_rows(cosine), own_rows(sine))
    )
    dkraw, dgk = norm_back(kraw[...], gains[1:2, :], rotate_back(dk, cosine, sine))
    dqraw, dkraw = dqraw.astype(BF), dkraw.astype(BF)
    dgains[0:1, :] = dgq
    dgains[1:2, :] = dgk
    x = join(*xs)
    width = x.shape[1]
    parts = (
        (mm(own_rows(x), dqraw, TN), 0),
        (mm(x, dkraw, TN), 1),
        (mm(x, dv, TN), 2),
        (mm(da, att[...], TN), 3),
    )
    slab = dw.shape[1] // 2
    for part, place in parts:
        for d in range(dw.shape[0]):
            both = [part[at : at + slab] for at in (d * slab, width // 2 + d * slab)]
            dw[d, :, place * hd : (place + 1) * hd] = jnp.concatenate(both, axis=0).astype(BF)
    back = mm(dkraw, w[:, hd : 2 * hd], NT) + mm(dv, w[:, 2 * hd : 3 * hd], NT)
    qback = mm(dqraw, w[:, :hd], NT)
    rows = ns[0].shape[0]
    for i, part in enumerate(ns):
        at = slice(i * rows, (i + 1) * rows)
        part[...] = (back[at] + qback[at] if i < 4 else back[at]).astype(BF)


def gelu_parts(gate):
    inner = GELU_C * (gate + 0.044715 * gate * gate * gate)
    th = jnp.tanh(inner)
    value = 0.5 * gate * (1.0 + th)
    slope = 0.5 * (1.0 + th) + 0.5 * gate * (1.0 - th * th) * GELU_C * (
        1.0 + 3.0 * 0.044715 * gate * gate
    )
    return value, slope


def ffn_fwd_kernel(*refs):
    xs, w, (slope_o, value_o, hidden_o), parts, acc = refs[:8], refs[8], refs[9:12], refs[12:20], refs[20]
    slabs, _, rows, width = w.shape
    x = join(*xs)
    gate = mm(x, w[:, 0].reshape(slabs * rows, width), NT)
    up = mm(x, w[:, 1].reshape(slabs * rows, width), NT)
    value, slope = gelu_parts(gate)
    hidden = (value * up).astype(BF)
    slope_o[...] = (slope * up).astype(BF)
    value_o[...] = value.astype(BF)
    hidden_o[...] = hidden
    accumulate(pl.program_id(0), acc, mm(hidden, w[:, 2].reshape(slabs * rows, width)), *parts)


def accumulate(step, acc, term, *parts):
    last = pl.num_programs(0) - 1

    @pl.when(step == 0)
    def _():
        acc[...] = term

    @pl.when((step > 0) & (step < last))
    def _():
        acc[...] += term

    @pl.when(step == last)
    def _():
        total = (acc[...] + term).astype(BF)
        rows = parts[0].shape[0]
        for i, part in enumerate(parts):
            part[...] = total[i * rows : (i + 1) * rows]


def ffn_units_kernel(*refs):
    xs, ds, (w, slope_i, value_i, hidden_i, dgate_o, dup_o, dw) = refs[:8], refs[8:16], refs[16:]
    slabs, _, rows, width = dw.shape
    x, d = join(*xs), join(*ds)
    dhid = mm(d, w[...].reshape(slabs * rows, width), NT)
    dgate = (dhid * slope_i[...].astype(F32)).astype(BF)
    dup = (dhid * value_i[...].astype(F32)).astype(BF)
    dgate_o[...] = dgate
    dup_o[...] = dup
    for i, (left, right) in enumerate(((dgate, x), (dup, x), (hidden_i[...], d))):
        dw[:, i] = mm(left, right, TN).astype(BF).reshape(slabs, rows, width)


def ffn_tokens_kernel(dgate, dup, w, *refs):
    parts, acc = refs[:8], refs[8]
    slabs, _, rows, width = w.shape
    term = mm(dgate[...], w[:, 0].reshape(slabs * rows, width)) + mm(
        dup[...], w[:, 1].reshape(slabs * rows, width)
    )
    accumulate(pl.program_id(0), acc, term, *parts)


def split(values, count):
    pieces = []
    for _ in range(count):
        pieces.append(values.astype(BF))
        values = values - pieces[-1].astype(F32)
    return pieces


def stacks(values):
    a, b = split(values, 2)
    return jnp.concatenate([a, a, b], axis=0), jnp.concatenate([a, b, a], axis=0)


def sym_parts(left, right, n):
    return [mm(left[:, at:], right[:, at : at + 256], TN) for at in range(0, n, 256)]


def sym_full(parts):
    columns = []
    for j, part in enumerate(parts):
        above = [parts[i][(j - i) * 256 : (j - i) * 256 + part.shape[1]].T for i in range(j)]
        columns.append(jnp.concatenate(above + [part], axis=0) if above else part)
    return jnp.concatenate(columns, axis=1) if len(columns) > 1 else columns[0]


def sym_mm(left, right, n):
    return sym_full(sym_parts(left, right, n))


def muon_chains(grams, currents):
    n = grams[0].shape[0]
    diag = lax.broadcasted_iota(jnp.int32, (n, n), 0) == lax.broadcasted_iota(jnp.int32, (n, n), 1)
    a, x = [], []
    for gram, current in zip(grams, currents):
        trace = jnp.sum(
            jnp.sum(jnp.where(diag, gram, 0.0), axis=1, keepdims=True), axis=0, keepdims=True
        )
        factor = 1.0 / (jnp.sqrt(trace) + MUON_EPS)
        a.append(gram * (factor * factor))
        x.append(current * factor)
    for step in range(NS_STEPS):
        sa = [stacks(m) for m in a]
        square = [sym_mm(l, r, n) for l, r in sa]
        poly = [COEF_B * m + COEF_C * q + jnp.where(diag, COEF_A, 0.0) for m, q in zip(a, square)]
        sp = [stacks(p) for p in poly]
        if step < NS_STEPS - 1:
            half = [stacks(sym_mm(l, sp[i][1], n)) for i, (l, _) in enumerate(sa)]
            a = [sym_mm(l, sp[i][1], n) for i, (l, _) in enumerate(half)]
        x = [mm(sp[i][0], stacks(m)[1], TN) for i, m in enumerate(x)]
    return x


def pack_rows(n):
    return sum(2 * (n - at) if n - at >= 256 else n - at for at in range(0, n, 256))


def ff_gram_kernel(flag, mine, theirs, mom_gu, mom_d, gu_o, d_o, gu_c, d_c, packed):
    first = flag[0] == 0
    n = mom_gu.shape[0]
    work = (((0, 1), mom_gu, gu_o, gu_c), ((2,), mom_d, d_o, d_c))
    for place, (kinds, mom, m_o, compact_o) in enumerate(work):
        rows = []
        for kind in kinds:
            own = mine[kind * PAD : (kind + 1) * PAD, :].astype(F32)
            got = theirs[kind * PAD : (kind + 1) * PAD, :].astype(F32)
            rows += [jnp.where(first, own, got), jnp.where(first, got, own)]
        part = mom.shape[1] // len(rows)
        blank = jnp.zeros((n, PAD - part), F32)
        spread = []
        for i in range(len(rows)):
            spread += [mom[:, i * part : (i + 1) * part], blank]
        m = MUON_DECAY * jnp.concatenate(spread, axis=1) + jnp.concatenate(rows, axis=0).T
        m_o[...] = m
        compact_o[...] = compact(m, compact_o.shape[1])
        pieces = []
        for start in range(0, n, 256):
            block = mm(m[start:], m[start : start + 256], NT, HIGH)
            if block.shape[1] == 256:
                pieces += [block[:, :128], block[:, 128:]]
            else:
                pieces.append(jnp.pad(block, ((0, 0), (0, 128 - block.shape[1]))))
        replicas, rows, _ = packed.shape
        rows //= 2
        whole = jnp.concatenate(pieces, axis=0)
        whole = jnp.pad(whole, ((0, replicas * rows - whole.shape[0]), (0, 0)))
        packed[:, place * rows : (place + 1) * rows, :] = whole.reshape(replicas, rows, 128)


def compact(values, width):
    count = values.shape[1] // PAD
    part = width // count
    return jnp.concatenate([values[:, i * PAD : i * PAD + part] for i in range(count)], axis=1)


def muon_large_kernel(scale, packed, m, out):
    n = m.shape[0]
    parts, at = [], 0
    for start in range(0, n, 256):
        rows, cols = n - start, min(256, n - start)
        if cols == 256:
            parts.append(
                jnp.concatenate(
                    [packed[at : at + rows, :], packed[at + rows : at + 2 * rows, :]], axis=1
                )
            )
            at += 2 * rows
        else:
            parts.append(packed[at : at + rows, :cols])
            at += rows
    (x,) = muon_chains([sym_full(parts)], [m[...]])
    out[...] = compact(x * scale, out.shape[1])


def muon_small_kernel(every, m, out, gains):
    count, rows, n = m.shape
    lead = every.shape[1] - gains.shape[0]
    step = lead // count
    grams = []
    for i in range(count):
        whole = every[:, i * step : (i + 1) * step, :].reshape(every.shape[0] * step, n)
        grams.append(mm(whole, whole, TN, HIGH))
    for i, x in enumerate(muon_chains(grams, [m[i].T for i in range(count)])):
        out[i] = x.T
    gains[...] = jnp.sum(every[:, lead:, :], axis=0)


def kernel(body, out_shape, flops, nbytes, **extra):
    return pl.pallas_call(
        body,
        out_shape=out_shape,
        compiler_params=pltpu.CompilerParams(vmem_limit_bytes=VMEM),
        cost_estimate=pl.CostEstimate(flops=flops, bytes_accessed=nbytes, transcendentals=0),
        **extra,
    )


def sds(shape, dtype):
    return jax.ShapeDtypeStruct(shape, dtype)


def shards(
    tokens,
    cotangent,
    branch,
    w_query,
    w_keyval,
    w_out,
    w_gate_up,
    w_down,
    mom_query,
    mom_keyval,
    mom_out,
    mom_gate_up,
    mom_down,
    norm_gains,
    qk_gains,
    mom_norm,
    mom_qk,
):
    rows, width = tokens.shape
    hd = w_query.shape[3]
    replicas = lax.axis_size("dp")
    half = width // 2
    slab = half // replicas
    cols = w_down.shape[3] // half
    part = cols // 2
    row_index = lax.axis_index("row")
    col_index = lax.axis_index("col")
    me = row_index * 4 + col_index
    first_row = row_index == 0
    row_len = 4 * rows
    rep = 8 * rows

    ff_own = (
        jnp.concatenate(
            [
                w_gate_up.reshape(half, 2, cols).astype(BF).transpose(1, 2, 0),
                w_down.reshape(half, 1, cols).astype(BF).transpose(1, 2, 0),
            ],
            axis=0,
        )
        .reshape(3, 2, part, half)
    )
    ff_keep = jnp.where(first_row, ff_own[:, 0], ff_own[:, 1])
    ff_send = jnp.where(first_row, ff_own[:, 1], ff_own[:, 0])
    ff_send, wq, wk, wo = lax.optimization_barrier((ff_send, w_query, w_keyval, w_out))
    ff_got = flip(ff_send, 4)
    att_own = jnp.concatenate(
        [
            wq.reshape(slab, hd),
            wk[0].reshape(slab, hd),
            wk[1].reshape(slab, hd),
            wo.reshape(hd, slab).T,
        ],
        axis=1,
    ).astype(BF)
    att_other = flip(att_own, 4)
    att_pack = jnp.concatenate(
        [jnp.where(first_row, att_own, att_other), jnp.where(first_row, att_other, att_own)]
    )
    att_shares = jnp.broadcast_to(att_pack[None], (replicas,) + att_pack.shape)
    att_shares, tokens, mom_query, mom_keyval, mom_out, mom_gate_up, mom_down = (
        lax.optimization_barrier(
            (att_shares, tokens, mom_query, mom_keyval, mom_out, mom_gate_up, mom_down)
        )
    )
    ff_pack = jnp.concatenate(
        [jnp.where(first_row, ff_keep, ff_got), jnp.where(first_row, ff_got, ff_keep)], axis=2
    )
    ff_pack = jnp.pad(ff_pack, ((0, 0), (0, PAD - part), (0, 0)))
    ff_w = lax.all_gather(ff_pack.reshape(3 * PAD, width), "dp", axis=0, tiled=True).reshape(
        replicas, 3, PAD, width
    )
    att_all = swap_all(att_shares)
    mom_gu = mom_gate_up.reshape(half, 2 * cols)
    mom_d = mom_down.reshape(half, cols)
    mom_small = jnp.stack(
        [
            mom_query.reshape(slab, hd),
            mom_keyval[0].reshape(slab, hd),
            mom_keyval[1].reshape(slab, hd),
            mom_out.reshape(hd, slab).T,
        ]
    )
    att_all, mom_gu, mom_d, mom_small = lax.optimization_barrier((att_all, mom_gu, mom_d, mom_small))
    slots = jnp.asarray(
        [2 * k + core for pair in (0, 2) for core in (0, 1) for k in (pair, pair + 1)], jnp.int32
    )
    ids = ((me ^ slots)[:, None] * rows + jnp.arange(rows, dtype=jnp.int32)[None, :]).reshape(rep)
    starts = branch[0]
    in_prompt = ids < row_len
    offset = jnp.maximum(ids - row_len, 0)
    segment = jnp.where(in_prompt, -1, offset // CONT_LEN)
    start = jnp.max(
        jnp.where(
            segment[:, None] == jnp.arange(starts.shape[0], dtype=jnp.int32)[None, :],
            starts[None, :],
            0,
        ),
        axis=1,
    )
    position = jnp.where(in_prompt, ids, start + offset % CONT_LEN)
    q_seg, q_pos, q_start = own_rows(segment), own_rows(position), own_rows(start)
    same = (q_seg[:, None] == segment[None, :]) & (position[None, :] <= q_pos[:, None])
    forked = (q_seg[:, None] >= 0) & (segment[None, :] < 0) & (position[None, :] < q_start[:, None])
    seen = (same | forked) & (q_pos[:, None] - position[None, :] < WINDOW)
    mask = jnp.where(seen, 0.0, MASKED).astype(F32)
    steps = jnp.arange(hd // 2, dtype=F32) * (2.0 / hd)
    angle = position.astype(F32)[:, None] * jnp.exp(-math.log(ROPE_BASE) * steps)[None, :]
    cosine, sine = jnp.cos(angle), jnp.sin(angle)

    stream = tokens.astype(F32)
    normed = (stream * inv_rms(stream) * norm_gains[0]).astype(BF)
    normed_all = gather8(normed)
    *attn_parts, att_w, q_raw, k_raw, q, k, v, att, lse = kernel(
        attn_fwd_kernel,
        (sds((rows, width), BF),) * 4
        + (
            sds((width, 4 * hd), BF),
            sds((row_len, hd), F32),
            sds((rep, hd), F32),
            sds((row_len, hd), BF),
            sds((rep, hd), BF),
            sds((rep, hd), BF),
            sds((row_len, hd), BF),
            sds((row_len, 128), F32),
        ),
        3 * 10**9,
        12 * 10**6,
        name="attn_fwd",
    )(*normed_all, att_all, mask, cosine, sine, qk_gains)
    attn_branch = scatter4(attn_parts)
    middle = stream + attn_branch * inv_rms(attn_branch) * norm_gains[1]
    normed_ff = (middle * inv_rms(middle) * norm_gains[2]).astype(BF)

    nf_all = gather8(normed_ff)
    group = 8
    units = group * PAD
    hidden_units = replicas * PAD
    part_spec = pl.BlockSpec((rows, width), lambda i: (0, 0))
    w_spec = pl.BlockSpec((group, 3, PAD, width), lambda i: (i, 0, 0, 0))
    gu_spec = pl.BlockSpec((group, 2, PAD, width), lambda i: (i, 0, 0, 0))
    h_spec = pl.BlockSpec((rep, units), lambda i: (0, i))
    h_out = sds((rep, hidden_units), BF)
    x_out = sds((rows, width), BF)
    acc = pltpu.VMEM((rep, width), F32)
    grid = (replicas // group,)
    slope, value, hidden, *ff_parts = kernel(
        ffn_fwd_kernel,
        (h_out,) * 3 + (x_out,) * 8,
        8 * 10**9,
        20 * 10**6,
        grid=grid,
        in_specs=[part_spec] * 8 + [w_spec],
        out_specs=[h_spec] * 3 + [part_spec] * 8,
        scratch_shapes=[acc],
        name="ffn_fwd",
    )(*nf_all, ff_w)
    ff_branch = scatter8(ff_parts)
    layer_out = middle + ff_branch * inv_rms(ff_branch) * norm_gains[3]

    upstream = cotangent.astype(F32)
    ff_grad, grad_post_ff = norm_back(ff_branch, norm_gains[3], upstream)
    df_all = gather8(ff_grad.astype(BF))
    dgate, dup, ff_dw = kernel(
        ffn_units_kernel,
        (h_out,) * 2 + (sds((replicas, 3, PAD, width), BF),),
        10 * 10**9,
        30 * 10**6,
        grid=grid,
        in_specs=[part_spec] * 16
        + [pl.BlockSpec((group, 1, PAD, width), lambda i: (i, 2, 0, 0))]
        + [h_spec] * 3,
        out_specs=[h_spec, h_spec, w_spec],
        name="ffn_units",
    )(*nf_all, *df_all, ff_w, slope, value, hidden)
    ff_sum = lax.psum_scatter(
        ff_dw.reshape(replicas * 3 * PAD, width), "dp", scatter_dimension=0, tiled=True
    )
    nf_parts = kernel(
        ffn_tokens_kernel,
        (x_out,) * 8,
        5 * 10**9,
        12 * 10**6,
        grid=grid,
        in_specs=[h_spec, h_spec, gu_spec],
        out_specs=[part_spec] * 8,
        scratch_shapes=[acc],
        name="ffn_tokens",
    )(dgate, dup, ff_w)
    normed_ff_grad = scatter8(nf_parts)
    middle_part, grad_pre_ff = norm_back(middle, norm_gains[2], normed_ff_grad)
    middle_grad = upstream + middle_part
    attn_grad, grad_post = norm_back(attn_branch, norm_gains[1], middle_grad)

    da_all = gather4(attn_grad.astype(BF))
    *dn_parts, att_dw, grad_qk = kernel(
        attn_bwd_kernel,
        (x_out,) * 8 + (sds((replicas, 2 * slab, 4 * hd), BF), sds((2, hd), F32)),
        6 * 10**9,
        20 * 10**6,
        name="attn_bwd",
    )(*da_all, *normed_all, att_w, mask, cosine, sine, qk_gains, q_raw, k_raw, q, k, v, att, lse)
    att_got = swap_all(att_dw)
    normed_grad = scatter8(dn_parts)
    stream_part, grad_pre = norm_back(stream, norm_gains[0], normed_grad)
    input_grad = middle_grad + stream_part

    flag = row_index.astype(jnp.int32).reshape(1)

    low, high = ff_sum[:, :half], ff_sum[:, half:]
    mine = jnp.where(first_row, low, high)
    swapped = jnp.where(first_row, high, low)
    theirs = flip(swapped, 4)
    share_rows = -(-pack_rows(half) // (8 * replicas)) * 8
    vmem = pl.BlockSpec(memory_space=pltpu.VMEM)
    padded_gu, padded_d, new_gu, new_d, packed = kernel(
        ff_gram_kernel,
        (
            sds((half, 4 * PAD), F32),
            sds((half, 2 * PAD), F32),
            sds((half, 2 * cols), F32),
            sds((half, cols), F32),
            sds((replicas, 2 * share_rows, 128), F32),
        ),
        3 * 10**9,
        6 * 10**6,
        in_specs=[pl.BlockSpec(memory_space=pltpu.SMEM)] + [vmem] * 4,
        name="gram_ff",
    )(flag, mine, theirs, mom_gu, mom_d)
    gram_share = jnp.sum(swap_all(packed), axis=0)
    gram_share = gram_share.reshape(2, -1, 128)

    def everywhere(share):
        return swap_all(jnp.broadcast_to(share[None], (replicas,) + share.shape)).reshape(-1, 128)

    total_gu, total_d = everywhere(gram_share[0]), everywhere(gram_share[1])

    def orthogonal(total, padded, width, name):
        scale = MUON_RATE * math.sqrt(max(1.0, half / (width * replicas)))
        return kernel(
            functools.partial(muon_large_kernel, scale),
            sds((half, width), F32),
            12 * 10**9,
            5 * 10**6,
            name="muon_" + name,
        )(total, padded)

    att_sum = jnp.sum(after(att_got, swapped).astype(F32), axis=0)
    gain_part = jnp.concatenate([grad_pre, grad_post, grad_pre_ff, grad_post_ff], axis=0)
    gain_pack = jnp.concatenate([gain_part.reshape(-1), grad_qk.reshape(-1)])
    gain_rows = gain_pack.shape[0] // (4 * hd)
    gain_pack = gain_pack.reshape(gain_rows, 4 * hd)
    att_lo, att_hi = att_sum[:slab], att_sum[slab:]
    att_g = jnp.concatenate([jnp.where(first_row, att_lo, att_hi), gain_pack]) + flip(
        jnp.concatenate([jnp.where(first_row, att_hi, att_lo), gain_pack]), 4
    )
    ring_g = jnp.concatenate(
        [att_g[:slab, hd : 3 * hd], att_g[slab:].reshape(2 * gain_rows, 2 * hd)], axis=0
    )
    ring_g = ring_g + flip(ring_g, 1)
    ring_g = ring_g + flip(ring_g, 2)
    grad_small = jnp.stack(
        [att_g[:slab, :hd], ring_g[:slab, :hd], ring_g[:slab, hd:], att_g[:slab, 3 * hd :]]
    )
    new_small = MUON_DECAY * mom_small + grad_small
    tile = 8
    slab_rows = -(-slab // tile) * tile
    gains_in = ring_g[slab:].reshape(-1, hd)
    gain_tile = -(-gains_in.shape[0] // tile) * tile
    share = jnp.concatenate(
        [
            jnp.pad(new_small, ((0, 0), (0, slab_rows - slab), (0, 0))).reshape(-1, hd),
            jnp.pad(gains_in, ((0, gain_tile - gains_in.shape[0]), (0, 0))),
        ]
    )
    every = lax.all_gather(share, "dp", axis=0, tiled=True).reshape((replicas,) + share.shape)

    gu_x = orthogonal(total_gu, padded_gu, 2 * cols, "gu")
    d_x = orthogonal(after(total_d, gu_x), padded_d, cols, "down")
    small_x, gain_sum = kernel(
        muon_small_kernel,
        (sds((4, slab, hd), F32), sds((gain_tile, hd), F32)),
        2 * 10**9,
        4 * 10**6,
        name="muon_small",
    )(after(every, d_x), new_small)
    gain_sum = gain_sum.reshape(-1)
    norm_total = gain_sum[: 4 * width].reshape(4, width)
    qk_total = gain_sum[4 * width : 4 * width + 2 * hd].reshape(2, hd)

    shrink = 1.0 - MUON_RATE * WEIGHT_DECAY
    tall = MUON_RATE * math.sqrt(max(1.0, half / hd))
    flat = MUON_RATE * math.sqrt(max(1.0, hd / half))
    new_query = w_query * shrink - tall * small_x[0].reshape(w_query.shape)
    new_keyval = w_keyval * shrink - tall * small_x[1:3].reshape(w_keyval.shape)
    new_out = w_out * shrink - flat * small_x[3].T.reshape(w_out.shape)
    new_gate_up = w_gate_up * shrink - gu_x.reshape(w_gate_up.shape)
    new_down = w_down * shrink - d_x.reshape(w_down.shape)
    norm_renewed = GAIN_MOMENTUM * mom_norm + norm_total
    qk_renewed = GAIN_MOMENTUM * mom_qk + qk_total
    return (
        layer_out.astype(BF),
        input_grad,
        new_small[0].reshape(mom_query.shape),
        new_query,
        new_query.astype(BF),
        new_small[1:3].reshape(mom_keyval.shape),
        new_keyval,
        new_keyval.astype(BF),
        new_small[3].T.reshape(mom_out.shape),
        new_out,
        new_out.astype(BF),
        new_gu.reshape(mom_gate_up.shape),
        new_gate_up,
        new_gate_up.astype(BF),
        new_d.reshape(mom_down.shape),
        new_down,
        new_down.astype(BF),
        norm_renewed,
        norm_gains - GAIN_RATE * norm_renewed,
        qk_renewed,
        qk_gains - GAIN_RATE * qk_renewed,
    )


def solution(mesh):
    tok = P(("dp", "row", "col"), None)
    query = P("row", "dp", "col", None)
    keyval = P(None, "row", "dp", None)
    out = P("col", None, "row", "dp")
    slabs = P("row", "col", "dp", None)
    weights = (query, keyval, out, slabs, slabs)
    in_specs = (tok, tok, P("dp", None)) + weights + weights + (P(),) * 4
    out_specs = (tok, tok) + tuple(spec for spec in weights for _ in range(3)) + (P(),) * 4
    return jax.shard_map(shards, mesh=mesh, in_specs=in_specs, out_specs=out_specs, check_vma=False)
```

```python
import functools
import math

import jax
import jax.numpy as jnp
from jax import lax
from jax.experimental import pallas as pl
from jax.experimental.pallas import tpu as pltpu
from jax.sharding import PartitionSpec as P

CONT_LEN = 256
WINDOW = 512
NS_STEPS = 5
NORM_EPS = 1e-06
MUON_EPS = 1e-07
COEF_A = 3.4445
COEF_B = -4.775
COEF_C = 2.0315
MUON_RATE = 0.5
MUON_DECAY = 0.5
WEIGHT_DECAY = 0.01
GAIN_RATE = 0.003
GAIN_MOMENTUM = 0.5
ROPE_BASE = 10000.0
HIGH = lax.Precision.HIGHEST
BF = jnp.bfloat16
F32 = jnp.float32
RING = ("row", "col")
MASKED = -1e30
MIB = 2**20
PAD = 64
GELU_C = math.sqrt(2.0 / math.pi)

NN = (((1,), (0,)), ((), ()))
NT = (((1,), (1,)), ((), ()))
TN = (((0,), (0,)), ((), ()))


def mm(left, right, dims=NN, precision=None):
    return lax.dot_general(left, right, dims, precision=precision, preferred_element_type=F32)


def flip(block, bits):
    return lax.ppermute(block, RING, [(i, i ^ bits) for i in range(8)])


def gather4(block):
    near = [block, flip(block, 2)]
    return near + [flip(part, 1) for part in near]


def gather8(block):
    near = [flip(block, 4), flip(block, 6)]
    return gather4(block) + near + [flip(part, 1) for part in near]


def scatter8(parts):
    def paired(near, far):
        return near.astype(F32) + flip(far, 1).astype(F32)

    across, last = paired(parts[4], parts[6]), paired(parts[5], parts[7])
    beside, total = paired(parts[1], parts[3]), paired(parts[0], parts[2])
    for value, bits in ((across, 4), (last, 6), (beside, 2)):
        total = total + flip(value.astype(BF), bits).astype(F32)
    return total


def scatter4(parts):
    total = parts[0].astype(F32)
    for slot, bits in ((1, 2), (2, 1), (3, 3)):
        total = total + flip(parts[slot], bits).astype(F32)
    return total


def after(value, *others):
    return lax.optimization_barrier((value,) + others)[0]


def swap_all(blocks):
    return lax.all_to_all(blocks, "dp", 0, 0, tiled=True)


def inv_rms(vector):
    return lax.rsqrt(jnp.mean(vector * vector, axis=-1, keepdims=True) + NORM_EPS)


def norm_back(vector, gain, grad):
    scale = inv_rms(vector)
    gz = grad * gain
    du = scale * gz - vector * (scale * scale * scale) * jnp.mean(
        gz * vector, axis=-1, keepdims=True
    )
    return du, jnp.sum(grad * vector * scale, axis=0, keepdims=True)


def rotate(vector, cosine, sine):
    half = vector.shape[-1] // 2
    first, second = vector[:, :half], vector[:, half:]
    return jnp.concatenate([first * cosine - second * sine, second * cosine + first * sine], axis=1)


def rotate_back(vector, cosine, sine):
    half = vector.shape[-1] // 2
    first, second = vector[:, :half], vector[:, half:]
    return jnp.concatenate([first * cosine + second * sine, second * cosine - first * sine], axis=1)


def own_rows(values):
    return values[: values.shape[0] // 2]


def join(*parts):
    return jnp.concatenate([part[...] for part in parts], axis=0)


def attn_fwd_kernel(*refs):
    xs, (w_all, mask, cos, sin, gains), bs = refs[:8], refs[8:13], refs[13:17]
    w, qraw_o, kraw_o, q_o, k_o, v_o, att_o, lse_o = refs[17:]
    hd = q_o.shape[1]
    half = w.shape[0] // 2
    slab = w_all.shape[1] // 2
    slabs = [w_all[d].astype(F32) for d in range(w_all.shape[0])]
    for side in (0, 1):
        rows = [both[side * slab : (side + 1) * slab] for both in slabs]
        w[side * half : (side + 1) * half, :] = jnp.concatenate(rows, axis=0).astype(BF)
    x = join(*xs)
    qraw = mm(own_rows(x), w[:, :hd])
    kv = mm(x, w[:, hd : 3 * hd])
    kraw = kv[:, :hd]
    cosine, sine = cos[...], sin[...]
    q = rotate(qraw * inv_rms(qraw) * gains[0:1, :], own_rows(cosine), own_rows(sine)).astype(BF)
    k = rotate(kraw * inv_rms(kraw) * gains[1:2, :], cosine, sine).astype(BF)
    v = kv[:, hd:].astype(BF)
    scores = mm(q, k, NT) * (hd**-0.5) + mask[...].astype(F32)
    largest = jnp.max(scores, axis=1, keepdims=True)
    weights = jnp.exp(scores - largest)
    total = jnp.sum(weights, axis=1, keepdims=True)
    att = mm((weights / total).astype(BF), v).astype(BF)
    branch = mm(att, w[:, 3 * hd :], NT).astype(BF)
    rows = bs[0].shape[0]
    for i, part in enumerate(bs):
        part[...] = branch[i * rows : (i + 1) * rows]
    qraw_o[...] = qraw
    kraw_o[...] = kraw
    q_o[...] = q
    k_o[...] = k
    v_o[...] = v
    att_o[...] = att
    lse_o[...] = jnp.broadcast_to(largest + jnp.log(total), lse_o.shape)


def attn_bwd_kernel(*refs):
    das, xs, refs = refs[:4], refs[4:12], refs[12:]
    w, mask, cos, sin, gains, qraw, kraw, q, k, v, att, lse = refs[:12]
    ns, (dw, dgains) = refs[12:20], refs[20:]
    hd = q.shape[1]
    half = q.shape[0]
    scale = hd**-0.5
    da = join(*das)
    datt = mm(da, w[:, 3 * hd :]).astype(BF)
    scores = mm(q[...], k[...], NT) * scale + mask[...].astype(F32)
    weights = jnp.exp(scores - lse[:, 0:1])
    dv = mm(weights.astype(BF), datt, TN).astype(BF)
    dp = mm(datt, v[...], NT)
    inner = jnp.sum(weights * dp, axis=1, keepdims=True)
    ds = (weights * (dp - inner)).astype(BF)
    dq = mm(ds, k[...]) * scale
    dk = mm(ds, q[...], TN) * scale
    cosine, sine = cos[...], sin[...]
    dqraw, dgq = norm_back(
        qraw[...], gains[0:1, :], rotate_back(dq, own_rows(cosine), own_rows(sine))
    )
    dkraw, dgk = norm_back(kraw[...], gains[1:2, :], rotate_back(dk, cosine, sine))
    dqraw, dkraw = dqraw.astype(BF), dkraw.astype(BF)
    dgains[0:1, :] = dgq
    dgains[1:2, :] = dgk
    x = join(*xs)
    width = x.shape[1]
    parts = (
        (mm(own_rows(x), dqraw, TN), 0),
        (mm(x, dkraw, TN), 1),
        (mm(x, dv, TN), 2),
        (mm(da, att[...], TN), 3),
    )
    slab = dw.shape[1] // 2
    for part, place in parts:
        for d in range(dw.shape[0]):
            both = [part[at : at + slab] for at in (d * slab, width // 2 + d * slab)]
            dw[d, :, place * hd : (place + 1) * hd] = jnp.concatenate(both, axis=0).astype(BF)
    back = mm(dkraw, w[:, hd : 2 * hd], NT) + mm(dv, w[:, 2 * hd : 3 * hd], NT)
    qback = mm(dqraw, w[:, :hd], NT)
    rows = ns[0].shape[0]
    for i, part in enumerate(ns):
        at = slice(i * rows, (i + 1) * rows)
        part[...] = (back[at] + qback[at] if i < 4 else back[at]).astype(BF)


def gelu_parts(gate):
    inner = GELU_C * (gate + 0.044715 * gate * gate * gate)
    th = jnp.tanh(inner)
    value = 0.5 * gate * (1.0 + th)
    slope = 0.5 * (1.0 + th) + 0.5 * gate * (1.0 - th * th) * GELU_C * (
        1.0 + 3.0 * 0.044715 * gate * gate
    )
    return value, slope


def ffn_fwd_kernel(*refs):
    xs, w, (slope_o, value_o, hidden_o), parts = refs[:8], refs[8], refs[9:12], refs[12:20]
    x, units, down = refs[20:]
    step = pl.program_id(0)
    slabs, _, rows, width = w.shape
    count = slabs * rows

    @pl.when(step == 0)
    def _():
        gather_rows(x, xs)

    gate = mm(x[...], w[:, 0].reshape(count, width), NT)
    up = mm(x[...], w[:, 1].reshape(count, width), NT)
    value, slope = gelu_parts(gate)
    hidden = (value * up).astype(BF)
    slope_o[...] = (slope * up).astype(BF)
    value_o[...] = value.astype(BF)
    hidden_o[...] = hidden
    units[step] = hidden
    down[pl.ds(pl.multiple_of(step * count, count), count), :] = w[:, 2].reshape(count, width)

    @pl.when(step == pl.num_programs(0) - 1)
    def _():
        whole = jnp.concatenate([units[i] for i in range(units.shape[0])], axis=1)
        total = mm(whole, down[...]).astype(BF)
        height = parts[0].shape[0]
        for i, part in enumerate(parts):
            part[...] = total[i * height : (i + 1) * height]


def gather_rows(whole, parts):
    height = parts[0].shape[0]
    for i, part in enumerate(parts):
        whole[i * height : (i + 1) * height, :] = part[...]


def accumulate(step, acc, term, *parts):
    last = pl.num_programs(0) - 1

    @pl.when(step == 0)
    def _():
        acc[...] = term

    @pl.when((step > 0) & (step < last))
    def _():
        acc[...] += term

    @pl.when(step == last)
    def _():
        total = (acc[...] + term).astype(BF)
        rows = parts[0].shape[0]
        for i, part in enumerate(parts):
            part[...] = total[i * rows : (i + 1) * rows]


def ffn_units_kernel(*refs):
    xs, ds, refs = refs[:8], refs[8:16], refs[16:]
    w, slope_i, value_i, hidden_i, dgate_o, dup_o, dw, x, d = refs
    slabs, _, rows, width = dw.shape

    @pl.when(pl.program_id(0) == 0)
    def _():
        gather_rows(x, xs)
        gather_rows(d, ds)

    dhid = mm(d[...], w[...].reshape(slabs * rows, width), NT)
    dgate = (dhid * slope_i[...].astype(F32)).astype(BF)
    dup = (dhid * value_i[...].astype(F32)).astype(BF)
    dgate_o[...] = dgate
    dup_o[...] = dup
    for i, (left, right) in enumerate(((dgate, x), (dup, x), (hidden_i[...], d))):
        dw[:, i] = mm(left, right[...], TN).astype(BF).reshape(slabs, rows, width)


def ffn_tokens_kernel(dgate, dup, w, *refs):
    parts, acc = refs[:8], refs[8]
    slabs, _, rows, width = w.shape
    term = mm(dgate[...], w[:, 0].reshape(slabs * rows, width)) + mm(
        dup[...], w[:, 1].reshape(slabs * rows, width)
    )
    accumulate(pl.program_id(0), acc, term, *parts)


def split(values, count):
    pieces = []
    for _ in range(count):
        pieces.append(values.astype(BF))
        values = values - pieces[-1].astype(F32)
    return pieces


def stacks(values):
    a, b = split(values, 2)
    return jnp.concatenate([a, a, b], axis=0), jnp.concatenate([a, b, a], axis=0)


def sym_parts(left, right, n):
    return [mm(left[:, at:], right[:, at : at + 256], TN) for at in range(0, n, 256)]


def sym_full(parts):
    columns = []
    for j, part in enumerate(parts):
        above = [parts[i][(j - i) * 256 : (j - i) * 256 + part.shape[1]].T for i in range(j)]
        columns.append(jnp.concatenate(above + [part], axis=0) if above else part)
    return jnp.concatenate(columns, axis=1) if len(columns) > 1 else columns[0]


def sym_mm(left, right, n):
    return sym_full(sym_parts(left, right, n))


def muon_chains(grams, currents):
    n = grams[0].shape[0]
    diag = lax.broadcasted_iota(jnp.int32, (n, n), 0) == lax.broadcasted_iota(jnp.int32, (n, n), 1)
    a, x = [], []
    for gram, current in zip(grams, currents):
        trace = jnp.sum(
            jnp.sum(jnp.where(diag, gram, 0.0), axis=1, keepdims=True), axis=0, keepdims=True
        )
        factor = 1.0 / (jnp.sqrt(trace) + MUON_EPS)
        a.append(gram * (factor * factor))
        x.append(current * factor)
    for step in range(NS_STEPS):
        sa = [stacks(m) for m in a]
        square = [sym_mm(l, r, n) for l, r in sa]
        poly = [COEF_B * m + COEF_C * q + jnp.where(diag, COEF_A, 0.0) for m, q in zip(a, square)]
        sp = [stacks(p) for p in poly]
        if step < NS_STEPS - 1:
            half = [stacks(sym_mm(l, sp[i][1], n)) for i, (l, _) in enumerate(sa)]
            a = [sym_mm(l, sp[i][1], n) for i, (l, _) in enumerate(half)]
        x = [mm(sp[i][0], stacks(m)[1], TN) for i, m in enumerate(x)]
    return x


def pack_rows(n):
    return sum(2 * (n - at) if n - at >= 256 else n - at for at in range(0, n, 256))


def ff_gram_kernel(flag, mine, theirs, mom_gu, mom_d, gu_o, d_o, gu_c, d_c, packed):
    first = flag[0] == 0
    n = mom_gu.shape[0]
    work = (((0, 1), mom_gu, gu_o, gu_c), ((2,), mom_d, d_o, d_c))
    for place, (kinds, mom, m_o, compact_o) in enumerate(work):
        rows = []
        for kind in kinds:
            own = mine[kind * PAD : (kind + 1) * PAD, :].astype(F32)
            got = theirs[kind * PAD : (kind + 1) * PAD, :].astype(F32)
            rows += [jnp.where(first, own, got), jnp.where(first, got, own)]
        part = mom.shape[1] // len(rows)
        blank = jnp.zeros((n, PAD - part), F32)
        spread = []
        for i in range(len(rows)):
            spread += [mom[:, i * part : (i + 1) * part], blank]
        m = MUON_DECAY * jnp.concatenate(spread, axis=1) + jnp.concatenate(rows, axis=0).T
        m_o[...] = m
        compact_o[...] = compact(m, compact_o.shape[1])
        pieces = []
        for start in range(0, n, 256):
            block = mm(m[start:], m[start : start + 256], NT, HIGH)
            if block.shape[1] == 256:
                pieces += [block[:, :128], block[:, 128:]]
            else:
                pieces.append(jnp.pad(block, ((0, 0), (0, 128 - block.shape[1]))))
        replicas, rows, _ = packed.shape
        rows //= 2
        whole = jnp.concatenate(pieces, axis=0)
        whole = jnp.pad(whole, ((0, replicas * rows - whole.shape[0]), (0, 0)))
        packed[:, place * rows : (place + 1) * rows, :] = whole.reshape(replicas, rows, 128)


def compact(values, width):
    count = values.shape[1] // PAD
    part = width // count
    return jnp.concatenate([values[:, i * PAD : i * PAD + part] for i in range(count)], axis=1)


def muon_large_kernel(scale, packed, m, out):
    n = m.shape[0]
    parts, at = [], 0
    for start in range(0, n, 256):
        rows, cols = n - start, min(256, n - start)
        if cols == 256:
            parts.append(
                jnp.concatenate(
                    [packed[at : at + rows, :], packed[at + rows : at + 2 * rows, :]], axis=1
                )
            )
            at += 2 * rows
        else:
            parts.append(packed[at : at + rows, :cols])
            at += rows
    (x,) = muon_chains([sym_full(parts)], [m[...]])
    out[...] = compact(x * scale, out.shape[1])


def muon_small_kernel(every, m, out, gains):
    count, rows, n = m.shape
    lead = every.shape[1] - gains.shape[0]
    step = lead // count
    grams = []
    for i in range(count):
        whole = every[:, i * step : (i + 1) * step, :].reshape(every.shape[0] * step, n)
        grams.append(mm(whole, whole, TN, HIGH))
    for i, x in enumerate(muon_chains(grams, [m[i].T for i in range(count)])):
        out[i] = x.T
    gains[...] = jnp.sum(every[:, lead:, :], axis=0)


def kernel(body, out_shape, flops, nbytes, vmem=32, **extra):
    return pl.pallas_call(
        body,
        out_shape=out_shape,
        compiler_params=pltpu.CompilerParams(vmem_limit_bytes=vmem * MIB),
        cost_estimate=pl.CostEstimate(flops=flops, bytes_accessed=nbytes, transcendentals=0),
        **extra,
    )


def sds(shape, dtype):
    return jax.ShapeDtypeStruct(shape, dtype)


def in_hbm(value):
    return pltpu.with_memory_space_constraint(value, pltpu.HBM)


def shards(
    tokens,
    cotangent,
    branch,
    w_query,
    w_keyval,
    w_out,
    w_gate_up,
    w_down,
    mom_query,
    mom_keyval,
    mom_out,
    mom_gate_up,
    mom_down,
    norm_gains,
    qk_gains,
    mom_norm,
    mom_qk,
):
    rows, width = tokens.shape
    hd = w_query.shape[3]
    replicas = lax.axis_size("dp")
    half = width // 2
    slab = half // replicas
    cols = w_down.shape[3] // half
    part = cols // 2
    row_index = lax.axis_index("row")
    col_index = lax.axis_index("col")
    me = row_index * 4 + col_index
    first_row = row_index == 0
    row_len = 4 * rows
    rep = 8 * rows

    ff_own = (
        jnp.concatenate(
            [
                w_gate_up.reshape(half, 2, cols).astype(BF).transpose(1, 2, 0),
                w_down.reshape(half, 1, cols).astype(BF).transpose(1, 2, 0),
            ],
            axis=0,
        )
        .reshape(3, 2, part, half)
    )
    ff_keep = jnp.where(first_row, ff_own[:, 0], ff_own[:, 1])
    ff_send = jnp.where(first_row, ff_own[:, 1], ff_own[:, 0])
    ff_send, wq, wk, wo = lax.optimization_barrier((ff_send, w_query, w_keyval, w_out))
    ff_got = flip(ff_send, 4)
    att_own = jnp.concatenate(
        [
            wq.reshape(slab, hd),
            wk[0].reshape(slab, hd),
            wk[1].reshape(slab, hd),
            wo.reshape(hd, slab).T,
        ],
        axis=1,
    ).astype(BF)
    att_other = flip(att_own, 4)
    att_pack = jnp.concatenate(
        [jnp.where(first_row, att_own, att_other), jnp.where(first_row, att_other, att_own)]
    )
    att_shares = jnp.broadcast_to(att_pack[None], (replicas,) + att_pack.shape)
    att_shares, tokens, mom_query, mom_keyval, mom_out, mom_gate_up, mom_down = (
        lax.optimization_barrier(
            (att_shares, tokens, mom_query, mom_keyval, mom_out, mom_gate_up, mom_down)
        )
    )
    ff_pack = jnp.concatenate(
        [jnp.where(first_row, ff_keep, ff_got), jnp.where(first_row, ff_got, ff_keep)], axis=2
    )
    ff_pack = jnp.pad(ff_pack, ((0, 0), (0, PAD - part), (0, 0)))
    ff_w = lax.all_gather(ff_pack.reshape(3 * PAD, width), "dp", axis=0, tiled=True)
    ff_w = ff_w.reshape(replicas, 3, PAD, width)
    att_all = swap_all(att_shares)
    mom_gu = mom_gate_up.reshape(half, 2 * cols)
    mom_d = mom_down.reshape(half, cols)
    mom_small = jnp.stack(
        [
            mom_query.reshape(slab, hd),
            mom_keyval[0].reshape(slab, hd),
            mom_keyval[1].reshape(slab, hd),
            mom_out.reshape(hd, slab).T,
        ]
    )
    att_all, mom_gu, mom_d, mom_small = lax.optimization_barrier((att_all, mom_gu, mom_d, mom_small))
    slots = jnp.asarray(
        [2 * k + core for pair in (0, 2) for core in (0, 1) for k in (pair, pair + 1)], jnp.int32
    )
    ids = ((me ^ slots)[:, None] * rows + jnp.arange(rows, dtype=jnp.int32)[None, :]).reshape(rep)
    starts = branch[0]
    in_prompt = ids < row_len
    offset = jnp.maximum(ids - row_len, 0)
    segment = jnp.where(in_prompt, -1, offset // CONT_LEN)
    start = jnp.max(
        jnp.where(
            segment[:, None] == jnp.arange(starts.shape[0], dtype=jnp.int32)[None, :],
            starts[None, :],
            0,
        ),
        axis=1,
    )
    position = jnp.where(in_prompt, ids, start + offset % CONT_LEN)
    q_seg, q_pos, q_start = own_rows(segment), own_rows(position), own_rows(start)
    same = (q_seg[:, None] == segment[None, :]) & (position[None, :] <= q_pos[:, None])
    forked = (q_seg[:, None] >= 0) & (segment[None, :] < 0) & (position[None, :] < q_start[:, None])
    seen = (same | forked) & (q_pos[:, None] - position[None, :] < WINDOW)
    mask = jnp.where(seen, 0.0, MASKED).astype(BF)
    steps = jnp.arange(hd // 2, dtype=F32) * (2.0 / hd)
    angle = position.astype(F32)[:, None] * jnp.exp(-math.log(ROPE_BASE) * steps)[None, :]
    cosine, sine = jnp.cos(angle), jnp.sin(angle)

    stream = tokens.astype(F32)
    normed = (stream * inv_rms(stream) * norm_gains[0]).astype(BF)
    normed_all = gather8(normed)
    *attn_parts, att_w, q_raw, k_raw, q, k, v, att, lse = kernel(
        attn_fwd_kernel,
        (sds((rows, width), BF),) * 4
        + (
            pltpu.HBM((width, 4 * hd), BF),
            pltpu.HBM((row_len, hd), F32),
            pltpu.HBM((rep, hd), F32),
            pltpu.HBM((row_len, hd), BF),
            pltpu.HBM((rep, hd), BF),
            pltpu.HBM((rep, hd), BF),
            pltpu.HBM((row_len, hd), BF),
            pltpu.HBM((row_len, 128), F32),
        ),
        3 * 10**9,
        12 * 10**6,
        name="attn_fwd",
    )(*normed_all, att_all, mask, in_hbm(cosine), in_hbm(sine), qk_gains)
    attn_branch = scatter4(attn_parts)
    middle = stream + attn_branch * inv_rms(attn_branch) * norm_gains[1]
    normed_ff = (middle * inv_rms(middle) * norm_gains[2]).astype(BF)

    nf_all = gather8(normed_ff)
    hidden_units = replicas * PAD
    part_spec = pl.BlockSpec((rows, width), lambda i: (0, 0))
    h_out = sds((rep, hidden_units), BF)
    x_out = sds((rows, width), BF)
    rows_all = pltpu.VMEM((rep, width), BF)

    def specs(group):
        return (
            pl.BlockSpec((group, 3, PAD, width), lambda i: (i, 0, 0, 0)),
            pl.BlockSpec((rep, group * PAD), lambda i: (0, i)),
        )

    w_spec, h_spec = specs(4)
    slope, value, hidden, *ff_parts = kernel(
        ffn_fwd_kernel,
        (h_out,) * 3 + (x_out,) * 8,
        8 * 10**9,
        20 * 10**6,
        grid=(replicas // 4,),
        in_specs=[part_spec] * 8 + [w_spec],
        out_specs=[h_spec] * 3 + [part_spec] * 8,
        scratch_shapes=[
            rows_all,
            pltpu.VMEM((replicas // 4, rep, 4 * PAD), BF),
            pltpu.VMEM((hidden_units, width), BF),
        ],
        name="ffn_fwd",
    )(*nf_all, in_hbm(ff_w))
    ff_branch = scatter8(ff_parts)
    layer_out = middle + ff_branch * inv_rms(ff_branch) * norm_gains[3]

    upstream = cotangent.astype(F32)
    ff_grad, grad_post_ff = norm_back(ff_branch, norm_gains[3], upstream)
    df_all = gather8(ff_grad.astype(BF))
    dgate, dup, ff_dw = kernel(
        ffn_units_kernel,
        (pltpu.HBM((rep, hidden_units), BF),) * 2 + (pltpu.HBM((replicas, 3, PAD, width), BF),),
        10 * 10**9,
        30 * 10**6,
        vmem=34,
        grid=(replicas // 8,),
        in_specs=[part_spec] * 16
        + [pl.BlockSpec((8, 1, PAD, width), lambda i: (i, 2, 0, 0))]
        + [specs(8)[1]] * 3,
        out_specs=[specs(8)[1]] * 2 + [specs(8)[0]],
        scratch_shapes=[rows_all, rows_all],
        name="ffn_units",
    )(*nf_all, *df_all, in_hbm(ff_w), slope, value, hidden)
    ff_sum = lax.psum_scatter(
        ff_dw.reshape(replicas * 3 * PAD, width), "dp", scatter_dimension=0, tiled=True
    )
    nf_parts = kernel(
        ffn_tokens_kernel,
        (x_out,) * 8,
        5 * 10**9,
        12 * 10**6,
        grid=(replicas // 8,),
        in_specs=[specs(8)[1]] * 2
        + [pl.BlockSpec((8, 2, PAD, width), lambda i: (i, 0, 0, 0))],
        out_specs=[part_spec] * 8,
        scratch_shapes=[pltpu.VMEM((rep, width), F32)],
        name="ffn_tokens",
    )(in_hbm(dgate), in_hbm(dup), in_hbm(ff_w))
    normed_ff_grad = scatter8(nf_parts)
    middle_part, grad_pre_ff = norm_back(middle, norm_gains[2], normed_ff_grad)
    middle_grad = upstream + middle_part
    attn_grad, grad_post = norm_back(attn_branch, norm_gains[1], middle_grad)

    da_all = gather4(attn_grad.astype(BF))
    *dn_parts, att_dw, grad_qk = kernel(
        attn_bwd_kernel,
        (x_out,) * 8 + (sds((replicas, 2 * slab, 4 * hd), BF), sds((2, hd), F32)),
        6 * 10**9,
        20 * 10**6,
        name="attn_bwd",
    )(*da_all, *normed_all, att_w, mask, cosine, sine, qk_gains, q_raw, k_raw, q, k, v, att, lse)
    att_got = swap_all(att_dw)
    normed_grad = scatter8(dn_parts)
    stream_part, grad_pre = norm_back(stream, norm_gains[0], normed_grad)
    input_grad = middle_grad + stream_part

    flag = row_index.astype(jnp.int32).reshape(1)

    low, high = ff_sum[:, :half], ff_sum[:, half:]
    mine = jnp.where(first_row, low, high)
    swapped = jnp.where(first_row, high, low)
    theirs = flip(swapped, 4)
    share_rows = -(-pack_rows(half) // (8 * replicas)) * 8
    vmem = pl.BlockSpec(memory_space=pltpu.VMEM)
    padded_gu, padded_d, new_gu, new_d, packed = kernel(
        ff_gram_kernel,
        (
            sds((half, 4 * PAD), F32),
            sds((half, 2 * PAD), F32),
            sds((half, 2 * cols), F32),
            sds((half, cols), F32),
            sds((replicas, 2 * share_rows, 128), F32),
        ),
        3 * 10**9,
        6 * 10**6,
        in_specs=[pl.BlockSpec(memory_space=pltpu.SMEM)] + [vmem] * 4,
        name="gram_ff",
    )(flag, mine, theirs, mom_gu, mom_d)
    gram_share = jnp.sum(swap_all(packed), axis=0)
    gram_share = gram_share.reshape(2, -1, 128)

    def everywhere(share):
        return swap_all(jnp.broadcast_to(share[None], (replicas,) + share.shape)).reshape(-1, 128)

    total_gu, total_d = everywhere(gram_share[0]), everywhere(gram_share[1])

    def orthogonal(total, padded, width, name):
        scale = MUON_RATE * math.sqrt(max(1.0, half / (width * replicas)))
        return kernel(
            functools.partial(muon_large_kernel, scale),
            sds((half, width), F32),
            12 * 10**9,
            5 * 10**6,
            name="muon_" + name,
        )(total, padded)

    att_sum = jnp.sum(after(att_got, swapped).astype(F32), axis=0)
    gain_part = jnp.concatenate([grad_pre, grad_post, grad_pre_ff, grad_post_ff], axis=0)
    gain_pack = jnp.concatenate([gain_part.reshape(-1), grad_qk.reshape(-1)])
    gain_rows = gain_pack.shape[0] // (4 * hd)
    gain_pack = gain_pack.reshape(gain_rows, 4 * hd)
    att_lo, att_hi = att_sum[:slab], att_sum[slab:]
    att_g = jnp.concatenate([jnp.where(first_row, att_lo, att_hi), gain_pack]) + flip(
        jnp.concatenate([jnp.where(first_row, att_hi, att_lo), gain_pack]), 4
    )
    ring_g = jnp.concatenate(
        [att_g[:slab, hd : 3 * hd], att_g[slab:].reshape(2 * gain_rows, 2 * hd)], axis=0
    )
    ring_g = ring_g + flip(ring_g, 1)
    ring_g = ring_g + flip(ring_g, 2)
    grad_small = jnp.stack(
        [att_g[:slab, :hd], ring_g[:slab, :hd], ring_g[:slab, hd:], att_g[:slab, 3 * hd :]]
    )
    new_small = MUON_DECAY * mom_small + grad_small
    tile = 8
    slab_rows = -(-slab // tile) * tile
    gains_in = ring_g[slab:].reshape(-1, hd)
    gain_tile = -(-gains_in.shape[0] // tile) * tile
    share = jnp.concatenate(
        [
            jnp.pad(new_small, ((0, 0), (0, slab_rows - slab), (0, 0))).reshape(-1, hd),
            jnp.pad(gains_in, ((0, gain_tile - gains_in.shape[0]), (0, 0))),
        ]
    )
    every = lax.all_gather(share, "dp", axis=0, tiled=True).reshape((replicas,) + share.shape)

    gu_x = orthogonal(total_gu, padded_gu, 2 * cols, "gu")
    d_x = orthogonal(after(total_d, gu_x), padded_d, cols, "down")
    small_x, gain_sum = kernel(
        muon_small_kernel,
        (sds((4, slab, hd), F32), sds((gain_tile, hd), F32)),
        2 * 10**9,
        4 * 10**6,
        name="muon_small",
    )(in_hbm(after(every, d_x)), new_small)
    gain_sum = gain_sum.reshape(-1)
    norm_total = gain_sum[: 4 * width].reshape(4, width)
    qk_total = gain_sum[4 * width : 4 * width + 2 * hd].reshape(2, hd)

    shrink = 1.0 - MUON_RATE * WEIGHT_DECAY
    tall = MUON_RATE * math.sqrt(max(1.0, half / hd))
    flat = MUON_RATE * math.sqrt(max(1.0, hd / half))
    new_query = w_query * shrink - tall * small_x[0].reshape(w_query.shape)
    new_keyval = w_keyval * shrink - tall * small_x[1:3].reshape(w_keyval.shape)
    new_out = w_out * shrink - flat * small_x[3].T.reshape(w_out.shape)
    new_gate_up = w_gate_up * shrink - gu_x.reshape(w_gate_up.shape)
    new_down = w_down * shrink - d_x.reshape(w_down.shape)
    norm_renewed = GAIN_MOMENTUM * mom_norm + norm_total
    qk_renewed = GAIN_MOMENTUM * mom_qk + qk_total
    return (
        layer_out.astype(BF),
        input_grad,
        new_small[0].reshape(mom_query.shape),
        new_query,
        new_query.astype(BF),
        new_small[1:3].reshape(mom_keyval.shape),
        new_keyval,
        new_keyval.astype(BF),
        new_small[3].T.reshape(mom_out.shape),
        new_out,
        new_out.astype(BF),
        new_gu.reshape(mom_gate_up.shape),
        new_gate_up,
        new_gate_up.astype(BF),
        new_d.reshape(mom_down.shape),
        new_down,
        new_down.astype(BF),
        norm_renewed,
        norm_gains - GAIN_RATE * norm_renewed,
        qk_renewed,
        qk_gains - GAIN_RATE * qk_renewed,
    )


def solution(mesh):
    tok = P(("dp", "row", "col"), None)
    query = P("row", "dp", "col", None)
    keyval = P(None, "row", "dp", None)
    out = P("col", None, "row", "dp")
    slabs = P("row", "col", "dp", None)
    weights = (query, keyval, out, slabs, slabs)
    in_specs = (tok, tok, P("dp", None)) + weights + weights + (P(),) * 4
    out_specs = (tok, tok) + tuple(spec for spec in weights for _ in range(3)) + (P(),) * 4
    return jax.shard_map(shards, mesh=mesh, in_specs=in_specs, out_specs=out_specs, check_vma=False)
```

```python
import functools
import math

import jax
import jax.numpy as jnp
from jax import lax
from jax.experimental import pallas as pl
from jax.experimental.pallas import tpu as pltpu
from jax.sharding import PartitionSpec as P

CONT_LEN = 256
WINDOW = 512
NS_STEPS = 5
NORM_EPS = 1e-06
MUON_EPS = 1e-07
COEF_A = 3.4445
COEF_B = -4.775
COEF_C = 2.0315
MUON_RATE = 0.5
MUON_DECAY = 0.5
WEIGHT_DECAY = 0.01
GAIN_RATE = 0.003
GAIN_MOMENTUM = 0.5
ROPE_BASE = 10000.0
HIGH = lax.Precision.HIGHEST
BF = jnp.bfloat16
F32 = jnp.float32
RING = ("row", "col")
MASKED = -1e30
MIB = 2**20
PAD = 64
GELU_C = math.sqrt(2.0 / math.pi)

NN = (((1,), (0,)), ((), ()))
NT = (((1,), (1,)), ((), ()))
TN = (((0,), (0,)), ((), ()))


def mm(left, right, dims=NN, precision=None):
    return lax.dot_general(left, right, dims, precision=precision, preferred_element_type=F32)


def flip(block, bits):
    return lax.ppermute(block, RING, [(i, i ^ bits) for i in range(8)])


def gather4(block):
    near = [block, flip(block, 2)]
    return near + [flip(part, 1) for part in near]


def gather8(block):
    near = [flip(block, 4), flip(block, 6)]
    return gather4(block) + near + [flip(part, 1) for part in near]


def scatter8(parts):
    def paired(near, far):
        return near.astype(F32) + flip(far, 1).astype(F32)

    across, last = paired(parts[4], parts[6]), paired(parts[5], parts[7])
    beside, total = paired(parts[1], parts[3]), paired(parts[0], parts[2])
    for value, bits in ((across, 4), (last, 6), (beside, 2)):
        total = total + flip(value.astype(BF), bits).astype(F32)
    return total


def scatter4(parts):
    beside = parts[1].astype(F32) + flip(parts[3], 1).astype(F32)
    total = parts[0].astype(F32) + flip(parts[2], 1).astype(F32)
    return total + flip(beside.astype(BF), 2).astype(F32)


def after(value, *others):
    return lax.optimization_barrier((value,) + others)[0]


def swap_all(blocks):
    return lax.all_to_all(blocks, "dp", 0, 0, tiled=True)


def inv_rms(vector):
    return lax.rsqrt(jnp.mean(vector * vector, axis=-1, keepdims=True) + NORM_EPS)


def norm_back(vector, gain, grad):
    scale = inv_rms(vector)
    gz = grad * gain
    du = scale * gz - vector * (scale * scale * scale) * jnp.mean(
        gz * vector, axis=-1, keepdims=True
    )
    return du, jnp.sum(grad * vector * scale, axis=0, keepdims=True)


def rotate(vector, cosine, sine):
    half = vector.shape[-1] // 2
    first, second = vector[:, :half], vector[:, half:]
    return jnp.concatenate([first * cosine - second * sine, second * cosine + first * sine], axis=1)


def rotate_back(vector, cosine, sine):
    half = vector.shape[-1] // 2
    first, second = vector[:, :half], vector[:, half:]
    return jnp.concatenate([first * cosine + second * sine, second * cosine - first * sine], axis=1)


def own_rows(values):
    return values[: values.shape[0] // 2]


def join(*parts):
    return jnp.concatenate([part[...] for part in parts], axis=0)


def attn_fwd_kernel(*refs):
    xs, (w_all, mask, cos, sin, gains), bs = refs[:8], refs[8:13], refs[13:17]
    w, qraw_o, kraw_o, q_o, k_o, v_o, att_o, lse_o = refs[17:]
    hd = q_o.shape[1]
    half = w.shape[0] // 2
    slab = w_all.shape[1] // 2
    slabs = [w_all[d].astype(F32) for d in range(w_all.shape[0])]
    for side in (0, 1):
        rows = [both[side * slab : (side + 1) * slab] for both in slabs]
        w[side * half : (side + 1) * half, :] = jnp.concatenate(rows, axis=0).astype(BF)
    x = join(*xs)
    qraw = mm(own_rows(x), w[:, :hd])
    kv = mm(x, w[:, hd : 3 * hd])
    kraw = kv[:, :hd]
    cosine, sine = cos[...], sin[...]
    q = rotate(qraw * inv_rms(qraw) * gains[0:1, :], own_rows(cosine), own_rows(sine)).astype(BF)
    k = rotate(kraw * inv_rms(kraw) * gains[1:2, :], cosine, sine).astype(BF)
    v = kv[:, hd:].astype(BF)
    scores = mm(q, k, NT) * (hd**-0.5) + mask[...].astype(F32)
    largest = jnp.max(scores, axis=1, keepdims=True)
    weights = jnp.exp(scores - largest)
    total = jnp.sum(weights, axis=1, keepdims=True)
    att = mm((weights / total).astype(BF), v).astype(BF)
    branch = mm(att, w[:, 3 * hd :], NT).astype(BF)
    rows = bs[0].shape[0]
    for i, part in enumerate(bs):
        part[...] = branch[i * rows : (i + 1) * rows]
    qraw_o[...] = qraw
    kraw_o[...] = kraw
    q_o[...] = q
    k_o[...] = k
    v_o[...] = v
    att_o[...] = att
    lse_o[...] = jnp.broadcast_to(largest + jnp.log(total), lse_o.shape)


def attn_bwd_kernel(*refs):
    das, xs, refs = refs[:4], refs[4:12], refs[12:]
    w, mask, cos, sin, gains, qraw, kraw, q, k, v, att, lse = refs[:12]
    ns, (dw, dgains) = refs[12:20], refs[20:]
    hd = q.shape[1]
    half = q.shape[0]
    scale = hd**-0.5
    da = join(*das)
    datt = mm(da, w[:, 3 * hd :]).astype(BF)
    scores = mm(q[...], k[...], NT) * scale + mask[...].astype(F32)
    weights = jnp.exp(scores - lse[:, 0:1])
    dv = mm(weights.astype(BF), datt, TN).astype(BF)
    dp = mm(datt, v[...], NT)
    inner = jnp.sum(weights * dp, axis=1, keepdims=True)
    ds = (weights * (dp - inner)).astype(BF)
    dq = mm(ds, k[...]) * scale
    dk = mm(ds, q[...], TN) * scale
    cosine, sine = cos[...], sin[...]
    dqraw, dgq = norm_back(
        qraw[...], gains[0:1, :], rotate_back(dq, own_rows(cosine), own_rows(sine))
    )
    dkraw, dgk = norm_back(kraw[...], gains[1:2, :], rotate_back(dk, cosine, sine))
    dqraw, dkraw = dqraw.astype(BF), dkraw.astype(BF)
    dgains[0:1, :] = dgq
    dgains[1:2, :] = dgk
    x = join(*xs)
    width = x.shape[1]
    parts = (
        (mm(own_rows(x), dqraw, TN), 0),
        (mm(x, dkraw, TN), 1),
        (mm(x, dv, TN), 2),
        (mm(da, att[...], TN), 3),
    )
    slab = dw.shape[1] // 2
    for part, place in parts:
        for d in range(dw.shape[0]):
            both = [part[at : at + slab] for at in (d * slab, width // 2 + d * slab)]
            dw[d, :, place * hd : (place + 1) * hd] = jnp.concatenate(both, axis=0).astype(BF)
    back = mm(dkraw, w[:, hd : 2 * hd], NT) + mm(dv, w[:, 2 * hd : 3 * hd], NT)
    qback = mm(dqraw, w[:, :hd], NT)
    rows = ns[0].shape[0]
    for i, part in enumerate(ns):
        at = slice(i * rows, (i + 1) * rows)
        part[...] = (back[at] + qback[at] if i < 4 else back[at]).astype(BF)


def gelu_parts(gate):
    cube = GELU_C * 0.044715
    square = gate * gate
    h = 0.5 * jnp.tanh(gate * (cube * square + GELU_C)) + 0.5
    value = gate * h
    slope = h + value * (1.0 - h) * (6.0 * cube * square + 2.0 * GELU_C)
    return value, slope


def ffn_fwd_kernel(*refs):
    xs, w, (slope_o, value_o, hidden_o), parts = refs[:8], refs[8], refs[9:12], refs[12:20]
    x, units, down = refs[20:]
    step = pl.program_id(0)
    slabs, _, rows, width = w.shape
    count = slabs * rows

    @pl.when(step == 0)
    def _():
        gather_rows(x, xs)

    gate = mm(x[...], w[:, 0].reshape(count, width), NT)
    up = mm(x[...], w[:, 1].reshape(count, width), NT)
    value, slope = gelu_parts(gate)
    hidden = (value * up).astype(BF)
    slope_o[...] = (slope * up).astype(BF)
    value_o[...] = value.astype(BF)
    hidden_o[...] = hidden
    units[step] = hidden
    down[pl.ds(pl.multiple_of(step * count, count), count), :] = w[:, 2].reshape(count, width)

    @pl.when(step == pl.num_programs(0) - 1)
    def _():
        whole = jnp.concatenate([units[i] for i in range(units.shape[0])], axis=1)
        total = mm(whole, down[...]).astype(BF)
        height = parts[0].shape[0]
        for i, part in enumerate(parts):
            part[...] = total[i * height : (i + 1) * height]


def gather_rows(whole, parts):
    height = parts[0].shape[0]
    for i, part in enumerate(parts):
        whole[i * height : (i + 1) * height, :] = part[...]


def accumulate(step, acc, term, *parts):
    last = pl.num_programs(0) - 1

    @pl.when(step == 0)
    def _():
        acc[...] = term

    @pl.when((step > 0) & (step < last))
    def _():
        acc[...] += term

    @pl.when(step == last)
    def _():
        total = (acc[...] + term).astype(BF)
        rows = parts[0].shape[0]
        for i, part in enumerate(parts):
            part[...] = total[i * rows : (i + 1) * rows]


def ffn_units_kernel(*refs):
    xs, ds, refs = refs[:8], refs[8:16], refs[16:]
    w, slope_i, value_i, hidden_i, dgate_o, dup_o, dw, x, d = refs
    slabs, _, rows, width = dw.shape

    @pl.when(pl.program_id(0) == 0)
    def _():
        gather_rows(x, xs)
        gather_rows(d, ds)

    dhid = mm(d[...], w[...].reshape(slabs * rows, width), NT)
    dgate = (dhid * slope_i[...].astype(F32)).astype(BF)
    dup = (dhid * value_i[...].astype(F32)).astype(BF)
    dgate_o[...] = dgate
    dup_o[...] = dup
    for i, (left, right) in enumerate(((dgate, x), (dup, x), (hidden_i[...], d))):
        dw[:, i] = mm(left, right[...], TN).astype(BF).reshape(slabs, rows, width)


def ffn_tokens_kernel(dgate, dup, w, *refs):
    parts, acc = refs[:8], refs[8]
    slabs, _, rows, width = w.shape
    term = mm(dgate[...], w[:, 0].reshape(slabs * rows, width)) + mm(
        dup[...], w[:, 1].reshape(slabs * rows, width)
    )
    accumulate(pl.program_id(0), acc, term, *parts)


def split(values, count):
    pieces = []
    for _ in range(count):
        pieces.append(values.astype(BF))
        values = values - pieces[-1].astype(F32)
    return pieces


def stacks(values):
    a, b = split(values, 2)
    return jnp.concatenate([a, a, b], axis=0), jnp.concatenate([a, b, a], axis=0)


def sym_parts(left, right, n):
    return [mm(left[:, at:], right[:, at : at + 256], TN) for at in range(0, n, 256)]


def sym_full(parts):
    columns = []
    for j, part in enumerate(parts):
        above = [parts[i][(j - i) * 256 : (j - i) * 256 + part.shape[1]].T for i in range(j)]
        columns.append(jnp.concatenate(above + [part], axis=0) if above else part)
    return jnp.concatenate(columns, axis=1) if len(columns) > 1 else columns[0]


def sym_mm(left, right, n):
    return sym_full(sym_parts(left, right, n))


def muon_chains(grams, currents):
    n = grams[0].shape[0]
    diag = lax.broadcasted_iota(jnp.int32, (n, n), 0) == lax.broadcasted_iota(jnp.int32, (n, n), 1)
    a, x = [], []
    for gram, current in zip(grams, currents):
        trace = jnp.sum(
            jnp.sum(jnp.where(diag, gram, 0.0), axis=1, keepdims=True), axis=0, keepdims=True
        )
        factor = 1.0 / (jnp.sqrt(trace) + MUON_EPS)
        a.append(gram * (factor * factor))
        x.append(current * factor)
    for step in range(NS_STEPS):
        sa = [stacks(m) for m in a]
        square = [sym_mm(l, r, n) for l, r in sa]
        poly = [COEF_B * m + COEF_C * q + jnp.where(diag, COEF_A, 0.0) for m, q in zip(a, square)]
        sp = [stacks(p) for p in poly]
        if step < NS_STEPS - 1:
            half = [stacks(sym_mm(l, sp[i][1], n)) for i, (l, _) in enumerate(sa)]
            a = [sym_mm(l, sp[i][1], n) for i, (l, _) in enumerate(half)]
        x = [mm(sp[i][0], stacks(m)[1], TN) for i, m in enumerate(x)]
    return x


def pack_rows(n):
    return sum(2 * (n - at) if n - at >= 256 else n - at for at in range(0, n, 256))


def ff_gram_kernel(flag, mine, theirs, mom_gu, mom_d, gu_o, d_o, gu_c, d_c, packed):
    first = flag[0] == 0
    n = mom_gu.shape[0]
    work = (((0, 1), mom_gu, gu_o, gu_c), ((2,), mom_d, d_o, d_c))
    for place, (kinds, mom, m_o, compact_o) in enumerate(work):
        rows = []
        for kind in kinds:
            own = mine[kind * PAD : (kind + 1) * PAD, :].astype(F32)
            got = theirs[kind * PAD : (kind + 1) * PAD, :].astype(F32)
            rows += [jnp.where(first, own, got), jnp.where(first, got, own)]
        part = mom.shape[1] // len(rows)
        blank = jnp.zeros((n, PAD - part), F32)
        spread = []
        for i in range(len(rows)):
            spread += [mom[:, i * part : (i + 1) * part], blank]
        m = MUON_DECAY * jnp.concatenate(spread, axis=1) + jnp.concatenate(rows, axis=0).T
        m_o[...] = m
        compact_o[...] = compact(m, compact_o.shape[1])
        pieces = []
        for start in range(0, n, 256):
            block = mm(m[start:], m[start : start + 256], NT, HIGH)
            if block.shape[1] == 256:
                pieces += [block[:, :128], block[:, 128:]]
            else:
                pieces.append(jnp.pad(block, ((0, 0), (0, 128 - block.shape[1]))))
        replicas, rows, _ = packed.shape
        rows //= 2
        whole = jnp.concatenate(pieces, axis=0)
        whole = jnp.pad(whole, ((0, replicas * rows - whole.shape[0]), (0, 0)))
        packed[:, place * rows : (place + 1) * rows, :] = whole.reshape(replicas, rows, 128)


def compact(values, width):
    count = values.shape[1] // PAD
    part = width // count
    return jnp.concatenate([values[:, i * PAD : i * PAD + part] for i in range(count)], axis=1)


def muon_large_kernel(scale, packed, m, out):
    n = m.shape[0]
    parts, at = [], 0
    for start in range(0, n, 256):
        rows, cols = n - start, min(256, n - start)
        if cols == 256:
            parts.append(
                jnp.concatenate(
                    [packed[at : at + rows, :], packed[at + rows : at + 2 * rows, :]], axis=1
                )
            )
            at += 2 * rows
        else:
            parts.append(packed[at : at + rows, :cols])
            at += rows
    (x,) = muon_chains([sym_full(parts)], [m[...]])
    out[...] = compact(x * scale, out.shape[1])


def muon_small_kernel(every, m, out, gains):
    count, rows, n = m.shape
    lead = every.shape[1] - gains.shape[0]
    step = lead // count
    grams = []
    for i in range(count):
        whole = every[:, i * step : (i + 1) * step, :].reshape(every.shape[0] * step, n)
        grams.append(mm(whole, whole, TN, HIGH))
    for i, x in enumerate(muon_chains(grams, [m[i].T for i in range(count)])):
        out[i] = x.T
    gains[...] = jnp.sum(every[:, lead:, :], axis=0)


def kernel(body, out_shape, flops, nbytes, vmem=32, **extra):
    return pl.pallas_call(
        body,
        out_shape=out_shape,
        compiler_params=pltpu.CompilerParams(vmem_limit_bytes=vmem * MIB),
        cost_estimate=pl.CostEstimate(flops=flops, bytes_accessed=nbytes, transcendentals=0),
        **extra,
    )


def sds(shape, dtype):
    return jax.ShapeDtypeStruct(shape, dtype)


def in_hbm(value):
    return pltpu.with_memory_space_constraint(value, pltpu.HBM)


def shards(
    tokens,
    cotangent,
    branch,
    w_query,
    w_keyval,
    w_out,
    w_gate_up,
    w_down,
    mom_query,
    mom_keyval,
    mom_out,
    mom_gate_up,
    mom_down,
    norm_gains,
    qk_gains,
    mom_norm,
    mom_qk,
):
    rows, width = tokens.shape
    hd = w_query.shape[3]
    replicas = lax.axis_size("dp")
    half = width // 2
    slab = half // replicas
    cols = w_down.shape[3] // half
    part = cols // 2
    row_index = lax.axis_index("row")
    col_index = lax.axis_index("col")
    me = row_index * 4 + col_index
    first_row = row_index == 0
    row_len = 4 * rows
    rep = 8 * rows

    ff_own = (
        jnp.concatenate(
            [
                w_gate_up.reshape(half, 2, cols).astype(BF).transpose(1, 2, 0),
                w_down.reshape(half, 1, cols).astype(BF).transpose(1, 2, 0),
            ],
            axis=0,
        )
        .reshape(3, 2, part, half)
    )
    ff_keep = jnp.where(first_row, ff_own[:, 0], ff_own[:, 1])
    ff_send = jnp.where(first_row, ff_own[:, 1], ff_own[:, 0])
    ff_send, wq, wk, wo = lax.optimization_barrier((ff_send, w_query, w_keyval, w_out))
    ff_got = flip(ff_send, 4)
    att_own = jnp.concatenate(
        [
            wq.reshape(slab, hd),
            wk[0].reshape(slab, hd),
            wk[1].reshape(slab, hd),
            wo.reshape(hd, slab).T,
        ],
        axis=1,
    ).astype(BF)
    att_other = flip(att_own, 4)
    att_pack = jnp.concatenate(
        [jnp.where(first_row, att_own, att_other), jnp.where(first_row, att_other, att_own)]
    )
    att_shares = jnp.broadcast_to(att_pack[None], (replicas,) + att_pack.shape)
    att_shares, tokens, mom_query, mom_keyval, mom_out, mom_gate_up, mom_down = (
        lax.optimization_barrier(
            (att_shares, tokens, mom_query, mom_keyval, mom_out, mom_gate_up, mom_down)
        )
    )
    ff_pack = jnp.concatenate(
        [jnp.where(first_row, ff_keep, ff_got), jnp.where(first_row, ff_got, ff_keep)], axis=2
    )
    ff_pack = after(jnp.pad(ff_pack, ((0, 0), (0, PAD - part), (0, 0))), att_shares)
    ff_w = lax.all_gather(ff_pack.reshape(3 * PAD, width), "dp", axis=0, tiled=True)
    ff_w = ff_w.reshape(replicas, 3, PAD, width)
    att_all = swap_all(att_shares)
    mom_gu = mom_gate_up.reshape(half, 2 * cols)
    mom_d = mom_down.reshape(half, cols)
    mom_small = jnp.stack(
        [
            mom_query.reshape(slab, hd),
            mom_keyval[0].reshape(slab, hd),
            mom_keyval[1].reshape(slab, hd),
            mom_out.reshape(hd, slab).T,
        ]
    )
    att_all, mom_gu, mom_d, mom_small = lax.optimization_barrier((att_all, mom_gu, mom_d, mom_small))
    slots = jnp.asarray(
        [2 * k + core for pair in (0, 2) for core in (0, 1) for k in (pair, pair + 1)], jnp.int32
    )
    ids = ((me ^ slots)[:, None] * rows + jnp.arange(rows, dtype=jnp.int32)[None, :]).reshape(rep)
    starts = branch[0]
    in_prompt = ids < row_len
    offset = jnp.maximum(ids - row_len, 0)
    segment = jnp.where(in_prompt, -1, offset // CONT_LEN)
    start = jnp.max(
        jnp.where(
            segment[:, None] == jnp.arange(starts.shape[0], dtype=jnp.int32)[None, :],
            starts[None, :],
            0,
        ),
        axis=1,
    )
    position = jnp.where(in_prompt, ids, start + offset % CONT_LEN)
    q_seg, q_pos, q_start = own_rows(segment), own_rows(position), own_rows(start)
    same = (q_seg[:, None] == segment[None, :]) & (position[None, :] <= q_pos[:, None])
    forked = (q_seg[:, None] >= 0) & (segment[None, :] < 0) & (position[None, :] < q_start[:, None])
    seen = (same | forked) & (q_pos[:, None] - position[None, :] < WINDOW)
    mask = jnp.where(seen, 0.0, MASKED).astype(BF)
    steps = jnp.arange(hd // 2, dtype=F32) * (2.0 / hd)
    angle = position.astype(F32)[:, None] * jnp.exp(-math.log(ROPE_BASE) * steps)[None, :]
    cosine, sine = jnp.cos(angle), jnp.sin(angle)

    stream = tokens.astype(F32)
    normed = (stream * inv_rms(stream) * norm_gains[0]).astype(BF)
    normed_all = gather8(normed)
    *attn_parts, att_w, q_raw, k_raw, q, k, v, att, lse = kernel(
        attn_fwd_kernel,
        (sds((rows, width), BF),) * 4
        + (
            pltpu.HBM((width, 4 * hd), BF),
            pltpu.HBM((row_len, hd), F32),
            pltpu.HBM((rep, hd), F32),
            pltpu.HBM((row_len, hd), BF),
            pltpu.HBM((rep, hd), BF),
            pltpu.HBM((rep, hd), BF),
            pltpu.HBM((row_len, hd), BF),
            pltpu.HBM((row_len, 128), F32),
        ),
        3 * 10**9,
        12 * 10**6,
        name="attn_fwd",
    )(*normed_all, att_all, mask, in_hbm(cosine), in_hbm(sine), qk_gains)
    attn_branch = scatter4(attn_parts)
    middle = stream + attn_branch * inv_rms(attn_branch) * norm_gains[1]
    normed_ff = (middle * inv_rms(middle) * norm_gains[2]).astype(BF)

    nf_all = gather8(normed_ff)
    hidden_units = replicas * PAD
    part_spec = pl.BlockSpec((rows, width), lambda i: (0, 0))
    h_out = sds((rep, hidden_units), BF)
    x_out = sds((rows, width), BF)
    rows_all = pltpu.VMEM((rep, width), BF)

    def specs(group):
        return (
            pl.BlockSpec((group, 3, PAD, width), lambda i: (i, 0, 0, 0)),
            pl.BlockSpec((rep, group * PAD), lambda i: (0, i)),
        )

    w_spec, h_spec = specs(4)
    slope, value, hidden, *ff_parts = kernel(
        ffn_fwd_kernel,
        (h_out,) * 3 + (x_out,) * 8,
        8 * 10**9,
        20 * 10**6,
        grid=(replicas // 4,),
        in_specs=[part_spec] * 8 + [w_spec],
        out_specs=[h_spec] * 3 + [part_spec] * 8,
        scratch_shapes=[
            rows_all,
            pltpu.VMEM((replicas // 4, rep, 4 * PAD), BF),
            pltpu.VMEM((hidden_units, width), BF),
        ],
        name="ffn_fwd",
    )(*nf_all, in_hbm(ff_w))
    ff_branch = scatter8(ff_parts)
    layer_out = middle + ff_branch * inv_rms(ff_branch) * norm_gains[3]

    upstream = cotangent.astype(F32)
    ff_grad, grad_post_ff = norm_back(ff_branch, norm_gains[3], upstream)
    df_all = gather8(ff_grad.astype(BF))
    dgate, dup, ff_dw = kernel(
        ffn_units_kernel,
        (pltpu.HBM((rep, hidden_units), BF),) * 2 + (pltpu.HBM((replicas, 3, PAD, width), BF),),
        10 * 10**9,
        30 * 10**6,
        vmem=34,
        grid=(replicas // 8,),
        in_specs=[part_spec] * 16
        + [pl.BlockSpec((8, 1, PAD, width), lambda i: (i, 2, 0, 0))]
        + [specs(8)[1]] * 3,
        out_specs=[specs(8)[1]] * 2 + [specs(8)[0]],
        scratch_shapes=[rows_all, rows_all],
        name="ffn_units",
    )(*nf_all, *df_all, in_hbm(ff_w), slope, value, hidden)
    ff_sum = lax.psum_scatter(
        ff_dw.reshape(replicas * 3 * PAD, width), "dp", scatter_dimension=0, tiled=True
    )
    nf_parts = kernel(
        ffn_tokens_kernel,
        (x_out,) * 8,
        5 * 10**9,
        12 * 10**6,
        grid=(replicas // 8,),
        in_specs=[specs(8)[1]] * 2
        + [pl.BlockSpec((8, 2, PAD, width), lambda i: (i, 0, 0, 0))],
        out_specs=[part_spec] * 8,
        scratch_shapes=[pltpu.VMEM((rep, width), F32)],
        name="ffn_tokens",
    )(in_hbm(dgate), in_hbm(dup), in_hbm(ff_w))
    normed_ff_grad = scatter8(nf_parts)
    middle_part, grad_pre_ff = norm_back(middle, norm_gains[2], normed_ff_grad)
    middle_grad = upstream + middle_part
    attn_grad, grad_post = norm_back(attn_branch, norm_gains[1], middle_grad)

    da_all = gather4(attn_grad.astype(BF))
    *dn_parts, att_dw, grad_qk = kernel(
        attn_bwd_kernel,
        (x_out,) * 8 + (sds((replicas, 2 * slab, 4 * hd), BF), sds((2, hd), F32)),
        6 * 10**9,
        20 * 10**6,
        name="attn_bwd",
    )(*da_all, *normed_all, att_w, mask, cosine, sine, qk_gains, q_raw, k_raw, q, k, v, att, lse)
    att_got = swap_all(att_dw)
    normed_grad = scatter8(dn_parts)
    stream_part, grad_pre = norm_back(stream, norm_gains[0], normed_grad)
    input_grad = middle_grad + stream_part

    flag = row_index.astype(jnp.int32).reshape(1)

    low, high = ff_sum[:, :half], ff_sum[:, half:]
    mine = jnp.where(first_row, low, high)
    swapped = jnp.where(first_row, high, low)
    theirs = flip(swapped, 4)
    share_rows = -(-pack_rows(half) // (8 * replicas)) * 8
    vmem = pl.BlockSpec(memory_space=pltpu.VMEM)
    padded_gu, padded_d, new_gu, new_d, packed = kernel(
        ff_gram_kernel,
        (
            sds((half, 4 * PAD), F32),
            sds((half, 2 * PAD), F32),
            sds((half, 2 * cols), F32),
            sds((half, cols), F32),
            sds((replicas, 2 * share_rows, 128), F32),
        ),
        3 * 10**9,
        6 * 10**6,
        in_specs=[pl.BlockSpec(memory_space=pltpu.SMEM)] + [vmem] * 4,
        name="gram_ff",
    )(flag, mine, theirs, mom_gu, mom_d)
    gram_share = jnp.sum(swap_all(packed), axis=0)
    gram_share = gram_share.reshape(2, -1, 128)

    def everywhere(share):
        return swap_all(jnp.broadcast_to(share[None], (replicas,) + share.shape)).reshape(-1, 128)

    total_gu, total_d = everywhere(gram_share[0]), everywhere(gram_share[1])

    def orthogonal(total, padded, width, name):
        scale = MUON_RATE * math.sqrt(max(1.0, half / (width * replicas)))
        return kernel(
            functools.partial(muon_large_kernel, scale),
            sds((half, width), F32),
            12 * 10**9,
            5 * 10**6,
            name="muon_" + name,
        )(total, padded)

    att_sum = jnp.sum(after(att_got, swapped).astype(F32), axis=0)
    gain_part = jnp.concatenate([grad_pre, grad_post, grad_pre_ff, grad_post_ff], axis=0)
    gain_pack = jnp.concatenate([gain_part.reshape(-1), grad_qk.reshape(-1)])
    gain_rows = gain_pack.shape[0] // (4 * hd)
    gain_pack = gain_pack.reshape(gain_rows, 4 * hd)
    att_lo, att_hi = att_sum[:slab], att_sum[slab:]
    att_g = jnp.concatenate([jnp.where(first_row, att_lo, att_hi), gain_pack]) + flip(
        jnp.concatenate([jnp.where(first_row, att_hi, att_lo), gain_pack]), 4
    )
    ring_g = jnp.concatenate(
        [att_g[:slab, hd : 3 * hd], att_g[slab:].reshape(2 * gain_rows, 2 * hd)], axis=0
    )
    ring_g = ring_g + flip(ring_g, 1)
    ring_g = ring_g + flip(ring_g, 2)
    grad_small = jnp.stack(
        [att_g[:slab, :hd], ring_g[:slab, :hd], ring_g[:slab, hd:], att_g[:slab, 3 * hd :]]
    )
    new_small = MUON_DECAY * mom_small + grad_small
    tile = 8
    slab_rows = -(-slab // tile) * tile
    gains_in = ring_g[slab:].reshape(-1, hd)
    gain_tile = -(-gains_in.shape[0] // tile) * tile
    share = jnp.concatenate(
        [
            jnp.pad(new_small, ((0, 0), (0, slab_rows - slab), (0, 0))).reshape(-1, hd),
            jnp.pad(gains_in, ((0, gain_tile - gains_in.shape[0]), (0, 0))),
        ]
    )
    every = lax.all_gather(share, "dp", axis=0, tiled=True).reshape((replicas,) + share.shape)

    gu_x = orthogonal(total_gu, padded_gu, 2 * cols, "gu")
    d_x = orthogonal(after(total_d, gu_x), padded_d, cols, "down")
    small_x, gain_sum = kernel(
        muon_small_kernel,
        (sds((4, slab, hd), F32), sds((gain_tile, hd), F32)),
        2 * 10**9,
        4 * 10**6,
        name="muon_small",
    )(in_hbm(after(every, d_x)), new_small)
    gain_sum = gain_sum.reshape(-1)
    norm_total = gain_sum[: 4 * width].reshape(4, width)
    qk_total = gain_sum[4 * width : 4 * width + 2 * hd].reshape(2, hd)

    shrink = 1.0 - MUON_RATE * WEIGHT_DECAY
    tall = MUON_RATE * math.sqrt(max(1.0, half / hd))
    flat = MUON_RATE * math.sqrt(max(1.0, hd / half))
    new_query = w_query * shrink - tall * small_x[0].reshape(w_query.shape)
    new_keyval = w_keyval * shrink - tall * small_x[1:3].reshape(w_keyval.shape)
    new_out = w_out * shrink - flat * small_x[3].T.reshape(w_out.shape)
    new_gate_up = w_gate_up * shrink - gu_x.reshape(w_gate_up.shape)
    new_down = w_down * shrink - d_x.reshape(w_down.shape)
    norm_renewed = GAIN_MOMENTUM * mom_norm + norm_total
    qk_renewed = GAIN_MOMENTUM * mom_qk + qk_total
    return (
        layer_out.astype(BF),
        input_grad,
        new_small[0].reshape(mom_query.shape),
        new_query,
        new_query.astype(BF),
        new_small[1:3].reshape(mom_keyval.shape),
        new_keyval,
        new_keyval.astype(BF),
        new_small[3].T.reshape(mom_out.shape),
        new_out,
        new_out.astype(BF),
        new_gu.reshape(mom_gate_up.shape),
        new_gate_up,
        new_gate_up.astype(BF),
        new_d.reshape(mom_down.shape),
        new_down,
        new_down.astype(BF),
        norm_renewed,
        norm_gains - GAIN_RATE * norm_renewed,
        qk_renewed,
        qk_gains - GAIN_RATE * qk_renewed,
    )


def solution(mesh):
    tok = P(("dp", "row", "col"), None)
    query = P("row", "dp", "col", None)
    keyval = P(None, "row", "dp", None)
    out = P("col", None, "row", "dp")
    slabs = P("row", "col", "dp", None)
    weights = (query, keyval, out, slabs, slabs)
    in_specs = (tok, tok, P("dp", None)) + weights + weights + (P(),) * 4
    out_specs = (tok, tok) + tuple(spec for spec in weights for _ in range(3)) + (P(),) * 4
    return jax.shard_map(shards, mesh=mesh, in_specs=in_specs, out_specs=out_specs, check_vma=False)
```

```python
import functools
import math

import jax
import jax.numpy as jnp
from jax import lax
from jax.experimental import pallas as pl
from jax.experimental.pallas import tpu as pltpu
from jax.sharding import PartitionSpec as P

CONT_LEN = 256
WINDOW = 512
NS_STEPS = 5
NORM_EPS = 1e-06
MUON_EPS = 1e-07
COEF_A = 3.4445
COEF_B = -4.775
COEF_C = 2.0315
MUON_RATE = 0.5
MUON_DECAY = 0.5
WEIGHT_DECAY = 0.01
GAIN_RATE = 0.003
GAIN_MOMENTUM = 0.5
ROPE_BASE = 10000.0
HIGH = lax.Precision.HIGHEST
BF = jnp.bfloat16
F32 = jnp.float32
RING = ("row", "col")
MASKED = -1e30
MIB = 2**20
PAD = 64
GELU_C = math.sqrt(2.0 / math.pi)

NN = (((1,), (0,)), ((), ()))
NT = (((1,), (1,)), ((), ()))
TN = (((0,), (0,)), ((), ()))


def mm(left, right, dims=NN, precision=None):
    return lax.dot_general(left, right, dims, precision=precision, preferred_element_type=F32)


def flip(block, bits):
    return lax.ppermute(block, RING, [(i, i ^ bits) for i in range(8)])


def gather4(block):
    near = [block, flip(block, 2)]
    return near + [flip(part, 1) for part in near]


def gather8(block):
    near = [flip(block, 4), flip(block, 6)]
    return gather4(block) + near + [flip(part, 1) for part in near]


def scatter8(parts):
    def paired(near, far):
        return near.astype(F32) + flip(far, 1).astype(F32)

    across, last = paired(parts[4], parts[6]), paired(parts[5], parts[7])
    beside, total = paired(parts[1], parts[3]), paired(parts[0], parts[2])
    for value, bits in ((across, 4), (last, 6), (beside, 2)):
        total = total + flip(value.astype(BF), bits).astype(F32)
    return total


def scatter4(parts):
    beside = parts[1].astype(F32) + flip(parts[3], 1).astype(F32)
    total = parts[0].astype(F32) + flip(parts[2], 1).astype(F32)
    return total + flip(beside.astype(BF), 2).astype(F32)


def after(value, *others):
    return lax.optimization_barrier((value,) + others)[0]


def swap_all(blocks):
    return lax.all_to_all(blocks, "dp", 0, 0, tiled=True)


def inv_rms(vector):
    return lax.rsqrt(jnp.mean(vector * vector, axis=-1, keepdims=True) + NORM_EPS)


def norm_back(vector, gain, grad):
    scale = inv_rms(vector)
    gz = grad * gain
    du = scale * gz - vector * (scale * scale * scale) * jnp.mean(
        gz * vector, axis=-1, keepdims=True
    )
    return du, jnp.sum(grad * vector * scale, axis=0, keepdims=True)


def rotate(vector, cosine, sine):
    half = vector.shape[-1] // 2
    first, second = vector[:, :half], vector[:, half:]
    return jnp.concatenate([first * cosine - second * sine, second * cosine + first * sine], axis=1)


def rotate_back(vector, cosine, sine):
    half = vector.shape[-1] // 2
    first, second = vector[:, :half], vector[:, half:]
    return jnp.concatenate([first * cosine + second * sine, second * cosine - first * sine], axis=1)


def own_rows(values):
    return values[: values.shape[0] // 2]


def join(*parts):
    return jnp.concatenate([part[...] for part in parts], axis=0)


def attn_fwd_kernel(*refs):
    xs, (w_all, mask, cos, sin, gains), bs = refs[:8], refs[8:13], refs[13:17]
    w, qraw_o, kraw_o, q_o, k_o, v_o, att_o, lse_o = refs[17:]
    hd = q_o.shape[1]
    half = w.shape[0] // 2
    slab = w_all.shape[1] // 2
    slabs = [w_all[d].astype(F32) for d in range(w_all.shape[0])]
    for side in (0, 1):
        rows = [both[side * slab : (side + 1) * slab] for both in slabs]
        w[side * half : (side + 1) * half, :] = jnp.concatenate(rows, axis=0).astype(BF)
    x = join(*xs)
    qraw = mm(own_rows(x), w[:, :hd])
    kv = mm(x, w[:, hd : 3 * hd])
    kraw = kv[:, :hd]
    cosine, sine = cos[...], sin[...]
    q = rotate(qraw * inv_rms(qraw) * gains[0:1, :], own_rows(cosine), own_rows(sine)).astype(BF)
    k = rotate(kraw * inv_rms(kraw) * gains[1:2, :], cosine, sine).astype(BF)
    v = kv[:, hd:].astype(BF)
    scores = mm(q, k, NT) * (hd**-0.5) + mask[...].astype(F32)
    largest = jnp.max(scores, axis=1, keepdims=True)
    weights = jnp.exp(scores - largest)
    total = jnp.sum(weights, axis=1, keepdims=True)
    att = mm((weights / total).astype(BF), v).astype(BF)
    branch = mm(att, w[:, 3 * hd :], NT).astype(BF)
    rows = bs[0].shape[0]
    for i, part in enumerate(bs):
        part[...] = branch[i * rows : (i + 1) * rows]
    qraw_o[...] = qraw
    kraw_o[...] = kraw
    q_o[...] = q
    k_o[...] = k
    v_o[...] = v
    att_o[...] = att
    lse_o[...] = jnp.broadcast_to(largest + jnp.log(total), lse_o.shape)


def attn_bwd_kernel(*refs):
    das, xs, refs = refs[:4], refs[4:12], refs[12:]
    w, mask, cos, sin, gains, qraw, kraw, q, k, v, att, lse = refs[:12]
    ns, (dw, dgains) = refs[12:20], refs[20:]
    hd = q.shape[1]
    half = q.shape[0]
    scale = hd**-0.5
    da = join(*das)
    datt = mm(da, w[:, 3 * hd :]).astype(BF)
    scores = mm(q[...], k[...], NT) * scale + mask[...].astype(F32)
    weights = jnp.exp(scores - lse[:, 0:1])
    dv = mm(weights.astype(BF), datt, TN).astype(BF)
    dp = mm(datt, v[...], NT)
    inner = jnp.sum(weights * dp, axis=1, keepdims=True)
    ds = (weights * (dp - inner)).astype(BF)
    dq = mm(ds, k[...]) * scale
    dk = mm(ds, q[...], TN) * scale
    cosine, sine = cos[...], sin[...]
    dqraw, dgq = norm_back(
        qraw[...], gains[0:1, :], rotate_back(dq, own_rows(cosine), own_rows(sine))
    )
    dkraw, dgk = norm_back(kraw[...], gains[1:2, :], rotate_back(dk, cosine, sine))
    dqraw, dkraw = dqraw.astype(BF), dkraw.astype(BF)
    dgains[0:1, :] = dgq
    dgains[1:2, :] = dgk
    x = join(*xs)
    width = x.shape[1]
    parts = (
        (mm(own_rows(x), dqraw, TN), 0),
        (mm(x, dkraw, TN), 1),
        (mm(x, dv, TN), 2),
        (mm(da, att[...], TN), 3),
    )
    slab = dw.shape[1] // 2
    for part, place in parts:
        for d in range(dw.shape[0]):
            both = [part[at : at + slab] for at in (d * slab, width // 2 + d * slab)]
            dw[d, :, place * hd : (place + 1) * hd] = jnp.concatenate(both, axis=0).astype(BF)
    back = mm(dkraw, w[:, hd : 2 * hd], NT) + mm(dv, w[:, 2 * hd : 3 * hd], NT)
    qback = mm(dqraw, w[:, :hd], NT)
    rows = ns[0].shape[0]
    for i, part in enumerate(ns):
        at = slice(i * rows, (i + 1) * rows)
        part[...] = (back[at] + qback[at] if i < 4 else back[at]).astype(BF)


def gelu_parts(gate):
    cube = GELU_C * 0.044715
    square = gate * gate
    h = 0.5 * jnp.tanh(gate * (cube * square + GELU_C)) + 0.5
    value = gate * h
    slope = h + value * (1.0 - h) * (6.0 * cube * square + 2.0 * GELU_C)
    return value, slope


def ffn_fwd_kernel(*refs):
    xs, w, (slope_o, value_o, hidden_o), parts = refs[:8], refs[8], refs[9:12], refs[12:20]
    x, units, down = refs[20:]
    step = pl.program_id(0)
    slabs, _, rows, width = w.shape
    count = slabs * rows

    @pl.when(step == 0)
    def _():
        gather_rows(x, xs)

    gate = mm(x[...], w[:, 0].reshape(count, width), NT)
    up = mm(x[...], w[:, 1].reshape(count, width), NT)
    value, slope = gelu_parts(gate)
    hidden = (value * up).astype(BF)
    slope_o[...] = (slope * up).astype(BF)
    value_o[...] = value.astype(BF)
    hidden_o[...] = hidden
    units[step] = hidden
    down[pl.ds(pl.multiple_of(step * count, count), count), :] = w[:, 2].reshape(count, width)

    @pl.when(step == pl.num_programs(0) - 1)
    def _():
        whole = jnp.concatenate([units[i] for i in range(units.shape[0])], axis=1)
        total = mm(whole, down[...]).astype(BF)
        height = parts[0].shape[0]
        for i, part in enumerate(parts):
            part[...] = total[i * height : (i + 1) * height]


def gather_rows(whole, parts):
    height = parts[0].shape[0]
    for i, part in enumerate(parts):
        whole[i * height : (i + 1) * height, :] = part[...]


def accumulate(step, acc, term, *parts):
    last = pl.num_programs(0) - 1

    @pl.when(step == 0)
    def _():
        acc[...] = term

    @pl.when((step > 0) & (step < last))
    def _():
        acc[...] += term

    @pl.when(step == last)
    def _():
        total = (acc[...] + term).astype(BF)
        rows = parts[0].shape[0]
        for i, part in enumerate(parts):
            part[...] = total[i * rows : (i + 1) * rows]


def ffn_units_kernel(*refs):
    xs, ds, refs = refs[:8], refs[8:16], refs[16:]
    w, slope_i, value_i, hidden_i, dgate_o, dup_o, dw, x, d = refs
    slabs, _, rows, width = dw.shape

    @pl.when(pl.program_id(0) == 0)
    def _():
        gather_rows(x, xs)
        gather_rows(d, ds)

    dhid = mm(d[...], w[...].reshape(slabs * rows, width), NT)
    dgate = (dhid * slope_i[...].astype(F32)).astype(BF)
    dup = (dhid * value_i[...].astype(F32)).astype(BF)
    dgate_o[...] = dgate
    dup_o[...] = dup
    for i, (left, right) in enumerate(((dgate, x), (dup, x), (hidden_i[...], d))):
        dw[:, i] = mm(left, right[...], TN).astype(BF).reshape(slabs, rows, width)


def ffn_tokens_kernel(dgate, dup, w, *refs):
    parts, acc = refs[:8], refs[8]
    slabs, _, rows, width = w.shape
    term = mm(dgate[...], w[:, 0].reshape(slabs * rows, width)) + mm(
        dup[...], w[:, 1].reshape(slabs * rows, width)
    )
    accumulate(pl.program_id(0), acc, term, *parts)


def split(values, count):
    pieces = []
    for _ in range(count):
        pieces.append(values.astype(BF))
        values = values - pieces[-1].astype(F32)
    return pieces


def stacks(values):
    a, b = split(values, 2)
    return jnp.concatenate([a, a, b], axis=0), jnp.concatenate([a, b, a], axis=0)


def sym_parts(left, right, n):
    return [mm(left[:, at:], right[:, at : at + 256], TN) for at in range(0, n, 256)]


def sym_full(parts):
    columns = []
    for j, part in enumerate(parts):
        above = [parts[i][(j - i) * 256 : (j - i) * 256 + part.shape[1]].T for i in range(j)]
        columns.append(jnp.concatenate(above + [part], axis=0) if above else part)
    return jnp.concatenate(columns, axis=1) if len(columns) > 1 else columns[0]


def sym_mm(left, right, n):
    return sym_full(sym_parts(left, right, n))


def muon_chains(grams, currents):
    n = grams[0].shape[0]
    diag = lax.broadcasted_iota(jnp.int32, (n, n), 0) == lax.broadcasted_iota(jnp.int32, (n, n), 1)
    a, x = [], []
    for gram, current in zip(grams, currents):
        trace = jnp.sum(
            jnp.sum(jnp.where(diag, gram, 0.0), axis=1, keepdims=True), axis=0, keepdims=True
        )
        factor = 1.0 / (jnp.sqrt(trace) + MUON_EPS)
        a.append(gram * (factor * factor))
        x.append(current * factor)
    for step in range(NS_STEPS):
        sa = [stacks(m) for m in a]
        square = [sym_mm(l, r, n) for l, r in sa]
        poly = [COEF_B * m + COEF_C * q + jnp.where(diag, COEF_A, 0.0) for m, q in zip(a, square)]
        sp = [stacks(p) for p in poly]
        if step < NS_STEPS - 1:
            half = [stacks(sym_mm(l, sp[i][1], n)) for i, (l, _) in enumerate(sa)]
            a = [sym_mm(l, sp[i][1], n) for i, (l, _) in enumerate(half)]
        x = [mm(sp[i][0], stacks(m)[1], TN) for i, m in enumerate(x)]
    return x


def pack_rows(n):
    return sum(2 * (n - at) if n - at >= 256 else n - at for at in range(0, n, 256))


def ff_gram_kernel(flag, mine, theirs, mom_gu, mom_d, gu_o, d_o, gu_c, d_c, packed):
    first = flag[0] == 0
    n = mom_gu.shape[0]
    work = (((0, 1), mom_gu, gu_o, gu_c), ((2,), mom_d, d_o, d_c))
    for place, (kinds, mom, m_o, compact_o) in enumerate(work):
        rows = []
        for kind in kinds:
            own = mine[kind * PAD : (kind + 1) * PAD, :].astype(F32)
            got = theirs[kind * PAD : (kind + 1) * PAD, :].astype(F32)
            rows += [jnp.where(first, own, got), jnp.where(first, got, own)]
        part = mom.shape[1] // len(rows)
        blank = jnp.zeros((n, PAD - part), F32)
        spread = []
        for i in range(len(rows)):
            spread += [mom[:, i * part : (i + 1) * part], blank]
        m = MUON_DECAY * jnp.concatenate(spread, axis=1) + jnp.concatenate(rows, axis=0).T
        m_o[...] = m
        compact_o[...] = compact(m, compact_o.shape[1])
        pieces = []
        for start in range(0, n, 256):
            block = mm(m[start:], m[start : start + 256], NT, HIGH)
            if block.shape[1] == 256:
                pieces += [block[:, :128], block[:, 128:]]
            else:
                pieces.append(jnp.pad(block, ((0, 0), (0, 128 - block.shape[1]))))
        replicas, rows, _ = packed.shape
        rows //= 2
        whole = jnp.concatenate(pieces, axis=0)
        whole = jnp.pad(whole, ((0, replicas * rows - whole.shape[0]), (0, 0)))
        packed[:, place * rows : (place + 1) * rows, :] = whole.reshape(replicas, rows, 128)


def compact(values, width):
    count = values.shape[1] // PAD
    part = width // count
    return jnp.concatenate([values[:, i * PAD : i * PAD + part] for i in range(count)], axis=1)


def muon_large_kernel(scale, packed, m, out):
    n = m.shape[0]
    parts, at = [], 0
    for start in range(0, n, 256):
        rows, cols = n - start, min(256, n - start)
        if cols == 256:
            parts.append(
                jnp.concatenate(
                    [packed[at : at + rows, :], packed[at + rows : at + 2 * rows, :]], axis=1
                )
            )
            at += 2 * rows
        else:
            parts.append(packed[at : at + rows, :cols])
            at += rows
    (x,) = muon_chains([sym_full(parts)], [m[...]])
    out[...] = compact(x * scale, out.shape[1])


def muon_small_kernel(every, m, out, gains):
    count, rows, n = m.shape
    lead = every.shape[1] - gains.shape[0]
    step = lead // count
    grams = []
    for i in range(count):
        whole = every[:, i * step : (i + 1) * step, :].reshape(every.shape[0] * step, n)
        grams.append(mm(whole, whole, TN, HIGH))
    for i, x in enumerate(muon_chains(grams, [m[i].T for i in range(count)])):
        out[i] = x.T
    gains[...] = jnp.sum(every[:, lead:, :], axis=0)


def kernel(body, out_shape, flops, nbytes, vmem=32, **extra):
    return pl.pallas_call(
        body,
        out_shape=out_shape,
        compiler_params=pltpu.CompilerParams(vmem_limit_bytes=vmem * MIB),
        cost_estimate=pl.CostEstimate(flops=flops, bytes_accessed=nbytes, transcendentals=0),
        **extra,
    )


def sds(shape, dtype):
    return jax.ShapeDtypeStruct(shape, dtype)


def in_hbm(value):
    return pltpu.with_memory_space_constraint(value, pltpu.HBM)


def shards(
    tokens,
    cotangent,
    branch,
    w_query,
    w_keyval,
    w_out,
    w_gate_up,
    w_down,
    mom_query,
    mom_keyval,
    mom_out,
    mom_gate_up,
    mom_down,
    norm_gains,
    qk_gains,
    mom_norm,
    mom_qk,
):
    rows, width = tokens.shape
    hd = w_query.shape[3]
    replicas = lax.axis_size("dp")
    half = width // 2
    slab = half // replicas
    cols = w_down.shape[3] // half
    part = cols // 2
    row_index = lax.axis_index("row")
    col_index = lax.axis_index("col")
    me = row_index * 4 + col_index
    first_row = row_index == 0
    row_len = 4 * rows
    rep = 8 * rows

    ff_own = (
        jnp.concatenate(
            [
                w_gate_up.reshape(half, 2, cols).astype(BF).transpose(1, 2, 0),
                w_down.reshape(half, 1, cols).astype(BF).transpose(1, 2, 0),
            ],
            axis=0,
        )
        .reshape(3, 2, part, half)
    )
    ff_keep = jnp.where(first_row, ff_own[:, 0], ff_own[:, 1])
    ff_send = jnp.where(first_row, ff_own[:, 1], ff_own[:, 0])
    ff_send, wq, wk, wo = lax.optimization_barrier((ff_send, w_query, w_keyval, w_out))
    ff_got = flip(ff_send, 4)
    att_own = jnp.concatenate(
        [
            wq.reshape(slab, hd),
            wk[0].reshape(slab, hd),
            wk[1].reshape(slab, hd),
            wo.reshape(hd, slab).T,
        ],
        axis=1,
    ).astype(BF)
    att_other = flip(att_own, 4)
    att_pack = jnp.concatenate(
        [jnp.where(first_row, att_own, att_other), jnp.where(first_row, att_other, att_own)]
    )
    att_shares = jnp.broadcast_to(att_pack[None], (replicas,) + att_pack.shape)
    att_shares, tokens, mom_query, mom_keyval, mom_out, mom_gate_up, mom_down = (
        lax.optimization_barrier(
            (att_shares, tokens, mom_query, mom_keyval, mom_out, mom_gate_up, mom_down)
        )
    )
    ff_pack = jnp.concatenate(
        [jnp.where(first_row, ff_keep, ff_got), jnp.where(first_row, ff_got, ff_keep)], axis=2
    )
    ff_pack = after(jnp.pad(ff_pack, ((0, 0), (0, PAD - part), (0, 0))), att_shares)
    ff_w = lax.all_gather(ff_pack.reshape(3 * PAD, width), "dp", axis=0, tiled=True)
    ff_w = ff_w.reshape(replicas, 3, PAD, width)
    att_all = swap_all(att_shares)
    mom_gu = mom_gate_up.reshape(half, 2 * cols)
    mom_d = mom_down.reshape(half, cols)
    mom_small = jnp.stack(
        [
            mom_query.reshape(slab, hd),
            mom_keyval[0].reshape(slab, hd),
            mom_keyval[1].reshape(slab, hd),
            mom_out.reshape(hd, slab).T,
        ]
    )
    att_all, mom_gu, mom_d, mom_small = lax.optimization_barrier((att_all, mom_gu, mom_d, mom_small))
    slots = jnp.asarray(
        [2 * k + core for pair in (0, 2) for core in (0, 1) for k in (pair, pair + 1)], jnp.int32
    )
    ids = ((me ^ slots)[:, None] * rows + jnp.arange(rows, dtype=jnp.int32)[None, :]).reshape(rep)
    starts = branch[0]
    in_prompt = ids < row_len
    offset = jnp.maximum(ids - row_len, 0)
    segment = jnp.where(in_prompt, -1, offset // CONT_LEN)
    start = jnp.max(
        jnp.where(
            segment[:, None] == jnp.arange(starts.shape[0], dtype=jnp.int32)[None, :],
            starts[None, :],
            0,
        ),
        axis=1,
    )
    position = jnp.where(in_prompt, ids, start + offset % CONT_LEN)
    q_seg, q_pos, q_start = own_rows(segment), own_rows(position), own_rows(start)
    same = (q_seg[:, None] == segment[None, :]) & (position[None, :] <= q_pos[:, None])
    forked = (q_seg[:, None] >= 0) & (segment[None, :] < 0) & (position[None, :] < q_start[:, None])
    seen = (same | forked) & (q_pos[:, None] - position[None, :] < WINDOW)
    mask = jnp.where(seen, 0.0, MASKED).astype(BF)
    steps = jnp.arange(hd // 2, dtype=F32) * (2.0 / hd)
    angle = position.astype(F32)[:, None] * jnp.exp(-math.log(ROPE_BASE) * steps)[None, :]
    cosine, sine = jnp.cos(angle), jnp.sin(angle)

    stream = tokens.astype(F32)
    normed = (stream * inv_rms(stream) * norm_gains[0]).astype(BF)
    normed_all = gather8(normed)
    *attn_parts, att_w, q_raw, k_raw, q, k, v, att, lse = kernel(
        attn_fwd_kernel,
        (sds((rows, width), BF),) * 4
        + (
            pltpu.HBM((width, 4 * hd), BF),
            pltpu.HBM((row_len, hd), F32),
            pltpu.HBM((rep, hd), F32),
            pltpu.HBM((row_len, hd), BF),
            pltpu.HBM((rep, hd), BF),
            pltpu.HBM((rep, hd), BF),
            pltpu.HBM((row_len, hd), BF),
            pltpu.HBM((row_len, 128), F32),
        ),
        3 * 10**9,
        12 * 10**6,
        name="attn_fwd",
    )(in_hbm(normed_all[0]), *normed_all[1:], att_all, in_hbm(mask), in_hbm(cosine), in_hbm(sine), qk_gains)
    attn_branch = scatter4(attn_parts)
    middle = stream + attn_branch * inv_rms(attn_branch) * norm_gains[1]
    normed_ff = (middle * inv_rms(middle) * norm_gains[2]).astype(BF)

    nf_all = gather8(normed_ff)
    hidden_units = replicas * PAD
    part_spec = pl.BlockSpec((rows, width), lambda i: (0, 0))
    h_out = sds((rep, hidden_units), BF)
    x_out = sds((rows, width), BF)
    rows_all = pltpu.VMEM((rep, width), BF)

    def specs(group):
        return (
            pl.BlockSpec((group, 3, PAD, width), lambda i: (i, 0, 0, 0)),
            pl.BlockSpec((rep, group * PAD), lambda i: (0, i)),
        )

    w_spec, h_spec = specs(4)
    slope, value, hidden, *ff_parts = kernel(
        ffn_fwd_kernel,
        (h_out,) * 3 + (x_out,) * 8,
        8 * 10**9,
        20 * 10**6,
        grid=(replicas // 4,),
        in_specs=[part_spec] * 8 + [w_spec],
        out_specs=[h_spec] * 3 + [part_spec] * 8,
        scratch_shapes=[
            rows_all,
            pltpu.VMEM((replicas // 4, rep, 4 * PAD), BF),
            pltpu.VMEM((hidden_units, width), BF),
        ],
        name="ffn_fwd",
    )(*nf_all, in_hbm(ff_w))
    ff_branch = scatter8(ff_parts)
    layer_out = middle + ff_branch * inv_rms(ff_branch) * norm_gains[3]

    upstream = cotangent.astype(F32)
    ff_grad, grad_post_ff = norm_back(ff_branch, norm_gains[3], upstream)
    df_all = gather8(ff_grad.astype(BF))
    dgate, dup, ff_dw = kernel(
        ffn_units_kernel,
        (pltpu.HBM((rep, hidden_units), BF),) * 2 + (pltpu.HBM((replicas, 3, PAD, width), BF),),
        10 * 10**9,
        30 * 10**6,
        vmem=34,
        grid=(replicas // 8,),
        in_specs=[part_spec] * 16
        + [pl.BlockSpec((8, 1, PAD, width), lambda i: (i, 2, 0, 0))]
        + [specs(8)[1]] * 3,
        out_specs=[specs(8)[1]] * 2 + [specs(8)[0]],
        scratch_shapes=[rows_all, rows_all],
        name="ffn_units",
    )(*nf_all, *df_all, in_hbm(ff_w), slope, value, hidden)
    ff_sum = lax.psum_scatter(
        ff_dw.reshape(replicas * 3 * PAD, width), "dp", scatter_dimension=0, tiled=True
    )
    nf_parts = kernel(
        ffn_tokens_kernel,
        (x_out,) * 8,
        5 * 10**9,
        12 * 10**6,
        grid=(replicas // 8,),
        in_specs=[specs(8)[1]] * 2
        + [pl.BlockSpec((8, 2, PAD, width), lambda i: (i, 0, 0, 0))],
        out_specs=[part_spec] * 8,
        scratch_shapes=[pltpu.VMEM((rep, width), F32)],
        name="ffn_tokens",
    )(in_hbm(dgate), in_hbm(dup), in_hbm(ff_w))
    normed_ff_grad = scatter8(nf_parts)
    middle_part, grad_pre_ff = norm_back(middle, norm_gains[2], normed_ff_grad)
    middle_grad = upstream + middle_part
    attn_grad, grad_post = norm_back(attn_branch, norm_gains[1], middle_grad)

    da_all = gather4(attn_grad.astype(BF))
    *dn_parts, att_dw, grad_qk = kernel(
        attn_bwd_kernel,
        (x_out,) * 8 + (sds((replicas, 2 * slab, 4 * hd), BF), sds((2, hd), F32)),
        6 * 10**9,
        20 * 10**6,
        name="attn_bwd",
    )(*da_all, *normed_all, att_w, mask, cosine, sine, qk_gains, q_raw, k_raw, q, k, v, att, lse)
    att_got = swap_all(att_dw)
    normed_grad = scatter8(dn_parts)
    stream_part, grad_pre = norm_back(stream, norm_gains[0], normed_grad)
    input_grad = middle_grad + stream_part

    flag = row_index.astype(jnp.int32).reshape(1)

    low, high = ff_sum[:, :half], ff_sum[:, half:]
    mine = jnp.where(first_row, low, high)
    swapped = jnp.where(first_row, high, low)
    theirs = flip(swapped, 4)
    share_rows = -(-pack_rows(half) // (8 * replicas)) * 8
    vmem = pl.BlockSpec(memory_space=pltpu.VMEM)
    padded_gu, padded_d, new_gu, new_d, packed = kernel(
        ff_gram_kernel,
        (
            sds((half, 4 * PAD), F32),
            sds((half, 2 * PAD), F32),
            sds((half, 2 * cols), F32),
            sds((half, cols), F32),
            sds((replicas, 2 * share_rows, 128), F32),
        ),
        3 * 10**9,
        6 * 10**6,
        in_specs=[pl.BlockSpec(memory_space=pltpu.SMEM)] + [vmem] * 4,
        name="gram_ff",
    )(flag, mine, theirs, mom_gu, mom_d)
    gram_share = jnp.sum(swap_all(packed), axis=0)
    gram_share = gram_share.reshape(2, -1, 128)

    def everywhere(share):
        return swap_all(jnp.broadcast_to(share[None], (replicas,) + share.shape)).reshape(-1, 128)

    total_gu, total_d = everywhere(gram_share[0]), everywhere(gram_share[1])

    def orthogonal(total, padded, width, name):
        scale = MUON_RATE * math.sqrt(max(1.0, half / (width * replicas)))
        return kernel(
            functools.partial(muon_large_kernel, scale),
            sds((half, width), F32),
            12 * 10**9,
            5 * 10**6,
            name="muon_" + name,
        )(total, padded)

    att_sum = jnp.sum(after(att_got, swapped).astype(F32), axis=0)
    gain_part = jnp.concatenate([grad_pre, grad_post, grad_pre_ff, grad_post_ff], axis=0)
    gain_pack = jnp.concatenate([gain_part.reshape(-1), grad_qk.reshape(-1)])
    gain_rows = gain_pack.shape[0] // (4 * hd)
    gain_pack = gain_pack.reshape(gain_rows, 4 * hd)
    att_lo, att_hi = att_sum[:slab], att_sum[slab:]
    att_g = jnp.concatenate([jnp.where(first_row, att_lo, att_hi), gain_pack]) + flip(
        jnp.concatenate([jnp.where(first_row, att_hi, att_lo), gain_pack]), 4
    )
    ring_g = jnp.concatenate(
        [att_g[:slab, hd : 3 * hd], att_g[slab:].reshape(2 * gain_rows, 2 * hd)], axis=0
    )
    ring_g = ring_g + flip(ring_g, 1)
    ring_g = ring_g + flip(ring_g, 2)
    grad_small = jnp.stack(
        [att_g[:slab, :hd], ring_g[:slab, :hd], ring_g[:slab, hd:], att_g[:slab, 3 * hd :]]
    )
    new_small = MUON_DECAY * mom_small + grad_small
    tile = 8
    slab_rows = -(-slab // tile) * tile
    gains_in = ring_g[slab:].reshape(-1, hd)
    gain_tile = -(-gains_in.shape[0] // tile) * tile
    share = jnp.concatenate(
        [
            jnp.pad(new_small, ((0, 0), (0, slab_rows - slab), (0, 0))).reshape(-1, hd),
            jnp.pad(gains_in, ((0, gain_tile - gains_in.shape[0]), (0, 0))),
        ]
    )
    every = lax.all_gather(share, "dp", axis=0, tiled=True).reshape((replicas,) + share.shape)

    gu_x = orthogonal(total_gu, padded_gu, 2 * cols, "gu")
    d_x = orthogonal(after(total_d, gu_x), padded_d, cols, "down")
    small_x, gain_sum = kernel(
        muon_small_kernel,
        (sds((4, slab, hd), F32), sds((gain_tile, hd), F32)),
        2 * 10**9,
        4 * 10**6,
        name="muon_small",
    )(in_hbm(after(every, d_x)), new_small)
    gain_sum = gain_sum.reshape(-1)
    norm_total = gain_sum[: 4 * width].reshape(4, width)
    qk_total = gain_sum[4 * width : 4 * width + 2 * hd].reshape(2, hd)

    shrink = 1.0 - MUON_RATE * WEIGHT_DECAY
    tall = MUON_RATE * math.sqrt(max(1.0, half / hd))
    flat = MUON_RATE * math.sqrt(max(1.0, hd / half))
    new_query = w_query * shrink - tall * small_x[0].reshape(w_query.shape)
    new_keyval = w_keyval * shrink - tall * small_x[1:3].reshape(w_keyval.shape)
    new_out = w_out * shrink - flat * small_x[3].T.reshape(w_out.shape)
    new_gate_up = w_gate_up * shrink - gu_x.reshape(w_gate_up.shape)
    new_down = w_down * shrink - d_x.reshape(w_down.shape)
    norm_renewed = GAIN_MOMENTUM * mom_norm + norm_total
    qk_renewed = GAIN_MOMENTUM * mom_qk + qk_total
    return (
        layer_out.astype(BF),
        input_grad,
        new_small[0].reshape(mom_query.shape),
        new_query,
        new_query.astype(BF),
        new_small[1:3].reshape(mom_keyval.shape),
        new_keyval,
        new_keyval.astype(BF),
        new_small[3].T.reshape(mom_out.shape),
        new_out,
        new_out.astype(BF),
        new_gu.reshape(mom_gate_up.shape),
        new_gate_up,
        new_gate_up.astype(BF),
        new_d.reshape(mom_down.shape),
        new_down,
        new_down.astype(BF),
        norm_renewed,
        norm_gains - GAIN_RATE * norm_renewed,
        qk_renewed,
        qk_gains - GAIN_RATE * qk_renewed,
    )


def solution(mesh):
    tok = P(("dp", "row", "col"), None)
    query = P("row", "dp", "col", None)
    keyval = P(None, "row", "dp", None)
    out = P("col", None, "row", "dp")
    slabs = P("row", "col", "dp", None)
    weights = (query, keyval, out, slabs, slabs)
    in_specs = (tok, tok, P("dp", None)) + weights + weights + (P(),) * 4
    out_specs = (tok, tok) + tuple(spec for spec in weights for _ in range(3)) + (P(),) * 4
    return jax.shard_map(shards, mesh=mesh, in_specs=in_specs, out_specs=out_specs, check_vma=False)
```

```python
import functools
import math

import jax
import jax.numpy as jnp
from jax import lax
from jax.experimental import pallas as pl
from jax.experimental.pallas import tpu as pltpu
from jax.sharding import PartitionSpec as P

CONT_LEN = 256
WINDOW = 512
NS_STEPS = 5
NORM_EPS = 1e-06
MUON_EPS = 1e-07
COEF_A = 3.4445
COEF_B = -4.775
COEF_C = 2.0315
MUON_RATE = 0.5
MUON_DECAY = 0.5
WEIGHT_DECAY = 0.01
GAIN_RATE = 0.003
GAIN_MOMENTUM = 0.5
ROPE_BASE = 10000.0
HIGH = lax.Precision.HIGHEST
BF = jnp.bfloat16
F32 = jnp.float32
RING = ("row", "col")
MASKED = -1e30
MIB = 2**20
PAD = 64
GELU_C = math.sqrt(2.0 / math.pi)

NN = (((1,), (0,)), ((), ()))
NT = (((1,), (1,)), ((), ()))
TN = (((0,), (0,)), ((), ()))


def mm(left, right, dims=NN, precision=None):
    return lax.dot_general(left, right, dims, precision=precision, preferred_element_type=F32)


def flip(block, bits):
    return lax.ppermute(block, RING, [(i, i ^ bits) for i in range(8)])


def gather4(block):
    near = [block, flip(block, 2)]
    return near + [flip(part, 1) for part in near]


def gather8(block):
    near = [flip(block, 4), flip(block, 6)]
    return gather4(block) + near + [flip(part, 1) for part in near]


def scatter8(parts):
    def paired(near, far):
        return near.astype(F32) + flip(far, 1).astype(F32)

    across, last = paired(parts[4], parts[6]), paired(parts[5], parts[7])
    beside, total = paired(parts[1], parts[3]), paired(parts[0], parts[2])
    for value, bits in ((across, 4), (last, 6), (beside, 2)):
        total = total + flip(value.astype(BF), bits).astype(F32)
    return total


def scatter4(parts):
    beside = parts[1].astype(F32) + flip(parts[3], 1).astype(F32)
    total = parts[0].astype(F32) + flip(parts[2], 1).astype(F32)
    return total + flip(beside.astype(BF), 2).astype(F32)


def after(value, *others):
    return lax.optimization_barrier((value,) + others)[0]


def swap_all(blocks):
    return lax.all_to_all(blocks, "dp", 0, 0, tiled=True)


def inv_rms(vector):
    return lax.rsqrt(jnp.mean(vector * vector, axis=-1, keepdims=True) + NORM_EPS)


def norm_back(vector, gain, grad):
    scale = inv_rms(vector)
    gz = grad * gain
    du = scale * gz - vector * (scale * scale * scale) * jnp.mean(
        gz * vector, axis=-1, keepdims=True
    )
    return du, jnp.sum(grad * vector * scale, axis=0, keepdims=True)


def rotate(vector, cosine, sine):
    half = vector.shape[-1] // 2
    first, second = vector[:, :half], vector[:, half:]
    return jnp.concatenate([first * cosine - second * sine, second * cosine + first * sine], axis=1)


def rotate_back(vector, cosine, sine):
    half = vector.shape[-1] // 2
    first, second = vector[:, :half], vector[:, half:]
    return jnp.concatenate([first * cosine + second * sine, second * cosine - first * sine], axis=1)


def own_rows(values):
    return values[: values.shape[0] // 2]


def join(*parts):
    return jnp.concatenate([part[...] for part in parts], axis=0)


def attn_fwd_kernel(*refs):
    xs, (w_all, mask, cos, sin, gains), bs = refs[:8], refs[8:13], refs[13:17]
    w, qraw_o, kraw_o, q_o, k_o, v_o, att_o, lse_o = refs[17:]
    hd = q_o.shape[1]
    half = w.shape[0] // 2
    slab = w_all.shape[1] // 2
    slabs = [w_all[d].astype(F32) for d in range(w_all.shape[0])]
    for side in (0, 1):
        rows = [both[side * slab : (side + 1) * slab] for both in slabs]
        w[side * half : (side + 1) * half, :] = jnp.concatenate(rows, axis=0).astype(BF)
    x = join(*xs)
    qraw = mm(own_rows(x), w[:, :hd])
    kv = mm(x, w[:, hd : 3 * hd])
    kraw = kv[:, :hd]
    cosine, sine = cos[...], sin[...]
    q = rotate(qraw * inv_rms(qraw) * gains[0:1, :], own_rows(cosine), own_rows(sine)).astype(BF)
    k = rotate(kraw * inv_rms(kraw) * gains[1:2, :], cosine, sine).astype(BF)
    v = kv[:, hd:].astype(BF)
    scores = mm(q, k, NT) * (hd**-0.5) + mask[...].astype(F32)
    largest = jnp.max(scores, axis=1, keepdims=True)
    weights = jnp.exp(scores - largest)
    total = jnp.sum(weights, axis=1, keepdims=True)
    att = mm((weights / total).astype(BF), v).astype(BF)
    branch = mm(att, w[:, 3 * hd :], NT).astype(BF)
    rows = bs[0].shape[0]
    for i, part in enumerate(bs):
        part[...] = branch[i * rows : (i + 1) * rows]
    qraw_o[...] = qraw
    kraw_o[...] = kraw
    q_o[...] = q
    k_o[...] = k
    v_o[...] = v
    att_o[...] = att
    lse_o[...] = jnp.broadcast_to(largest + jnp.log(total), lse_o.shape)


def attn_bwd_kernel(*refs):
    das, xs, refs = refs[:4], refs[4:12], refs[12:]
    w, mask, cos, sin, gains, qraw, kraw, q, k, v, att, lse = refs[:12]
    ns, (dw, dgains) = refs[12:20], refs[20:]
    hd = q.shape[1]
    half = q.shape[0]
    scale = hd**-0.5
    da = join(*das)
    datt = mm(da, w[:, 3 * hd :]).astype(BF)
    scores = mm(q[...], k[...], NT) * scale + mask[...].astype(F32)
    weights = jnp.exp(scores - lse[:, 0:1])
    dv = mm(weights.astype(BF), datt, TN).astype(BF)
    dp = mm(datt, v[...], NT)
    inner = jnp.sum(weights * dp, axis=1, keepdims=True)
    ds = (weights * (dp - inner)).astype(BF)
    dq = mm(ds, k[...]) * scale
    dk = mm(ds, q[...], TN) * scale
    cosine, sine = cos[...], sin[...]
    dqraw, dgq = norm_back(
        qraw[...], gains[0:1, :], rotate_back(dq, own_rows(cosine), own_rows(sine))
    )
    dkraw, dgk = norm_back(kraw[...], gains[1:2, :], rotate_back(dk, cosine, sine))
    dqraw, dkraw = dqraw.astype(BF), dkraw.astype(BF)
    dgains[0:1, :] = dgq
    dgains[1:2, :] = dgk
    x = join(*xs)
    width = x.shape[1]
    parts = (
        (mm(own_rows(x), dqraw, TN), 0),
        (mm(x, dkraw, TN), 1),
        (mm(x, dv, TN), 2),
        (mm(da, att[...], TN), 3),
    )
    slab = dw.shape[1] // 2
    for part, place in parts:
        for d in range(dw.shape[0]):
            both = [part[at : at + slab] for at in (d * slab, width // 2 + d * slab)]
            dw[d, :, place * hd : (place + 1) * hd] = jnp.concatenate(both, axis=0).astype(BF)
    back = mm(dkraw, w[:, hd : 2 * hd], NT) + mm(dv, w[:, 2 * hd : 3 * hd], NT)
    qback = mm(dqraw, w[:, :hd], NT)
    rows = ns[0].shape[0]
    for i, part in enumerate(ns):
        at = slice(i * rows, (i + 1) * rows)
        part[...] = (back[at] + qback[at] if i < 4 else back[at]).astype(BF)


def gelu_parts(gate):
    cube = GELU_C * 0.044715
    square = gate * gate
    h = 0.5 * jnp.tanh(gate * (cube * square + GELU_C)) + 0.5
    value = gate * h
    slope = h + value * (1.0 - h) * (6.0 * cube * square + 2.0 * GELU_C)
    return value, slope


def ffn_fwd_kernel(*refs):
    xs, w, (slope_o, value_o, hidden_o), parts = refs[:8], refs[8], refs[9:12], refs[12:20]
    x, units, down = refs[20:]
    step = pl.program_id(0)
    slabs, _, rows, width = w.shape
    count = slabs * rows

    @pl.when(step == 0)
    def _():
        gather_rows(x, xs)

    gate = mm(x[...], w[:, 0].reshape(count, width), NT)
    up = mm(x[...], w[:, 1].reshape(count, width), NT)
    value, slope = gelu_parts(gate)
    hidden = (value * up).astype(BF)
    slope_o[...] = (slope * up).astype(BF)
    value_o[...] = value.astype(BF)
    hidden_o[...] = hidden
    units[step] = hidden
    down[pl.ds(pl.multiple_of(step * count, count), count), :] = w[:, 2].reshape(count, width)

    @pl.when(step == pl.num_programs(0) - 1)
    def _():
        whole = jnp.concatenate([units[i] for i in range(units.shape[0])], axis=1)
        total = mm(whole, down[...]).astype(BF)
        height = parts[0].shape[0]
        for i, part in enumerate(parts):
            part[...] = total[i * height : (i + 1) * height]


def gather_rows(whole, parts):
    height = parts[0].shape[0]
    for i, part in enumerate(parts):
        whole[i * height : (i + 1) * height, :] = part[...]


def accumulate(step, acc, term, *parts):
    last = pl.num_programs(0) - 1

    @pl.when(step == 0)
    def _():
        acc[...] = term

    @pl.when((step > 0) & (step < last))
    def _():
        acc[...] += term

    @pl.when(step == last)
    def _():
        total = (acc[...] + term).astype(BF)
        rows = parts[0].shape[0]
        for i, part in enumerate(parts):
            part[...] = total[i * rows : (i + 1) * rows]


def ffn_units_kernel(*refs):
    xs, ds, refs = refs[:8], refs[8:16], refs[16:]
    w, slope_i, value_i, hidden_i, dgate_o, dup_o, dw, x, d = refs
    slabs, _, rows, width = dw.shape

    @pl.when(pl.program_id(0) == 0)
    def _():
        gather_rows(x, xs)
        gather_rows(d, ds)

    dhid = mm(d[...], w[...].reshape(slabs * rows, width), NT)
    dgate = (dhid * slope_i[...].astype(F32)).astype(BF)
    dup = (dhid * value_i[...].astype(F32)).astype(BF)
    dgate_o[...] = dgate
    dup_o[...] = dup
    for i, (left, right) in enumerate(((dgate, x), (dup, x), (hidden_i[...], d))):
        dw[:, i] = mm(left, right[...], TN).astype(BF).reshape(slabs, rows, width)


def ffn_tokens_kernel(dgate, dup, w, *refs):
    parts, acc = refs[:8], refs[8]
    slabs, _, rows, width = w.shape
    term = mm(dgate[...], w[:, 0].reshape(slabs * rows, width)) + mm(
        dup[...], w[:, 1].reshape(slabs * rows, width)
    )
    accumulate(pl.program_id(0), acc, term, *parts)


def split(values, count):
    pieces = []
    for _ in range(count):
        pieces.append(values.astype(BF))
        values = values - pieces[-1].astype(F32)
    return pieces


def stacks(values):
    a, b = split(values, 2)
    return jnp.concatenate([a, a, b], axis=0), jnp.concatenate([a, b, a], axis=0)


def sym_parts(left, right, n):
    return [mm(left[:, at:], right[:, at : at + 256], TN) for at in range(0, n, 256)]


def sym_full(parts):
    columns = []
    for j, part in enumerate(parts):
        above = [parts[i][(j - i) * 256 : (j - i) * 256 + part.shape[1]].T for i in range(j)]
        columns.append(jnp.concatenate(above + [part], axis=0) if above else part)
    return jnp.concatenate(columns, axis=1) if len(columns) > 1 else columns[0]


def sym_mm(left, right, n):
    return sym_full(sym_parts(left, right, n))


def muon_chains(grams, currents):
    n = grams[0].shape[0]
    diag = lax.broadcasted_iota(jnp.int32, (n, n), 0) == lax.broadcasted_iota(jnp.int32, (n, n), 1)
    a, x = [], []
    for gram, current in zip(grams, currents):
        trace = jnp.sum(
            jnp.sum(jnp.where(diag, gram, 0.0), axis=1, keepdims=True), axis=0, keepdims=True
        )
        factor = 1.0 / (jnp.sqrt(trace) + MUON_EPS)
        a.append(gram * (factor * factor))
        x.append(current * factor)
    for step in range(NS_STEPS):
        sa = [stacks(m) for m in a]
        square = [sym_mm(l, r, n) for l, r in sa]
        poly = [COEF_B * m + COEF_C * q + jnp.where(diag, COEF_A, 0.0) for m, q in zip(a, square)]
        sp = [stacks(p) for p in poly]
        if step < NS_STEPS - 1:
            half = [stacks(sym_mm(l, sp[i][1], n)) for i, (l, _) in enumerate(sa)]
            a = [sym_mm(l, sp[i][1], n) for i, (l, _) in enumerate(half)]
        x = [mm(sp[i][0], stacks(m)[1], TN) for i, m in enumerate(x)]
    return x


def pack_rows(n):
    return sum(2 * (n - at) if n - at >= 256 else n - at for at in range(0, n, 256))


def ff_gram_kernel(flag, mine, theirs, mom_gu, mom_d, gu_o, d_o, gu_c, d_c, packed):
    first = flag[0] == 0
    n = mom_gu.shape[0]
    work = (((0, 1), mom_gu, gu_o, gu_c), ((2,), mom_d, d_o, d_c))
    for place, (kinds, mom, m_o, compact_o) in enumerate(work):
        rows = []
        for kind in kinds:
            own = mine[kind * PAD : (kind + 1) * PAD, :].astype(F32)
            got = theirs[kind * PAD : (kind + 1) * PAD, :].astype(F32)
            rows += [jnp.where(first, own, got), jnp.where(first, got, own)]
        part = mom.shape[1] // len(rows)
        blank = jnp.zeros((n, PAD - part), F32)
        spread = []
        for i in range(len(rows)):
            spread += [mom[:, i * part : (i + 1) * part], blank]
        m = MUON_DECAY * jnp.concatenate(spread, axis=1) + jnp.concatenate(rows, axis=0).T
        m_o[...] = m
        compact_o[...] = compact(m, compact_o.shape[1])
        pieces = []
        for start in range(0, n, 256):
            block = mm(m[start:], m[start : start + 256], NT, HIGH)
            if block.shape[1] == 256:
                pieces += [block[:, :128], block[:, 128:]]
            else:
                pieces.append(jnp.pad(block, ((0, 0), (0, 128 - block.shape[1]))))
        replicas, rows, _ = packed.shape
        rows //= 2
        whole = jnp.concatenate(pieces, axis=0)
        whole = jnp.pad(whole, ((0, replicas * rows - whole.shape[0]), (0, 0)))
        packed[:, place * rows : (place + 1) * rows, :] = whole.reshape(replicas, rows, 128)


def compact(values, width):
    count = values.shape[1] // PAD
    part = width // count
    return jnp.concatenate([values[:, i * PAD : i * PAD + part] for i in range(count)], axis=1)


def muon_large_kernel(scale, packed, m, out):
    n = m.shape[0]
    parts, at = [], 0
    for start in range(0, n, 256):
        rows, cols = n - start, min(256, n - start)
        if cols == 256:
            parts.append(
                jnp.concatenate(
                    [packed[at : at + rows, :], packed[at + rows : at + 2 * rows, :]], axis=1
                )
            )
            at += 2 * rows
        else:
            parts.append(packed[at : at + rows, :cols])
            at += rows
    (x,) = muon_chains([sym_full(parts)], [m[...]])
    out[...] = compact(x * scale, out.shape[1])


def muon_small_kernel(every, m, out, gains):
    count, rows, n = m.shape
    lead = every.shape[1] - gains.shape[0]
    step = lead // count
    grams = []
    for i in range(count):
        whole = every[:, i * step : (i + 1) * step, :].reshape(every.shape[0] * step, n)
        grams.append(mm(whole, whole, TN, HIGH))
    for i, x in enumerate(muon_chains(grams, [m[i].T for i in range(count)])):
        out[i] = x.T
    gains[...] = jnp.sum(every[:, lead:, :], axis=0)


def kernel(body, out_shape, flops, nbytes, vmem=32, **extra):
    return pl.pallas_call(
        body,
        out_shape=out_shape,
        compiler_params=pltpu.CompilerParams(vmem_limit_bytes=vmem * MIB),
        cost_estimate=pl.CostEstimate(flops=flops, bytes_accessed=nbytes, transcendentals=0),
        **extra,
    )


def sds(shape, dtype):
    return jax.ShapeDtypeStruct(shape, dtype)


def in_hbm(value):
    return pltpu.with_memory_space_constraint(value, pltpu.HBM)


def shards(
    tokens,
    cotangent,
    branch,
    w_query,
    w_keyval,
    w_out,
    w_gate_up,
    w_down,
    mom_query,
    mom_keyval,
    mom_out,
    mom_gate_up,
    mom_down,
    norm_gains,
    qk_gains,
    mom_norm,
    mom_qk,
):
    rows, width = tokens.shape
    hd = w_query.shape[3]
    replicas = lax.axis_size("dp")
    half = width // 2
    slab = half // replicas
    cols = w_down.shape[3] // half
    part = cols // 2
    row_index = lax.axis_index("row")
    col_index = lax.axis_index("col")
    me = row_index * 4 + col_index
    first_row = row_index == 0
    row_len = 4 * rows
    rep = 8 * rows

    ff_own = (
        jnp.concatenate(
            [
                w_gate_up.reshape(half, 2, cols).astype(BF).transpose(1, 2, 0),
                w_down.reshape(half, 1, cols).astype(BF).transpose(1, 2, 0),
            ],
            axis=0,
        )
        .reshape(3, 2, part, half)
    )
    ff_keep = jnp.where(first_row, ff_own[:, 0], ff_own[:, 1])
    ff_send = jnp.where(first_row, ff_own[:, 1], ff_own[:, 0])
    ff_send, wq, wk, wo = lax.optimization_barrier((ff_send, w_query, w_keyval, w_out))
    ff_got = flip(ff_send, 4)
    att_own = jnp.concatenate(
        [
            wq.reshape(slab, hd),
            wk[0].reshape(slab, hd),
            wk[1].reshape(slab, hd),
            wo.reshape(hd, slab).T,
        ],
        axis=1,
    ).astype(BF)
    att_other = flip(att_own, 4)
    att_pack = jnp.concatenate(
        [jnp.where(first_row, att_own, att_other), jnp.where(first_row, att_other, att_own)]
    )
    att_shares = jnp.broadcast_to(att_pack[None], (replicas,) + att_pack.shape)
    att_shares, tokens, mom_query, mom_keyval, mom_out, mom_gate_up, mom_down = (
        lax.optimization_barrier(
            (att_shares, tokens, mom_query, mom_keyval, mom_out, mom_gate_up, mom_down)
        )
    )
    ff_pack = jnp.concatenate(
        [jnp.where(first_row, ff_keep, ff_got), jnp.where(first_row, ff_got, ff_keep)], axis=2
    )
    ff_pack = after(jnp.pad(ff_pack, ((0, 0), (0, PAD - part), (0, 0))), att_shares)
    ff_w = lax.all_gather(ff_pack.reshape(3 * PAD, width), "dp", axis=0, tiled=True)
    ff_w = ff_w.reshape(replicas, 3, PAD, width)
    att_all = swap_all(att_shares)
    mom_gu = mom_gate_up.reshape(half, 2 * cols)
    mom_d = mom_down.reshape(half, cols)
    mom_small = jnp.stack(
        [
            mom_query.reshape(slab, hd),
            mom_keyval[0].reshape(slab, hd),
            mom_keyval[1].reshape(slab, hd),
            mom_out.reshape(hd, slab).T,
        ]
    )
    att_all, mom_gu, mom_d, mom_small = lax.optimization_barrier((att_all, mom_gu, mom_d, mom_small))
    slots = jnp.asarray(
        [2 * k + core for pair in (0, 2) for core in (0, 1) for k in (pair, pair + 1)], jnp.int32
    )
    ids = ((me ^ slots)[:, None] * rows + jnp.arange(rows, dtype=jnp.int32)[None, :]).reshape(rep)
    starts = branch[0]
    in_prompt = ids < row_len
    offset = jnp.maximum(ids - row_len, 0)
    segment = jnp.where(in_prompt, -1, offset // CONT_LEN)
    start = jnp.max(
        jnp.where(
            segment[:, None] == jnp.arange(starts.shape[0], dtype=jnp.int32)[None, :],
            starts[None, :],
            0,
        ),
        axis=1,
    )
    position = jnp.where(in_prompt, ids, start + offset % CONT_LEN)
    q_seg, q_pos, q_start = own_rows(segment), own_rows(position), own_rows(start)
    same = (q_seg[:, None] == segment[None, :]) & (position[None, :] <= q_pos[:, None])
    forked = (q_seg[:, None] >= 0) & (segment[None, :] < 0) & (position[None, :] < q_start[:, None])
    seen = (same | forked) & (q_pos[:, None] - position[None, :] < WINDOW)
    mask = jnp.where(seen, 0.0, MASKED).astype(BF)
    steps = jnp.arange(hd // 2, dtype=F32) * (2.0 / hd)
    angle = position.astype(F32)[:, None] * jnp.exp(-math.log(ROPE_BASE) * steps)[None, :]
    cosine, sine = jnp.cos(angle), jnp.sin(angle)

    stream = tokens.astype(F32)
    normed = (stream * inv_rms(stream) * norm_gains[0]).astype(BF)
    normed_all = gather8(normed)
    *attn_parts, att_w, q_raw, k_raw, q, k, v, att, lse = kernel(
        attn_fwd_kernel,
        (sds((rows, width), BF),) * 4
        + (
            pltpu.HBM((width, 4 * hd), BF),
            pltpu.HBM((row_len, hd), F32),
            pltpu.HBM((rep, hd), F32),
            pltpu.HBM((row_len, hd), BF),
            pltpu.HBM((rep, hd), BF),
            pltpu.HBM((rep, hd), BF),
            pltpu.HBM((row_len, hd), BF),
            pltpu.HBM((row_len, 128), F32),
        ),
        3 * 10**9,
        12 * 10**6,
        name="attn_fwd",
    )(in_hbm(normed_all[0]), *normed_all[1:], att_all, in_hbm(mask), in_hbm(cosine), in_hbm(sine), qk_gains)
    attn_branch = scatter4(attn_parts)
    middle = stream + attn_branch * inv_rms(attn_branch) * norm_gains[1]
    normed_ff = (middle * inv_rms(middle) * norm_gains[2]).astype(BF)

    nf_all = gather8(normed_ff)
    hidden_units = replicas * PAD
    part_spec = pl.BlockSpec((rows, width), lambda i: (0, 0))
    h_out = sds((rep, hidden_units), BF)
    x_out = sds((rows, width), BF)
    rows_all = pltpu.VMEM((rep, width), BF)

    def specs(group):
        return (
            pl.BlockSpec((group, 3, PAD, width), lambda i: (i, 0, 0, 0)),
            pl.BlockSpec((rep, group * PAD), lambda i: (0, i)),
        )

    w_spec, h_spec = specs(4)
    slope, value, hidden, *ff_parts = kernel(
        ffn_fwd_kernel,
        (h_out,) * 3 + (x_out,) * 8,
        8 * 10**9,
        20 * 10**6,
        grid=(replicas // 4,),
        in_specs=[part_spec] * 8 + [w_spec],
        out_specs=[h_spec] * 3 + [part_spec] * 8,
        scratch_shapes=[
            rows_all,
            pltpu.VMEM((replicas // 4, rep, 4 * PAD), BF),
            pltpu.VMEM((hidden_units, width), BF),
        ],
        name="ffn_fwd",
    )(*nf_all, in_hbm(ff_w))
    ff_branch = scatter8(ff_parts)
    layer_out = middle + ff_branch * inv_rms(ff_branch) * norm_gains[3]

    upstream = cotangent.astype(F32)
    ff_grad, grad_post_ff = norm_back(ff_branch, norm_gains[3], upstream)
    df_all = gather8(ff_grad.astype(BF))
    dgate, dup, ff_dw = kernel(
        ffn_units_kernel,
        (pltpu.HBM((rep, hidden_units), BF),) * 2 + (pltpu.HBM((replicas, 3, PAD, width), BF),),
        10 * 10**9,
        30 * 10**6,
        vmem=34,
        grid=(replicas // 8,),
        in_specs=[part_spec] * 16
        + [pl.BlockSpec((8, 1, PAD, width), lambda i: (i, 2, 0, 0))]
        + [specs(8)[1]] * 3,
        out_specs=[specs(8)[1]] * 2 + [specs(8)[0]],
        scratch_shapes=[rows_all, rows_all],
        name="ffn_units",
    )(*nf_all, *df_all, in_hbm(ff_w), slope, value, hidden)
    ff_sum = lax.psum_scatter(
        ff_dw.reshape(replicas * 3 * PAD, width), "dp", scatter_dimension=0, tiled=True
    )
    nf_parts = kernel(
        ffn_tokens_kernel,
        (x_out,) * 8,
        5 * 10**9,
        12 * 10**6,
        grid=(replicas // 8,),
        in_specs=[specs(8)[1]] * 2
        + [pl.BlockSpec((8, 2, PAD, width), lambda i: (i, 0, 0, 0))],
        out_specs=[part_spec] * 8,
        scratch_shapes=[pltpu.VMEM((rep, width), F32)],
        name="ffn_tokens",
    )(in_hbm(dgate), in_hbm(dup), in_hbm(ff_w))
    normed_ff_grad = scatter8(nf_parts)
    middle_part, grad_pre_ff = norm_back(middle, norm_gains[2], normed_ff_grad)
    middle_grad = upstream + middle_part
    attn_grad, grad_post = norm_back(attn_branch, norm_gains[1], middle_grad)

    da_all = gather4(attn_grad.astype(BF))
    *dn_parts, att_dw, grad_qk = kernel(
        attn_bwd_kernel,
        (x_out,) * 8 + (sds((replicas, 2 * slab, 4 * hd), BF), sds((2, hd), F32)),
        6 * 10**9,
        20 * 10**6,
        name="attn_bwd",
    )(*da_all, *normed_all, att_w, mask, cosine, sine, qk_gains, q_raw, k_raw, q, k, v, att, lse)
    att_got = swap_all(att_dw)
    normed_grad = scatter8(dn_parts)
    stream_part, grad_pre = norm_back(stream, norm_gains[0], normed_grad)
    input_grad = middle_grad + stream_part

    flag = row_index.astype(jnp.int32).reshape(1)

    low, high = ff_sum[:, :half], ff_sum[:, half:]
    mine = jnp.where(first_row, low, high)
    swapped = jnp.where(first_row, high, low)
    theirs = flip(swapped, 4)
    share_rows = -(-pack_rows(half) // (8 * replicas)) * 8
    vmem = pl.BlockSpec(memory_space=pltpu.VMEM)
    padded_gu, padded_d, new_gu, new_d, packed = kernel(
        ff_gram_kernel,
        (
            pltpu.HBM((half, 4 * PAD), F32),
            pltpu.HBM((half, 2 * PAD), F32),
            sds((half, 2 * cols), F32),
            sds((half, cols), F32),
            sds((replicas, 2 * share_rows, 128), F32),
        ),
        3 * 10**9,
        6 * 10**6,
        in_specs=[pl.BlockSpec(memory_space=pltpu.SMEM)] + [vmem] * 4,
        name="gram_ff",
    )(flag, mine, theirs, mom_gu, mom_d)
    gram_share = jnp.sum(swap_all(packed), axis=0)
    gram_share = gram_share.reshape(2, -1, 128)

    def everywhere(share):
        return swap_all(jnp.broadcast_to(share[None], (replicas,) + share.shape)).reshape(-1, 128)

    total_gu, total_d = everywhere(gram_share[0]), everywhere(gram_share[1])

    def orthogonal(total, padded, width, name):
        scale = MUON_RATE * math.sqrt(max(1.0, half / (width * replicas)))
        return kernel(
            functools.partial(muon_large_kernel, scale),
            sds((half, width), F32),
            12 * 10**9,
            5 * 10**6,
            name="muon_" + name,
        )(total, in_hbm(padded))

    att_sum = jnp.sum(after(att_got, swapped).astype(F32), axis=0)
    gain_part = jnp.concatenate([grad_pre, grad_post, grad_pre_ff, grad_post_ff], axis=0)
    gain_pack = jnp.concatenate([gain_part.reshape(-1), grad_qk.reshape(-1)])
    gain_rows = gain_pack.shape[0] // (4 * hd)
    gain_pack = gain_pack.reshape(gain_rows, 4 * hd)
    att_lo, att_hi = att_sum[:slab], att_sum[slab:]
    att_g = jnp.concatenate([jnp.where(first_row, att_lo, att_hi), gain_pack]) + flip(
        jnp.concatenate([jnp.where(first_row, att_hi, att_lo), gain_pack]), 4
    )
    ring_g = jnp.concatenate(
        [att_g[:slab, hd : 3 * hd], att_g[slab:].reshape(2 * gain_rows, 2 * hd)], axis=0
    )
    ring_g = ring_g + flip(ring_g, 1)
    ring_g = ring_g + flip(ring_g, 2)
    grad_small = jnp.stack(
        [att_g[:slab, :hd], ring_g[:slab, :hd], ring_g[:slab, hd:], att_g[:slab, 3 * hd :]]
    )
    new_small = MUON_DECAY * mom_small + grad_small
    tile = 8
    slab_rows = -(-slab // tile) * tile
    gains_in = ring_g[slab:].reshape(-1, hd)
    gain_tile = -(-gains_in.shape[0] // tile) * tile
    share = jnp.concatenate(
        [
            jnp.pad(new_small, ((0, 0), (0, slab_rows - slab), (0, 0))).reshape(-1, hd),
            jnp.pad(gains_in, ((0, gain_tile - gains_in.shape[0]), (0, 0))),
        ]
    )
    every = lax.all_gather(share, "dp", axis=0, tiled=True).reshape((replicas,) + share.shape)

    gu_x = orthogonal(total_gu, padded_gu, 2 * cols, "gu")
    d_x = orthogonal(after(total_d, gu_x), padded_d, cols, "down")
    small_x, gain_sum = kernel(
        muon_small_kernel,
        (sds((4, slab, hd), F32), sds((gain_tile, hd), F32)),
        2 * 10**9,
        4 * 10**6,
        name="muon_small",
    )(in_hbm(after(every, d_x)), new_small)
    gain_sum = gain_sum.reshape(-1)
    norm_total = gain_sum[: 4 * width].reshape(4, width)
    qk_total = gain_sum[4 * width : 4 * width + 2 * hd].reshape(2, hd)

    shrink = 1.0 - MUON_RATE * WEIGHT_DECAY
    tall = MUON_RATE * math.sqrt(max(1.0, half / hd))
    flat = MUON_RATE * math.sqrt(max(1.0, hd / half))
    new_query = w_query * shrink - tall * small_x[0].reshape(w_query.shape)
    new_keyval = w_keyval * shrink - tall * small_x[1:3].reshape(w_keyval.shape)
    new_out = w_out * shrink - flat * small_x[3].T.reshape(w_out.shape)
    new_gate_up = w_gate_up * shrink - gu_x.reshape(w_gate_up.shape)
    new_down = w_down * shrink - d_x.reshape(w_down.shape)
    norm_renewed = GAIN_MOMENTUM * mom_norm + norm_total
    qk_renewed = GAIN_MOMENTUM * mom_qk + qk_total
    return (
        layer_out.astype(BF),
        input_grad,
        new_small[0].reshape(mom_query.shape),
        new_query,
        new_query.astype(BF),
        new_small[1:3].reshape(mom_keyval.shape),
        new_keyval,
        new_keyval.astype(BF),
        new_small[3].T.reshape(mom_out.shape),
        new_out,
        new_out.astype(BF),
        new_gu.reshape(mom_gate_up.shape),
        new_gate_up,
        new_gate_up.astype(BF),
        new_d.reshape(mom_down.shape),
        new_down,
        new_down.astype(BF),
        norm_renewed,
        norm_gains - GAIN_RATE * norm_renewed,
        qk_renewed,
        qk_gains - GAIN_RATE * qk_renewed,
    )


def solution(mesh):
    tok = P(("dp", "row", "col"), None)
    query = P("row", "dp", "col", None)
    keyval = P(None, "row", "dp", None)
    out = P("col", None, "row", "dp")
    slabs = P("row", "col", "dp", None)
    weights = (query, keyval, out, slabs, slabs)
    in_specs = (tok, tok, P("dp", None)) + weights + weights + (P(),) * 4
    out_specs = (tok, tok) + tuple(spec for spec in weights for _ in range(3)) + (P(),) * 4
    return jax.shard_map(shards, mesh=mesh, in_specs=in_specs, out_specs=out_specs, check_vma=False)
```
